32 devices in a mesh: dp: 2 (over core), proto: 16 (over z, y, x).
Axes of the slice: x: 2, y: 2, z: 4, core: 2. Of those that a mesh axis runs over, the one named last changes fastest.
Arguments:
- features: bfloat16 [1280, 1536], P('dp'), may hold values from -6 to 6
- teacher_features: bfloat16 [256, 1536], P('dp'), may hold values from -8 to 8
- crop_image: int32 [1280], P('dp'), may hold values from 0 to 127, as said below
- crop_view: int32 [1280], P('dp'), may hold values from 0 to 2, as said below
- head_w1: bfloat16 [1536, 2048], P(None, 'proto'), may hold values from -0.15625 to 0.15625
- head_w2: bfloat16 [2048, 256], P('proto'), may hold values from -1 to 1
- protos: bfloat16 [256, 65536], P(None, 'proto'), may hold values from -8 to 8
- teacher_w1: bfloat16 [1536, 2048], P(None, 'proto'), may hold values from -1 to 1
- teacher_w2: bfloat16 [2048, 256], P('proto'), may hold values from -1 to 1
- teacher_protos: bfloat16 [256, 65536], P(None, 'proto'), may hold values from -8 to 8
Outputs:
- grad_features: bfloat16 [1280, 1536], P('dp', 'proto')
- grad_w1: float32 [1536, 2048], P(None, 'proto')
- grad_w2: float32 [2048, 256], P('proto')
- grad_protos: float32 [256, 65536], P(None, 'proto')
The draws below stay inside these ranges and needn't reach their ends.
Inputs may be any that keep to these rules, and one draw needn't show every extreme that they name: `crop_image`: the rows of each aligned block of 640 crops name exactly the images of that block's index b, b * 64 to (b + 1) * 64 - 1, each ten times, in drawn order. `crop_view`: of the ten crops of each image, one has view 0, one view 1 and eight view 2.
All inputs are finite; a program needn't handle non-finite values.
Results may differ from the reference program's by a relative error of at most 0.006.
Values may be sent and summed in bfloat16 or wider, within the bound.
No kernel may reach another device: no remote copies, remote signals or barrier semaphores. Data moves between devices by JAX's collectives and lax.ppermute only.
A program may use at most 64 MiB of HBM per device.

```python
import jax
import jax.numpy as jnp
from jax import lax

D = 1536
HID = 2048
BOT = 256
PROTOS = 65536
IMG_DEV = 64
ITERS = 3
IMAGES = 128
CROPS = 1280
TEACH = 256
N_DP = 2


def crop_layout(key):
    per_block = 10 * IMG_DEV
    blocks = CROPS // per_block
    keys = jax.random.split(key, blocks)
    orders = jax.vmap(lambda one: jax.random.permutation(one, per_block))(keys)
    offsets = jnp.arange(blocks, dtype=jnp.int32)[:, None] * IMG_DEV
    images = (orders // 10).astype(jnp.int32) + offsets
    views = jnp.minimum(orders % 10, 2).astype(jnp.int32)
    return (images.reshape(-1), views.reshape(-1))


def sign_vector(key, tag, count):
    sub = jax.random.fold_in(key, tag)
    return jnp.where(jax.random.bernoulli(sub, 0.5, (count,)), 1.0, -1.0).astype(jnp.float32)


def base_normal(key, shape, scale):
    return jax.random.truncated_normal(key, -6.0, 6.0, shape, jnp.float32) * scale


def draw_crop_image(key, part):
    shared = crop_layout(key)
    return shared[0]


def draw_crop_view(key, part):
    shared = crop_layout(key)
    return shared[1]


def draw_head_w2(key, part):
    direction = sign_vector(key, 501, BOT) / BOT ** 0.5
    key = jax.random.fold_in(key, 11)
    base = base_normal(key, (HID, BOT), HID ** (-0.5))
    return (base + 30.0 / HID * direction[None, :]).astype(jnp.bfloat16)


def draw_protos(key, part):
    direction = sign_vector(key, 501, BOT)
    key = jax.random.fold_in(key, 12)
    top = 0.6
    ramp = top * jnp.arange(PROTOS, dtype=jnp.float32) / (PROTOS - 1)
    base = base_normal(key, (BOT, PROTOS), 1.0)
    return (base + ramp[None, :] * direction[:, None]).astype(jnp.bfloat16)


def draw_teacher_w2(key, part):
    direction = sign_vector(key, 502, BOT) / BOT ** 0.5
    key = jax.random.fold_in(key, 13)
    base = base_normal(key, (HID, BOT), HID ** (-0.5))
    return (base + 16.0 / HID * direction[None, :]).astype(jnp.bfloat16)


def draw_teacher_protos(key, part):
    direction = sign_vector(key, 502, BOT)
    key = jax.random.fold_in(key, 14)
    ramp = jnp.arange(PROTOS, dtype=jnp.float32) / (PROTOS - 1)
    base = base_normal(key, (BOT, PROTOS), 1.0)
    return (base + ramp[None, :] * direction[:, None]).astype(jnp.bfloat16)


def draw_teacher_w1(key, part):
    direction = sign_vector(key, 503, D) / D ** 0.5
    key = jax.random.fold_in(key, 15)
    base = base_normal(key, (D, HID), D ** (-0.5))
    return (base + 0.3 * direction[:, None]).astype(jnp.bfloat16)


def draw_teacher_features(key, part):
    direction = sign_vector(key, 503, D) / D ** 0.5
    key = jax.random.fold_in(key, 16)
    top = 2.0
    ramp = top * jnp.arange(TEACH, dtype=jnp.float32) / (TEACH - 1)
    base = base_normal(key, (TEACH, D), 1.0)
    return (base + (ramp / 0.3)[:, None] * direction[None, :]).astype(jnp.bfloat16)


def level_of(key, dims, cuts, smallest, top_value):
    gain, own = 1.0, jax.random.fold_in(key, 6)
    for axis_at, parts in cuts:
        heights = jnp.exp(jax.random.uniform(jax.random.fold_in(own, axis_at), (parts,), jnp.float32, smallest / len(cuts), top_value / len(cuts)))
        gain = gain * jnp.repeat(heights, dims[axis_at] // parts).reshape([-1 if axis == axis_at else 1 for axis in range(len(dims))])
    return gain


def gaussian(stream_key, dims, scale, bound, cuts=(), held_as=jnp.bfloat16):
    entries = scale * jax.random.normal(stream_key, dims, jnp.float32)
    if cuts:
        entries = entries * level_of(stream_key, dims, cuts, -0.22, 0.18)
    return jnp.clip(entries, -bound, bound).astype(held_as)


def setup_inputs(seed: int = 0) -> dict:
    seeds = jax.random.split(jax.random.key(seed), 11)
    features = gaussian(seeds[0], (CROPS, D), 1.0, 6.0, ((0, 2),))
    teacher_features = draw_teacher_features(jax.random.fold_in(seeds[10], 71), 0)
    crop_image = draw_crop_image(jax.random.fold_in(seeds[10], 71), 0)
    crop_view = draw_crop_view(jax.random.fold_in(seeds[10], 71), 0)
    head_w1 = gaussian(seeds[4], (D, HID), D ** -0.5, 0.15625, ((1, 16),))
    head_w2 = draw_head_w2(jax.random.fold_in(seeds[10], 71), 0)
    protos = draw_protos(jax.random.fold_in(seeds[10], 71), 0)
    teacher_w1 = draw_teacher_w1(jax.random.fold_in(seeds[10], 71), 0)
    teacher_w2 = draw_teacher_w2(jax.random.fold_in(seeds[10], 71), 0)
    teacher_protos = draw_teacher_protos(jax.random.fold_in(seeds[10], 71), 0)
    return dict(features=features, teacher_features=teacher_features, crop_image=crop_image, crop_view=crop_view, head_w1=head_w1, head_w2=head_w2, protos=protos, teacher_w1=teacher_w1, teacher_w2=teacher_w2, teacher_protos=teacher_protos)


def unit_columns(mat):
    matf = mat.astype(jnp.float32)
    inv = lax.rsqrt(lax.optimization_barrier(jnp.sum(matf * matf, axis=0, keepdims=True)) + 1e-06)
    return (matf * inv, inv)

def unit_rows(mat):
    inv = lax.rsqrt(lax.optimization_barrier(jnp.sum(mat * mat, axis=1, keepdims=True)) + 1e-06)
    return (mat * inv, inv)

def gelu_exact(act):
    return act * 0.5 * (1.0 + lax.erf(act * 0.7071067811865476))

def gelu_slope(act):
    return 0.5 * (1.0 + lax.erf(act * 0.7071067811865476)) + act * jnp.exp(-0.5 * act * act) * 0.3989422804014327

def reference(features, teacher_features, crop_image, crop_view, head_w1, head_w2, protos, teacher_w1, teacher_w2, teacher_protos):
    pn, pinv = unit_columns(protos)
    pnb = pn.astype(jnp.bfloat16)
    tpn, tinv = unit_columns(teacher_protos)
    tpnb = tpn.astype(jnp.bfloat16)
    act = jnp.dot(features, head_w1, preferred_element_type=jnp.float32)
    hidden = gelu_exact(act).astype(jnp.bfloat16)
    zfull = jnp.dot(hidden, head_w2, preferred_element_type=jnp.float32)
    tact = jnp.dot(teacher_features, teacher_w1, preferred_element_type=jnp.float32)
    thidden = gelu_exact(tact).astype(jnp.bfloat16)
    tfull = jnp.dot(thidden, teacher_w2, preferred_element_type=jnp.float32)
    zn, zinv = unit_rows(zfull)
    znb = zn.astype(jnp.bfloat16)
    tzn, tzinv = unit_rows(tfull)
    tznb = tzn.astype(jnp.bfloat16)
    weights = jnp.exp(jnp.dot(tznb, tpnb, preferred_element_type=jnp.float32) / 0.07)
    for step in range(ITERS):
        weights = weights / lax.optimization_barrier(jnp.sum(weights, axis=0, keepdims=True))
        weights = weights / lax.optimization_barrier(jnp.sum(weights, axis=1, keepdims=True))
    qb = weights.astype(jnp.bfloat16)
    crop_blk = 10 * IMG_DEV
    teach_blk = 2 * IMG_DEV
    factor = 10.0 / (18 * IMAGES)
    slots = jnp.arange(teach_blk, dtype=jnp.int32)

    def block_step(dpn_acc, index):
        zrows = lax.dynamic_slice_in_dim(znb, (index * crop_blk).astype(jnp.int32), crop_blk, 0)
        images = lax.dynamic_slice_in_dim(crop_image, (index * crop_blk).astype(jnp.int32), crop_blk, 0) - index * IMG_DEV
        views = lax.dynamic_slice_in_dim(crop_view, (index * crop_blk).astype(jnp.int32), crop_blk, 0)
        qrows = lax.dynamic_slice_in_dim(qb, (index * teach_blk).astype(jnp.int32), teach_blk, 0)
        select = (slots[None, :] // 2 == images[:, None]) & (slots[None, :] % 2 != views[:, None])
        target = jnp.dot(select.astype(jnp.bfloat16), qrows, preferred_element_type=jnp.float32)
        count = jnp.where(views == 2, 2.0, 1.0).astype(jnp.float32)
        logits = jnp.dot(zrows, pnb, preferred_element_type=jnp.float32) / 0.1
        ex = jnp.exp(logits)
        esum = lax.optimization_barrier(jnp.sum(ex, axis=1))
        grad = ((ex / esum[:, None] * count[:, None] - target) * factor).astype(jnp.bfloat16)
        dpn_acc = dpn_acc + lax.dot_general(zrows, grad, (((0,), (0,)), ((), ())), preferred_element_type=jnp.float32)
        dzn_blk = lax.dot_general(grad, pnb, (((1,), (1,)), ((), ())), preferred_element_type=jnp.float32)
        return (dpn_acc, dzn_blk)
    start = jnp.zeros((BOT, PROTOS), jnp.float32)
    dpn, dzn_blocks = lax.scan(block_step, start, jnp.arange(N_DP, dtype=jnp.int32))
    dzn = dzn_blocks.reshape(CROPS, BOT)
    grad_protos = pinv * (dpn - pn * lax.optimization_barrier(jnp.sum(pn * dpn, axis=0, keepdims=True)))
    dzb = (zinv * (dzn - zn * lax.optimization_barrier(jnp.sum(zn * dzn, axis=1, keepdims=True)))).astype(jnp.bfloat16)
    grad_w2 = lax.dot_general(hidden, dzb, (((0,), (0,)), ((), ())), preferred_element_type=jnp.float32)
    dhid = (lax.dot_general(dzb, head_w2, (((1,), (1,)), ((), ())), preferred_element_type=jnp.float32) * gelu_slope(act)).astype(jnp.bfloat16)
    grad_w1 = lax.dot_general(features, dhid, (((0,), (0,)), ((), ())), preferred_element_type=jnp.float32)
    grad_features = lax.dot_general(dhid, head_w1, (((1,), (1,)), ((), ())), preferred_element_type=jnp.float32).astype(jnp.bfloat16)
    return (grad_features, grad_w1, grad_w2, grad_protos)
```

```python
import jax
import jax.numpy as jnp
from jax import lax
from jax.sharding import PartitionSpec as P

ITERS = 3
ALL = ("dp", "proto")
F32 = jnp.float32
BF16 = jnp.bfloat16


def gelu_parts(act):
    phi = 0.5 * (1.0 + lax.erf(act * 0.7071067811865476))
    slope = phi + act * jnp.exp(-0.5 * act * act) * 0.3989422804014327
    return (act * phi).astype(BF16), slope


def dot(a, b, dims):
    return lax.dot_general(a, b, (dims, ((), ())), preferred_element_type=F32)


def swap(value, axis, step):
    count = lax.axis_size(axis)
    return lax.ppermute(value, axis, [(i, i ^ step) for i in range(count)])


def over_dp(value):
    return [value] + [swap(value, "dp", s) for s in range(1, lax.axis_size("dp"))]


def tree_sum(parts):
    while len(parts) > 1:
        parts = [parts[i] + parts[i + 1] for i in range(0, len(parts), 2)]
    return parts[0]


def send_all(value, axes):
    count = lax.axis_size(axes)
    return lax.all_to_all(jnp.broadcast_to(value[None], (count,) + value.shape), axes, 0, 0)


def unit_cols(mat):
    matf = mat.astype(F32)
    inv = lax.rsqrt(jnp.sum(matf * matf, axis=0, keepdims=True) + 1e-06)
    return matf * inv, inv


def body(
    features,
    teacher_features,
    crop_image,
    crop_view,
    head_w1,
    head_w2,
    protos,
    teacher_w1,
    teacher_w2,
    teacher_protos,
):
    nd, n = lax.axis_size("dp"), lax.axis_size("proto")
    d, p = lax.axis_index("dp"), lax.axis_index("proto")
    rows, img = features.shape[0], teacher_features.shape[0] // 2
    per = rows // img
    sr, tr = rows // n, 2 * img // n
    bot = head_w2.shape[1]
    factor = 10.0 / (18 * img * nd)
    absolute = d ^ jnp.arange(nd)

    im = crop_image - d * img
    at = jnp.arange(rows, dtype=jnp.int32)
    rank = jnp.sum((im[:, None] == im[None, :]) & (at[None, :] < at[:, None]), axis=1)
    place = im * per + rank
    hit = at[:, None] == place[None, :]
    order = hit.astype(BF16)
    view = jnp.sum(jnp.where(hit, crop_view[None, :], 0), axis=1)
    views = jnp.stack(over_dp(view))[absolute]

    w1_block = lax.all_to_all(head_w1, "proto", split_axis=0, concat_axis=1, tiled=True)
    feats = over_dp(features)
    act = jnp.dot(features, head_w1, preferred_element_type=F32)
    hidden, slope = gelu_parts(act)
    zpart = jnp.dot(hidden, head_w2, preferred_element_type=F32).astype(BF16)
    zpart = jnp.dot(order, zpart, preferred_element_type=F32).astype(BF16)
    tact = jnp.dot(teacher_features, teacher_w1, preferred_element_type=F32)
    thidden, _ = gelu_parts(tact)
    tpart = jnp.dot(thidden, teacher_w2, preferred_element_type=F32).astype(BF16)
    parts = jnp.concatenate([zpart.reshape(n, sr, bot), tpart.reshape(n, tr, bot)], axis=1)
    parts = lax.all_to_all(parts, "proto", 0, 0)
    early = jnp.concatenate(
        [slope.astype(BF16)] + [head_w2[:, i : i + head_w1.shape[1]] for i in range(0, bot, head_w1.shape[1])],
        axis=0,
    )
    early = lax.all_gather(early, "proto")
    zrow = jnp.sum(parts.astype(F32), axis=0)
    zinv = lax.rsqrt(jnp.sum(zrow * zrow, axis=1, keepdims=True) + 1e-06)
    zn = zrow * zinv
    znb = send_all(zn.astype(BF16), "proto")
    znb = jnp.stack(over_dp(znb))[absolute]
    student = znb[:, :, :sr].reshape(nd * rows, bot)
    teacher = znb[:, :, sr:].reshape(nd * 2 * img, bot)

    cols = protos.shape[1] // nd
    pn, pinv = unit_cols(lax.dynamic_slice_in_dim(protos, d * cols, cols, 1))
    pnb = pn.astype(BF16)
    tpnb = unit_cols(lax.dynamic_slice_in_dim(teacher_protos, d * cols, cols, 1))[0].astype(BF16)

    kern = jnp.exp(jnp.dot(teacher, tpnb, preferred_element_type=F32) / 0.07)
    ex = jnp.exp(jnp.dot(student, pnb, preferred_element_type=F32) / 0.1)
    esum = jnp.sum(ex, axis=1)
    exb = ex.astype(BF16)
    sums = dot(exb, pnb, ((1,), (1,)))
    colscale = 1.0 / jnp.sum(kern, axis=0)
    for step in range(ITERS - 1):
        mass = jnp.sum(send_all(jnp.sum(kern * colscale[None, :], axis=1), ALL), axis=0)
        colscale = 1.0 / jnp.sum(kern / mass[:, None], axis=0)
    last = kern * colscale[None, :]
    lastb = last.astype(BF16)
    tsums = dot(lastb, pnb, ((1,), (1,)))
    tot = jnp.sum(send_all(jnp.concatenate([esum, jnp.sum(last, axis=1)]), ALL), axis=0)
    esum, mass = tot[: nd * rows], tot[nd * rows :]

    out = jnp.concatenate([sums.reshape(nd, n, sr, bot), tsums.reshape(nd, n, tr, bot)], axis=2)
    out = out[absolute]
    out = tree_sum([out[0]] + [swap(out[s], "dp", s) for s in range(1, nd)])
    out = lax.all_to_all(out.astype(BF16), "proto", 0, 0)
    out = jnp.sum(out.astype(F32), axis=0)
    crop_scale = jnp.where(views == 2, 2.0, 1.0).reshape(-1) / esum * factor
    image_scale = factor / mass
    mine = (d * n + p)
    my_view = lax.dynamic_slice_in_dim(views.reshape(-1), mine * sr, sr)
    my_scale = lax.dynamic_slice_in_dim(crop_scale, mine * sr, sr)
    my_image = lax.dynamic_slice_in_dim(image_scale, mine * tr, tr)
    slot = jnp.arange(tr)
    pick = (slot[None, :] // 2 == jnp.arange(sr)[:, None] // per) & (slot[None, :] % 2 != my_view[:, None])
    target = jnp.sum(jnp.where(pick, my_image[None, :], 0.0)[:, :, None] * out[None, sr:], axis=1)
    dzn = my_scale[:, None] * out[:sr] - target
    zs, zi = zn[:sr], zinv[:sr]
    dz = (zi * (dzn - zs * jnp.sum(zs * dzn, axis=1, keepdims=True))).astype(BF16)
    dz = send_all(dz, "proto").reshape(rows, bot)
    dz = dot(order, dz, ((0,), (0,))).astype(BF16)
    dzs = over_dp(dz)

    tslot = jnp.arange(2 * img)
    picks = (tslot[None, None, :] // 2 == at[None, :, None] // per) & (tslot[None, None, :] % 2 != views[:, :, None])
    own = lax.dot_general(
        picks.astype(BF16), student.reshape(nd, rows, bot), (((1,), (1,)), ((0,), (0,))), preferred_element_type=F32
    ).reshape(nd * 2 * img, bot)
    left = (student.astype(F32) * crop_scale[:, None]).astype(BF16)
    right = (own * image_scale[:, None]).astype(BF16)
    dpn = dot(left, exb, ((0,), (0,))) - dot(right, lastb, ((0,), (0,)))
    gp = pinv * (dpn - pn * jnp.sum(pn * dpn, axis=0, keepdims=True))
    gps = over_dp(gp)
    grad_protos = jnp.zeros(protos.shape, F32)
    for s in range(nd):
        grad_protos = lax.dynamic_update_slice_in_dim(grad_protos, gps[s], (d ^ s) * cols, 1)

    w1_parts, w2_parts = [], []
    for s in range(nd):
        if s:
            hid, slp = gelu_parts(jnp.dot(feats[s], head_w1, preferred_element_type=F32))
        else:
            hid, slp = hidden, slope
        w2_parts.append(dot(hid, dzs[s], ((0,), (0,))))
        dhid = (dot(dzs[s], head_w2, ((1,), (1,))) * slp).astype(BF16)
        w1_parts.append(dot(feats[s], dhid, ((0,), (0,))))
    grad_w1, grad_w2 = tree_sum(w1_parts), tree_sum(w2_parts)
    slopes = early[:, :rows].transpose(1, 0, 2).reshape(rows, -1)
    w2_all = early[:, rows:].reshape(n, -1, head_w1.shape[1], head_w1.shape[1]).transpose(1, 3, 0, 2)
    w2_all = w2_all.reshape(bot, -1)
    dhid = (jnp.dot(dz, w2_all, preferred_element_type=F32) * slopes).astype(BF16)
    grad_features = dot(dhid, w1_block, ((1,), (1,))).astype(BF16)
    return (grad_features, grad_w1, grad_w2, grad_protos)


def solution(mesh):
    in_specs = (
        P("dp", None),
        P("dp", None),
        P("dp"),
        P("dp"),
        P(None, "proto"),
        P("proto", None),
        P(None, "proto"),
        P(None, "proto"),
        P("proto", None),
        P(None, "proto"),
    )
    out_specs = (P("dp", "proto"), P(None, "proto"), P("proto", None), P(None, "proto"))
    return jax.shard_map(body, mesh=mesh, in_specs=in_specs, out_specs=out_specs, check_vma=False)
```

```python
import jax
import jax.numpy as jnp
from jax import lax
from jax.experimental import pallas as pl
from jax.experimental.pallas import tpu as pltpu
from jax.sharding import PartitionSpec as P

ITERS = 3
ALL = ("dp", "proto")
F32 = jnp.float32
BF16 = jnp.bfloat16


def gelu_parts(act):
    phi = 0.5 * (1.0 + lax.erf(act * 0.7071067811865476))
    slope = phi + act * jnp.exp(-0.5 * act * act) * 0.3989422804014327
    return (act * phi).astype(BF16), slope


def dot(a, b, dims):
    return lax.dot_general(a, b, (dims, ((), ())), preferred_element_type=F32)


def swap(value, axis, step):
    count = lax.axis_size(axis)
    return lax.ppermute(value, axis, [(i, i ^ step) for i in range(count)])


def over_dp(value):
    return [value] + [swap(value, "dp", s) for s in range(1, lax.axis_size("dp"))]


def tree_sum(parts):
    while len(parts) > 1:
        parts = [parts[i] + parts[i + 1] for i in range(0, len(parts), 2)]
    return parts[0]


def send_all(value, axes):
    count = lax.axis_size(axes)
    return lax.all_to_all(jnp.broadcast_to(value[None], (count,) + value.shape), axes, 0, 0)


def unit_cols(mat):
    matf = mat.astype(F32)
    inv = lax.rsqrt(jnp.sum(matf * matf, axis=0, keepdims=True) + 1e-06)
    return matf * inv, inv


def general_body(
    features,
    teacher_features,
    crop_image,
    crop_view,
    head_w1,
    head_w2,
    protos,
    teacher_w1,
    teacher_w2,
    teacher_protos,
):
    nd, n = lax.axis_size("dp"), lax.axis_size("proto")
    d, p = lax.axis_index("dp"), lax.axis_index("proto")
    rows, img = features.shape[0], teacher_features.shape[0] // 2
    per = rows // img
    sr, tr = rows // n, 2 * img // n
    bot = head_w2.shape[1]
    factor = 10.0 / (18 * img * nd)
    absolute = d ^ jnp.arange(nd)

    im = crop_image - d * img
    at = jnp.arange(rows, dtype=jnp.int32)
    rank = jnp.sum((im[:, None] == im[None, :]) & (at[None, :] < at[:, None]), axis=1)
    place = im * per + rank
    hit = at[:, None] == place[None, :]
    order = hit.astype(BF16)
    view = jnp.sum(jnp.where(hit, crop_view[None, :], 0), axis=1)
    views = jnp.stack(over_dp(view))[absolute]

    w1_block = lax.all_to_all(head_w1, "proto", split_axis=0, concat_axis=1, tiled=True)
    feats = over_dp(features)
    act = jnp.dot(features, head_w1, preferred_element_type=F32)
    hidden, slope = gelu_parts(act)
    zpart = jnp.dot(hidden, head_w2, preferred_element_type=F32).astype(BF16)
    zpart = jnp.dot(order, zpart, preferred_element_type=F32).astype(BF16)
    tact = jnp.dot(teacher_features, teacher_w1, preferred_element_type=F32)
    thidden, _ = gelu_parts(tact)
    tpart = jnp.dot(thidden, teacher_w2, preferred_element_type=F32).astype(BF16)
    parts = jnp.concatenate([zpart.reshape(n, sr, bot), tpart.reshape(n, tr, bot)], axis=1)
    parts = lax.all_to_all(parts, "proto", 0, 0)
    early = jnp.concatenate(
        [(slope - 0.5).astype(BF16)] + [head_w2[:, i : i + head_w1.shape[1]] for i in range(0, bot, head_w1.shape[1])],
        axis=0,
    )
    early = lax.all_gather(early, "proto")
    zrow = jnp.sum(parts.astype(F32), axis=0)
    zinv = lax.rsqrt(jnp.sum(zrow * zrow, axis=1, keepdims=True) + 1e-06)
    zn = zrow * zinv
    znb = send_all(zn.astype(BF16), "proto")
    znb = jnp.stack(over_dp(znb))[absolute]
    student = znb[:, :, :sr].reshape(nd * rows, bot)
    teacher = znb[:, :, sr:].reshape(nd * 2 * img, bot)

    cols = protos.shape[1] // nd
    pn, pinv = unit_cols(lax.dynamic_slice_in_dim(protos, d * cols, cols, 1))
    pnb = pn.astype(BF16)
    tpnb = unit_cols(lax.dynamic_slice_in_dim(teacher_protos, d * cols, cols, 1))[0].astype(BF16)

    kern = jnp.exp(jnp.dot(teacher, tpnb, preferred_element_type=F32) / 0.07)
    ex = jnp.exp(jnp.dot(student, pnb, preferred_element_type=F32) / 0.1)
    esum = jnp.sum(ex, axis=1)
    exb = ex.astype(BF16)
    sums = dot(exb, pnb, ((1,), (1,)))
    colscale = 1.0 / jnp.sum(kern, axis=0)
    for step in range(ITERS - 1):
        mass = jnp.sum(send_all(jnp.sum(kern * colscale[None, :], axis=1), ALL), axis=0)
        colscale = 1.0 / jnp.sum(kern / mass[:, None], axis=0)
    last = kern * colscale[None, :]
    lastb = last.astype(BF16)
    tsums = dot(lastb, pnb, ((1,), (1,)))
    tot = jnp.sum(send_all(jnp.concatenate([esum, jnp.sum(last, axis=1)]), ALL), axis=0)
    esum, mass = tot[: nd * rows], tot[nd * rows :]

    out = jnp.concatenate([sums.reshape(nd, n, sr, bot), tsums.reshape(nd, n, tr, bot)], axis=2)
    out = out[absolute]
    out = tree_sum([out[0]] + [swap(out[s], "dp", s) for s in range(1, nd)])
    out = jnp.sum(lax.all_to_all(out, "proto", 0, 0), axis=0)
    crop_scale = jnp.where(views == 2, 2.0, 1.0).reshape(-1) / esum * factor
    image_scale = factor / mass
    mine = (d * n + p)
    my_view = lax.dynamic_slice_in_dim(views.reshape(-1), mine * sr, sr)
    my_scale = lax.dynamic_slice_in_dim(crop_scale, mine * sr, sr)
    my_image = lax.dynamic_slice_in_dim(image_scale, mine * tr, tr)
    slot = jnp.arange(tr)
    pick = (slot[None, :] // 2 == jnp.arange(sr)[:, None] // per) & (slot[None, :] % 2 != my_view[:, None])
    target = jnp.sum(jnp.where(pick, my_image[None, :], 0.0)[:, :, None] * out[None, sr:], axis=1)
    dzn = my_scale[:, None] * out[:sr] - target
    zs, zi = zn[:sr], zinv[:sr]
    dz = (zi * (dzn - zs * jnp.sum(zs * dzn, axis=1, keepdims=True))).astype(BF16)
    dz = send_all(dz, "proto").reshape(rows, bot)
    dz = dot(order, dz, ((0,), (0,))).astype(BF16)
    dzs = over_dp(dz)

    tslot = jnp.arange(2 * img)
    picks = (tslot[None, None, :] // 2 == at[None, :, None] // per) & (tslot[None, None, :] % 2 != views[:, :, None])
    own = lax.dot_general(
        picks.astype(BF16), student.reshape(nd, rows, bot), (((1,), (1,)), ((0,), (0,))), preferred_element_type=F32
    ).reshape(nd * 2 * img, bot)
    left = (student.astype(F32) * crop_scale[:, None]).astype(BF16)
    right = (own * image_scale[:, None]).astype(BF16)
    dpn = dot(left, exb, ((0,), (0,))) - dot(right, lastb, ((0,), (0,)))
    gp = pinv * (dpn - pn * jnp.sum(pn * dpn, axis=0, keepdims=True))
    gps = over_dp(gp)
    grad_protos = jnp.zeros(protos.shape, F32)
    for s in range(nd):
        grad_protos = lax.dynamic_update_slice_in_dim(grad_protos, gps[s], (d ^ s) * cols, 1)

    w1_parts, w2_parts = [], []
    for s in range(nd):
        if s:
            hid, slp = gelu_parts(jnp.dot(feats[s], head_w1, preferred_element_type=F32))
        else:
            hid, slp = hidden, slope
        w2_parts.append(dot(hid, dzs[s], ((0,), (0,))))
        dhid = (dot(dzs[s], head_w2, ((1,), (1,))) * slp).astype(BF16)
        w1_parts.append(dot(feats[s], dhid, ((0,), (0,))))
    grad_w1, grad_w2 = tree_sum(w1_parts), tree_sum(w2_parts)
    slopes = 0.5 + early[:, :rows].astype(F32).transpose(1, 0, 2).reshape(rows, -1)
    w2_all = early[:, rows:].reshape(n, -1, head_w1.shape[1], head_w1.shape[1]).transpose(1, 3, 0, 2)
    w2_all = w2_all.reshape(bot, -1)
    dhid = (jnp.dot(dz, w2_all, preferred_element_type=F32) * slopes).astype(BF16)
    grad_features = dot(dhid, w1_block, ((1,), (1,))).astype(BF16)
    return (grad_features, grad_w1, grad_w2, grad_protos)


def vmem(*shapes):
    return pl.BlockSpec(memory_space=pltpu.VMEM)


WHOLE = pl.BlockSpec(memory_space=pltpu.VMEM)


def call(kernel, outs, *args, **extra):
    params = dict(vmem_limit_bytes=48 * 1024 * 1024)
    return pl.pallas_call(
        kernel,
        out_shape=outs,
        in_specs=[pl.BlockSpec(memory_space=pltpu.VMEM)] * len(args),
        out_specs=jax.tree.map(lambda _: pl.BlockSpec(memory_space=pltpu.VMEM), outs),
        compiler_params=pltpu.CompilerParams(**params),
        **extra,
    )(*args)


def unsort_kernel(got_ref, back_ref, out_ref):
    n, slot, bot = got_ref.shape
    rows = back_ref.shape[0]
    sr = rows // n
    got = got_ref[...].astype(F32)
    dz = got[:, :sr].reshape(rows, bot).astype(BF16)
    out_ref[:rows] = dot(back_ref[...], dz, ((1,), (0,))).astype(BF16)
    out_ref[rows:] = got[:, sr:].reshape(n * (slot - sr), bot).astype(BF16)


def features_kernel(dz_ref, early_ref, w1_ref, out_ref, acc_ref):
    rows = dz_ref.shape[0]
    hs = early_ref.shape[2]
    step = pl.program_id(0)

    @pl.when(step == 0)
    def _():
        acc_ref[...] = jnp.zeros_like(acc_ref)

    early = early_ref[...]
    w2 = jnp.concatenate([early[:, rows : rows + hs], early[:, rows + hs :]], axis=2)
    w2 = w2.reshape(2 * hs, 2 * hs)
    pre = dot(dz_ref[...], w2, ((1,), (1,)))
    slope = jnp.concatenate([early[0, :rows], early[1, :rows]], axis=1).astype(F32) + 0.5
    dhid = (pre * slope).astype(BF16)
    w1 = jnp.concatenate([w1_ref[0], w1_ref[1]], axis=1)
    acc_ref[...] += dot(dhid, w1, ((1,), (1,)))

    @pl.when(step == pl.num_programs(0) - 1)
    def _():
        out_ref[...] = acc_ref[...].astype(BF16)


def feature_grads(dz, early, w1_block):
    n, tall, hs = early.shape
    width = w1_block.shape[1]
    rows, bot = dz.shape
    return pl.pallas_call(
        features_kernel,
        grid=(n // 2,),
        out_shape=jax.ShapeDtypeStruct((rows, width), BF16),
        in_specs=[
            pl.BlockSpec((rows, bot), lambda k: (0, 0)),
            pl.BlockSpec((2, tall, hs), lambda k: (k, 0, 0)),
            pl.BlockSpec((2, width, hs), lambda k: (k, 0, 0)),
        ],
        out_specs=pl.BlockSpec((rows, width), lambda k: (0, 0)),
        scratch_shapes=[pltpu.VMEM((rows, width), F32)],
        compiler_params=pltpu.CompilerParams(vmem_limit_bytes=32 * 1024 * 1024),
    )(dz, early, w1_block)


def weights_kernel(f0_ref, f1_ref, dz0_ref, dz1_ref, h0_ref, h1_ref, s0_ref, s1_ref, w2_ref, g1_ref, g2_ref):
    g1, g2 = [], []
    rows = f0_ref.shape[0]
    for f, z, h, s in ((f0_ref, dz0_ref, h0_ref, s0_ref), (f1_ref, dz1_ref, h1_ref, s1_ref)):
        dz = z[:rows]
        g2.append(dot(h[...], dz, ((0,), (0,))))
        dhid = (dot(dz, w2_ref[...], ((1,), (1,))) * s[...]).astype(BF16)
        g1.append(dot(dhid, f[...], ((0,), (0,))))
    g1_ref[...] = (g1[0] + g1[1]).T
    g2_ref[...] = g2[0] + g2[1]


def protos_kernel(d_ref, protos_ref, own_ref, other_ref, left_ref, right_ref, lown_ref, lother_ref, out_ref):
    half = pl.program_id(0) // (pl.num_programs(0) // 2)
    mine = half == d_ref[0]
    first = d_ref[0] == 0
    a, b = left_ref[...].astype(F32), right_ref[...].astype(F32)
    scaled = jnp.concatenate([jnp.where(first, a, b), jnp.where(first, b, a)], axis=0).astype(BF16)

    def finish(dpn_ref, last_ref):
        mat = protos_ref[...].astype(F32)
        inv = lax.rsqrt(jnp.sum(mat * mat, axis=0, keepdims=True) + 1e-06)
        pn = mat * inv
        dpn = dpn_ref[...] - dot(scaled, last_ref[...], ((0,), (0,)))
        out_ref[...] = inv * (dpn - pn * jnp.sum(pn * dpn, axis=0, keepdims=True))

    @pl.when(mine)
    def _():
        finish(own_ref, lown_ref)

    @pl.when(jnp.logical_not(mine))
    def _():
        finish(other_ref, lother_ref)


def protos_grads(d, protos, own, other, mine, yours, lown, lother):
    bot, wide = protos.shape
    tile = 512
    steps = wide // tile
    halfsteps = steps // 2
    teach = lown.shape[0]

    def place(i, d_ref, same):
        at = d_ref[0] if same else 1 - d_ref[0]
        return (0, jnp.clip(i - at * halfsteps, 0, halfsteps - 1))

    own_map = lambda i, d_ref: place(i, d_ref, True)
    other_map = lambda i, d_ref: place(i, d_ref, False)
    return pl.pallas_call(
        protos_kernel,
        grid_spec=pltpu.PrefetchScalarGridSpec(
            num_scalar_prefetch=1,
            grid=(steps,),
            in_specs=[
                pl.BlockSpec((bot, tile), lambda i, d_ref: (0, i)),
                pl.BlockSpec((bot, tile), own_map),
                pl.BlockSpec((bot, tile), other_map),
                pl.BlockSpec((teach // 2, bot), lambda i, d_ref: (0, 0)),
                pl.BlockSpec((teach // 2, bot), lambda i, d_ref: (0, 0)),
                pl.BlockSpec((teach, tile), own_map),
                pl.BlockSpec((teach, tile), other_map),
            ],
            out_specs=pl.BlockSpec((bot, tile), lambda i, d_ref: (0, i)),
        ),
        out_shape=jax.ShapeDtypeStruct((bot, wide), F32),
        compiler_params=pltpu.CompilerParams(vmem_limit_bytes=32 * 1024 * 1024),
    )(d.reshape(1), protos, own, other, mine, yours, lown, lother)


def by_dp(d, own, other):
    return jnp.stack([jnp.where(d == 0, own, other), jnp.where(d == 0, other, own)])


def paired_body(
    features,
    teacher_features,
    crop_image,
    crop_view,
    head_w1,
    head_w2,
    protos,
    teacher_w1,
    teacher_w2,
    teacher_protos,
):
    nd, n = lax.axis_size("dp"), lax.axis_size("proto")
    d, p = lax.axis_index("dp"), lax.axis_index("proto")
    rows, img = features.shape[0], teacher_features.shape[0] // 2
    per = rows // img
    sr, tr = rows // n, 2 * img // n
    bot, hs = head_w2.shape[1], head_w2.shape[0]
    factor = 10.0 / (18 * img * nd)

    w1_block = lax.all_to_all(head_w1.reshape(n, -1, hs), "proto", 0, 0)

    im = crop_image - d * img
    at = jnp.arange(rows, dtype=jnp.int32)
    rank = jnp.sum((im[:, None] == im[None, :]) & (at[None, :] < at[:, None]), axis=1)
    place = im * per + rank
    hit = at[:, None] == place[None, :]
    order = hit.astype(BF16)
    back = (place[:, None] == at[None, :]).astype(BF16)
    view = jnp.sum(jnp.where(hit, crop_view[None, :], 0), axis=1)
    view_other = swap(view, "dp", 1)

    feat_other = swap(features, "dp", 1)
    act = jnp.dot(features, head_w1, preferred_element_type=F32)
    hidden, slope = gelu_parts(act)
    zpart = jnp.dot(hidden, head_w2, preferred_element_type=F32).astype(BF16)
    zpart = jnp.dot(order, zpart, preferred_element_type=F32).astype(BF16)
    tact = jnp.dot(teacher_features, teacher_w1, preferred_element_type=F32)
    thidden, _ = gelu_parts(tact)
    tpart = jnp.dot(thidden, teacher_w2, preferred_element_type=F32).astype(BF16)
    parts = jnp.concatenate([zpart.reshape(n, sr, bot), tpart.reshape(n, tr, bot)], axis=1)
    early = jnp.concatenate([(slope - 0.5).astype(BF16), head_w2[:, :hs], head_w2[:, hs:]], axis=0)
    parts, w1_block = lax.optimization_barrier((parts, w1_block))
    early = lax.all_gather(early, "proto")
    parts = lax.all_to_all(parts, "proto", 0, 0)
    zrow = jnp.sum(parts.astype(F32), axis=0)
    zinv = lax.rsqrt(jnp.sum(zrow * zrow, axis=1, keepdims=True) + 1e-06)
    zn = zrow * zinv
    znb = zn.astype(BF16)
    got = send_all(znb, "proto")
    got_other = swap(got, "dp", 1)
    teacher = by_dp(d, got[:, sr:], got_other[:, sr:]).reshape(nd * 2 * img, bot)
    student = jnp.concatenate([got[:, :sr].reshape(rows, bot), got_other[:, :sr].reshape(rows, bot)], axis=0)

    cols = protos.shape[1] // nd
    pn, pinv = unit_cols(lax.dynamic_slice_in_dim(protos, d * cols, cols, 1))
    pnb = pn.astype(BF16)
    tpnb = unit_cols(lax.dynamic_slice_in_dim(teacher_protos, d * cols, cols, 1))[0].astype(BF16)

    kern = jnp.exp(jnp.dot(teacher, tpnb, preferred_element_type=F32) / 0.07)
    colscale = 1.0 / jnp.sum(kern, axis=0)
    mass = jnp.sum(send_all(jnp.sum(kern * colscale[None, :], axis=1), ALL), axis=0)
    ex = jnp.exp(jnp.dot(student, pnb, preferred_element_type=F32) / 0.1)
    esum = jnp.sum(ex, axis=1)
    exb = ex.astype(BF16)
    sums = dot(exb, pnb, ((1,), (1,)))
    sums_own, sums_other = sums[:rows], swap(sums[rows:], "dp", 1)
    colscale = 1.0 / jnp.sum(kern / mass[:, None], axis=0)
    esum = by_dp(d, esum[:rows], esum[rows:]).reshape(-1)
    tot = jnp.sum(send_all(jnp.concatenate([jnp.sum(kern * colscale[None, :], axis=1), esum]), ALL), axis=0)
    mass, esum = tot[: nd * 2 * img], tot[nd * 2 * img :]
    colscale = 1.0 / jnp.sum(kern / mass[:, None], axis=0)
    last = kern * colscale[None, :]
    lastb = last.astype(BF16)
    tsums = dot(lastb, pnb, ((1,), (1,)))
    tmass = jnp.sum(last, axis=1)

    tail = jnp.concatenate([tsums, jnp.broadcast_to(tmass[:, None], tsums.shape)], axis=1)
    tail = tail.reshape(nd, n, tr, 2 * bot)
    tail = jnp.where(d == 0, tail[0], tail[1]) + swap(jnp.where(d == 0, tail[1], tail[0]), "dp", 1)
    out = jnp.concatenate(
        [(sums_own + sums_other).reshape(n, sr, bot), tail[:, :, :bot], tail[:, :, bot:]], axis=1
    )
    out = jnp.sum(lax.all_to_all(out, "proto", 0, 0), axis=0)
    views = jnp.concatenate([view, view_other])
    count = jnp.where(views == 2, 2.0, 1.0)
    esum = esum.reshape(nd, rows)
    crop_scale = count * factor / jnp.concatenate([esum[d], esum[1 - d]])
    my_view = lax.dynamic_slice_in_dim(view, p * sr, sr)
    my_scale = lax.dynamic_slice_in_dim(crop_scale, p * sr, sr)
    my_image = factor / out[sr + tr :, 0]
    slot = jnp.arange(tr)
    pick = (slot[None, :] // 2 == jnp.arange(sr)[:, None] // per) & (slot[None, :] % 2 != my_view[:, None])
    pick = jnp.where(pick, my_image[None, :], 0.0)
    target = jnp.sum(pick[:, :, None] * out[None, sr : sr + tr], axis=1)
    dzn = my_scale[:, None] * out[:sr] - target
    zs, zi = zn[:sr], zinv[:sr]
    dz = (zi * (dzn - zs * jnp.sum(zs * dzn, axis=1, keepdims=True))).astype(BF16)
    own = jnp.sum(pick[:, :, None] * znb[:sr, None, :].astype(F32), axis=0).astype(BF16)
    got4 = send_all(jnp.concatenate([dz, own], axis=0), "proto")

    left = (student.astype(F32) * crop_scale[:, None]).astype(BF16)
    dpn = dot(left, exb, ((0,), (0,)))
    dpn_other, last_other = swap(dpn, "dp", 1), swap(lastb, "dp", 1)

    act_other = jnp.dot(feat_other, head_w1, preferred_element_type=F32)
    hidden_other, slope_other = gelu_parts(act_other)

    dz = call(unsort_kernel, jax.ShapeDtypeStruct((rows + 2 * img, bot), BF16), got4, back)
    dz_other = swap(dz, "dp", 1)
    grad_features = feature_grads(dz[:rows], early, w1_block)
    grad_w1, grad_w2 = call(
        weights_kernel,
        (jax.ShapeDtypeStruct(head_w1.shape, F32), jax.ShapeDtypeStruct(head_w2.shape, F32)),
        features, feat_other, dz, dz_other, hidden, hidden_other, slope, slope_other, head_w2,
    )
    grad_protos = protos_grads(
        d, protos, dpn, dpn_other, dz[rows:], dz_other[rows:], lastb, last_other
    )
    return (grad_features, grad_w1, grad_w2, grad_protos)


def body(features, teacher_features, *rest):
    n = lax.axis_size("proto")
    slot = (features.shape[0] // n, teacher_features.shape[0] // n)
    paired = lax.axis_size("dp") == 2 and n % 2 == 0 and slot[0] % 8 == 0 and slot[1] % 8 == 0
    return (paired_body if paired else general_body)(features, teacher_features, *rest)


def solution(mesh):
    in_specs = (
        P("dp", None),
        P("dp", None),
        P("dp"),
        P("dp"),
        P(None, "proto"),
        P("proto", None),
        P(None, "proto"),
        P(None, "proto"),
        P("proto", None),
        P(None, "proto"),
    )
    out_specs = (P("dp", "proto"), P(None, "proto"), P("proto", None), P(None, "proto"))
    return jax.shard_map(body, mesh=mesh, in_specs=in_specs, out_specs=out_specs, check_vma=False)
```

```python
import functools

import jax
import jax.numpy as jnp
from jax import lax
from jax.experimental import pallas as pl
from jax.experimental.pallas import tpu as pltpu
from jax.sharding import PartitionSpec as P

ITERS = 3
ALL = ("dp", "proto")
F32 = jnp.float32
BF16 = jnp.bfloat16


def gelu_parts(act):
    phi = 0.5 * (1.0 + lax.erf(act * 0.7071067811865476))
    slope = phi + act * jnp.exp(-0.5 * act * act) * 0.3989422804014327
    return (act * phi).astype(BF16), slope


def dot(a, b, dims):
    return lax.dot_general(a, b, (dims, ((), ())), preferred_element_type=F32)


def swap(value, axis, step):
    count = lax.axis_size(axis)
    return lax.ppermute(value, axis, [(i, i ^ step) for i in range(count)])


def over_dp(value):
    return [value] + [swap(value, "dp", s) for s in range(1, lax.axis_size("dp"))]


def tree_sum(parts):
    while len(parts) > 1:
        parts = [parts[i] + parts[i + 1] for i in range(0, len(parts), 2)]
    return parts[0]


def send_all(value, axes):
    count = lax.axis_size(axes)
    return lax.all_to_all(jnp.broadcast_to(value[None], (count,) + value.shape), axes, 0, 0)


def unit_cols(mat):
    matf = mat.astype(F32)
    inv = lax.rsqrt(jnp.sum(matf * matf, axis=0, keepdims=True) + 1e-06)
    return matf * inv, inv


def general_body(
    features,
    teacher_features,
    crop_image,
    crop_view,
    head_w1,
    head_w2,
    protos,
    teacher_w1,
    teacher_w2,
    teacher_protos,
):
    nd, n = lax.axis_size("dp"), lax.axis_size("proto")
    d, p = lax.axis_index("dp"), lax.axis_index("proto")
    rows, img = features.shape[0], teacher_features.shape[0] // 2
    per = rows // img
    sr, tr = rows // n, 2 * img // n
    bot = head_w2.shape[1]
    factor = 10.0 / (18 * img * nd)
    absolute = d ^ jnp.arange(nd)

    im = crop_image - d * img
    at = jnp.arange(rows, dtype=jnp.int32)
    rank = jnp.sum((im[:, None] == im[None, :]) & (at[None, :] < at[:, None]), axis=1)
    place = im * per + rank
    hit = at[:, None] == place[None, :]
    order = hit.astype(BF16)
    view = jnp.sum(jnp.where(hit, crop_view[None, :], 0), axis=1)
    views = jnp.stack(over_dp(view))[absolute]

    w1_block = lax.all_to_all(head_w1, "proto", split_axis=0, concat_axis=1, tiled=True)
    feats = over_dp(features)
    act = jnp.dot(features, head_w1, preferred_element_type=F32)
    hidden, slope = gelu_parts(act)
    zpart = jnp.dot(hidden, head_w2, preferred_element_type=F32).astype(BF16)
    zpart = jnp.dot(order, zpart, preferred_element_type=F32).astype(BF16)
    tact = jnp.dot(teacher_features, teacher_w1, preferred_element_type=F32)
    thidden, _ = gelu_parts(tact)
    tpart = jnp.dot(thidden, teacher_w2, preferred_element_type=F32).astype(BF16)
    parts = jnp.concatenate([zpart.reshape(n, sr, bot), tpart.reshape(n, tr, bot)], axis=1)
    parts = lax.all_to_all(parts, "proto", 0, 0)
    early = jnp.concatenate(
        [(slope - 0.5).astype(BF16)] + [head_w2[:, i : i + head_w1.shape[1]] for i in range(0, bot, head_w1.shape[1])],
        axis=0,
    )
    early = lax.all_gather(early, "proto")
    zrow = jnp.sum(parts.astype(F32), axis=0)
    zinv = lax.rsqrt(jnp.sum(zrow * zrow, axis=1, keepdims=True) + 1e-06)
    zn = zrow * zinv
    znb = send_all(zn.astype(BF16), "proto")
    znb = jnp.stack(over_dp(znb))[absolute]
    student = znb[:, :, :sr].reshape(nd * rows, bot)
    teacher = znb[:, :, sr:].reshape(nd * 2 * img, bot)

    cols = protos.shape[1] // nd
    pn, pinv = unit_cols(lax.dynamic_slice_in_dim(protos, d * cols, cols, 1))
    pnb = pn.astype(BF16)
    tpnb = unit_cols(lax.dynamic_slice_in_dim(teacher_protos, d * cols, cols, 1))[0].astype(BF16)

    kern = jnp.exp(jnp.dot(teacher, tpnb, preferred_element_type=F32) / 0.07)
    ex = jnp.exp(jnp.dot(student, pnb, preferred_element_type=F32) / 0.1)
    esum = jnp.sum(ex, axis=1)
    exb = ex.astype(BF16)
    sums = dot(exb, pnb, ((1,), (1,)))
    colscale = 1.0 / jnp.sum(kern, axis=0)
    for step in range(ITERS - 1):
        mass = jnp.sum(send_all(jnp.sum(kern * colscale[None, :], axis=1), ALL), axis=0)
        colscale = 1.0 / jnp.sum(kern / mass[:, None], axis=0)
    last = kern * colscale[None, :]
    lastb = last.astype(BF16)
    tsums = dot(lastb, pnb, ((1,), (1,)))
    tot = jnp.sum(send_all(jnp.concatenate([esum, jnp.sum(last, axis=1)]), ALL), axis=0)
    esum, mass = tot[: nd * rows], tot[nd * rows :]

    out = jnp.concatenate([sums.reshape(nd, n, sr, bot), tsums.reshape(nd, n, tr, bot)], axis=2)
    out = out[absolute]
    out = tree_sum([out[0]] + [swap(out[s], "dp", s) for s in range(1, nd)])
    out = jnp.sum(lax.all_to_all(out, "proto", 0, 0), axis=0)
    crop_scale = jnp.where(views == 2, 2.0, 1.0).reshape(-1) / esum * factor
    image_scale = factor / mass
    mine = (d * n + p)
    my_view = lax.dynamic_slice_in_dim(views.reshape(-1), mine * sr, sr)
    my_scale = lax.dynamic_slice_in_dim(crop_scale, mine * sr, sr)
    my_image = lax.dynamic_slice_in_dim(image_scale, mine * tr, tr)
    slot = jnp.arange(tr)
    pick = (slot[None, :] // 2 == jnp.arange(sr)[:, None] // per) & (slot[None, :] % 2 != my_view[:, None])
    target = jnp.sum(jnp.where(pick, my_image[None, :], 0.0)[:, :, None] * out[None, sr:], axis=1)
    dzn = my_scale[:, None] * out[:sr] - target
    zs, zi = zn[:sr], zinv[:sr]
    dz = (zi * (dzn - zs * jnp.sum(zs * dzn, axis=1, keepdims=True))).astype(BF16)
    dz = send_all(dz, "proto").reshape(rows, bot)
    dz = dot(order, dz, ((0,), (0,))).astype(BF16)
    dzs = over_dp(dz)

    tslot = jnp.arange(2 * img)
    picks = (tslot[None, None, :] // 2 == at[None, :, None] // per) & (tslot[None, None, :] % 2 != views[:, :, None])
    own = lax.dot_general(
        picks.astype(BF16), student.reshape(nd, rows, bot), (((1,), (1,)), ((0,), (0,))), preferred_element_type=F32
    ).reshape(nd * 2 * img, bot)
    left = (student.astype(F32) * crop_scale[:, None]).astype(BF16)
    right = (own * image_scale[:, None]).astype(BF16)
    dpn = dot(left, exb, ((0,), (0,))) - dot(right, lastb, ((0,), (0,)))
    gp = pinv * (dpn - pn * jnp.sum(pn * dpn, axis=0, keepdims=True))
    gps = over_dp(gp)
    grad_protos = jnp.zeros(protos.shape, F32)
    for s in range(nd):
        grad_protos = lax.dynamic_update_slice_in_dim(grad_protos, gps[s], (d ^ s) * cols, 1)

    w1_parts, w2_parts = [], []
    for s in range(nd):
        if s:
            hid, slp = gelu_parts(jnp.dot(feats[s], head_w1, preferred_element_type=F32))
        else:
            hid, slp = hidden, slope
        w2_parts.append(dot(hid, dzs[s], ((0,), (0,))))
        dhid = (dot(dzs[s], head_w2, ((1,), (1,))) * slp).astype(BF16)
        w1_parts.append(dot(feats[s], dhid, ((0,), (0,))))
    grad_w1, grad_w2 = tree_sum(w1_parts), tree_sum(w2_parts)
    slopes = 0.5 + early[:, :rows].astype(F32).transpose(1, 0, 2).reshape(rows, -1)
    w2_all = early[:, rows:].reshape(n, -1, head_w1.shape[1], head_w1.shape[1]).transpose(1, 3, 0, 2)
    w2_all = w2_all.reshape(bot, -1)
    dhid = (jnp.dot(dz, w2_all, preferred_element_type=F32) * slopes).astype(BF16)
    grad_features = dot(dhid, w1_block, ((1,), (1,))).astype(BF16)
    return (grad_features, grad_w1, grad_w2, grad_protos)


def params(mib=40):
    return pltpu.CompilerParams(vmem_limit_bytes=mib * 1024 * 1024)


def shape(dims, dtype):
    return jax.ShapeDtypeStruct(dims, dtype)


def call(kernel, outs, scalars, *args, us=1):
    smem = [jnp.asarray(s, jnp.int32).reshape(1) for s in scalars]
    return pl.pallas_call(
        kernel,
        out_shape=outs,
        in_specs=[pl.BlockSpec(memory_space=pltpu.SMEM)] * len(smem)
        + [pl.BlockSpec(memory_space=pltpu.VMEM)] * len(args),
        out_specs=jax.tree.map(lambda _: pl.BlockSpec(memory_space=pltpu.VMEM), outs),
        compiler_params=params(),
        cost_estimate=pl.CostEstimate(flops=us * 10**9, bytes_accessed=us * 10**6, transcendentals=0),
    )(*smem, *args)


def grids(dims):
    return lax.broadcasted_iota(jnp.int32, dims, 0), lax.broadcasted_iota(jnp.int32, dims, 1)


def to_row(col):
    down, along = grids((col.shape[0], col.shape[0]))
    return jnp.sum(jnp.where(down == along, col, jnp.zeros_like(col)), axis=0, keepdims=True)


def to_col(row):
    down, along = grids((row.shape[1], row.shape[1]))
    return jnp.sum(jnp.where(down == along, row, jnp.zeros_like(row)), axis=1, keepdims=True)


def head_kernel(d_ref, f_ref, w1_ref, w2_ref, tf_ref, tw1_ref, tw2_ref, im_ref, view_ref, parts_ref, back_ref, vs_ref):
    rows, teach = f_ref.shape[0], tf_ref.shape[0]
    n = parts_ref.shape[0]
    img = teach // 2
    per = rows // img
    im = (im_ref[...] - d_ref[0] * img).astype(F32)
    down, along = grids((rows, rows))
    imc = to_col(im)
    same = im == imc
    before = jnp.where(same & (along < down), 1.0, 0.0)
    after = jnp.where(same & (down < along), 1.0, 0.0)
    col = (imc * per + jnp.sum(before, axis=1, keepdims=True)).astype(jnp.int32)
    row = (im * per + jnp.sum(after, axis=0, keepdims=True)).astype(jnp.int32)
    back_ref[...] = jnp.where(col == along, 1.0, 0.0).astype(BF16)
    hit = row == down
    vs_ref[...] = jnp.sum(jnp.where(hit, view_ref[...].astype(F32), 0.0), axis=1, keepdims=True)
    order = jnp.where(hit, 1.0, 0.0).astype(BF16)

    def part(x, first, second):
        act = dot(x[...], first[...], ((1,), (0,)))
        hidden = (act * 0.5 * (1.0 + lax.erf(act * 0.7071067811865476))).astype(BF16)
        return dot(hidden, second[...], ((1,), (0,)))

    z = part(f_ref, w1_ref, w2_ref).astype(BF16)
    z = dot(order, z, ((1,), (0,))).reshape(n, rows // n, -1)
    t = part(tf_ref, tw1_ref, tw2_ref).reshape(n, teach // n, -1)
    parts_ref[...] = jnp.concatenate([z, t], axis=1).astype(BF16)


def rows_kernel(parts_ref, out_ref, zn_ref, zinv_ref):
    z = jnp.sum(parts_ref[...].astype(F32), axis=0)
    inv = lax.rsqrt(jnp.sum(z * z, axis=1, keepdims=True) + 1e-06)
    zn = z * inv
    zn_ref[...] = zn
    zinv_ref[...] = inv
    out_ref[...] = jnp.broadcast_to(zn[None], out_ref.shape).astype(BF16)


def row_mass(kern, mass):
    if mass is None:
        scale = 1.0 / jnp.sum(kern, axis=0, keepdims=True)
    else:
        scale = 1.0 / jnp.sum(kern * (1.0 / mass), axis=0, keepdims=True)
    return scale, jnp.sum(kern * scale, axis=1, keepdims=True)


def fold(col):
    row = to_row(col)
    return jnp.concatenate([row[:, k : k + 128] for k in range(0, row.shape[1], 128)], axis=0)


def unfold(block):
    return to_col(jnp.concatenate([block[k : k + 1] for k in range(block.shape[0])], axis=1))


def kern_kernel(d_ref, got_ref, other_ref, tpnb_ref, kern_ref, msg_ref, student_ref):
    n, slot, bot = got_ref.shape
    rows = student_ref.shape[0] // 2
    sr = rows // n
    own, other = got_ref[...].astype(F32), other_ref[...].astype(F32)
    student_ref[:rows] = own[:, :sr].reshape(rows, bot).astype(BF16)
    student_ref[rows:] = other[:, :sr].reshape(rows, bot).astype(BF16)
    own, other = own[:, sr:].reshape(-1, bot), other[:, sr:].reshape(-1, bot)
    first = d_ref[0] == 0
    teacher = jnp.concatenate([jnp.where(first, own, other), jnp.where(first, other, own)], axis=0).astype(BF16)
    kern = jnp.exp(dot(teacher, tpnb_ref[...], ((1,), (0,))) * (1.0 / 0.07))
    kern_ref[...] = kern
    _, mass = row_mass(kern, None)
    msg_ref[...] = jnp.broadcast_to(fold(mass)[None], msg_ref.shape)


def student_kernel(z_ref, pnb_ref, exb_ref, sums_ref, esum_ref):
    step = pl.program_id(0)
    ex = jnp.exp(dot(z_ref[...], pnb_ref[...], ((1,), (0,))) * 10.0)
    esum_ref[pl.ds(step, 1), :] = fold(jnp.sum(ex, axis=1, keepdims=True))
    exb = ex.astype(BF16)
    exb_ref[...] = exb
    sums_ref[...] = dot(exb, pnb_ref[...], ((1,), (1,)))


def student_sums(student, pnb):
    total, bot = student.shape
    cols = pnb.shape[1]
    return pl.pallas_call(
        student_kernel,
        grid=(total // 128,),
        out_shape=(shape((total, cols), BF16), shape((total, bot), F32), shape((total // 128, 128), F32)),
        in_specs=[pl.BlockSpec((128, bot), lambda i: (i, 0)), pl.BlockSpec((bot, cols), lambda i: (0, 0))],
        out_specs=(
            pl.BlockSpec((128, cols), lambda i: (i, 0)),
            pl.BlockSpec((128, bot), lambda i: (i, 0)),
            pl.BlockSpec((total // 128, 128), lambda i: (0, 0)),
        ),
        compiler_params=params(),
        cost_estimate=pl.CostEstimate(flops=5 * 10**9, bytes_accessed=10**7, transcendentals=0),
    )(student, pnb)


def second_kernel(d_ref, got_ref, kern_ref, esum_ref, msg_ref):
    mass = unfold(jnp.sum(got_ref[...], axis=0))
    _, mass = row_mass(kern_ref[...], mass)
    half = esum_ref.shape[0] // 2
    esum = esum_ref[...]
    turned = jnp.concatenate([esum[half:], esum[:half]], axis=0)
    esum = jnp.where(d_ref[0] == 0, esum, turned)
    msg_ref[...] = jnp.broadcast_to(jnp.concatenate([fold(mass), esum], axis=0)[None], msg_ref.shape)


def third_kernel(d_ref, got_ref, kern_ref, pnb_ref, esum_ref, last_ref, mine_ref, yours_ref):
    teach = kern_ref.shape[0]
    got = jnp.sum(got_ref[...], axis=0)
    top = teach // 128
    esum_ref[...] = got[top:]
    kern = kern_ref[...]
    scale, mass = row_mass(kern, unfold(got[:top]))
    last = (kern * scale).astype(BF16)
    last_ref[...] = last
    sums = dot(last, pnb_ref[...], ((1,), (1,)))
    sums = jnp.concatenate([sums, jnp.broadcast_to(mass, (teach, 128))], axis=1)
    half = teach // 2
    first = d_ref[0] == 0
    mine_ref[...] = jnp.where(first, sums[:half], sums[half:])
    yours_ref[...] = jnp.where(first, sums[half:], sums[:half])


def message_kernel(a0_ref, a1_ref, b0_ref, b1_ref, out_ref):
    n = out_ref.shape[0]
    rows, bot = a0_ref.shape
    sums = (a0_ref[...] + a1_ref[...]).reshape(n, rows // n, bot)
    both = b0_ref[...] + b1_ref[...]
    mass = both[:, bot:]
    high = mass.astype(BF16).astype(F32)
    tail = jnp.concatenate([high, mass - high], axis=1)
    teach = both.shape[0]
    both = both[:, :bot].reshape(n, teach // n, bot)
    out_ref[...] = jnp.concatenate([sums, both, tail.reshape(n, teach // n, bot)], axis=1).astype(BF16)


def bottleneck_kernel(factor, got_ref, zn_ref, zinv_ref, view_ref, scale_ref, out_ref):
    sr = view_ref.shape[0]
    tr = zn_ref.shape[0] - sr
    per = sr // (tr // 2)
    out = jnp.sum(got_ref[...].astype(F32), axis=0)
    tail = out[sr + tr :]
    image = factor / (tail[:, :1] + tail[:, 128:129])
    sums = out[sr : sr + tr] * image
    zn, zinv = zn_ref[:sr], zinv_ref[:sr]
    znb = zn.astype(BF16).astype(F32)
    view = view_ref[...].astype(jnp.int32)
    which = lax.broadcasted_iota(jnp.int32, (sr, 1), 0)
    dzn = scale_ref[...] * out[:sr]
    own = []
    for t in range(tr):
        base = (t // 2) * per
        pick = (which >= base) & (which < base + per) & (view != t % 2)
        dzn = dzn - jnp.where(pick, sums[t : t + 1], 0.0)
        own.append(jnp.sum(jnp.where(pick, znb, 0.0), axis=0, keepdims=True) * image[t : t + 1])
    dz = zinv * (dzn - zn * jnp.sum(zn * dzn, axis=1, keepdims=True))
    both = jnp.concatenate([dz] + own, axis=0)
    out_ref[...] = jnp.broadcast_to(both[None], out_ref.shape).astype(BF16)


def hidden_kernel(f0_ref, f1_ref, w1_ref, h0_ref, h1_ref, s0_ref, s1_ref):
    for f, h, s in ((f0_ref, h0_ref, s0_ref), (f1_ref, h1_ref, s1_ref)):
        act = dot(f[...], w1_ref[...], ((1,), (0,))).T
        phi = 0.5 * (1.0 + lax.erf(act * 0.7071067811865476))
        h[...] = (act * phi).astype(BF16)
        s[...] = phi + act * jnp.exp(-0.5 * act * act) * 0.3989422804014327


def slopes_kernel(d_ref, p_ref, f_ref, own_ref, other_ref, slope_ref, w2_ref, w1_ref):
    hs = own_ref.shape[2]
    deep = f_ref.shape[1] // 2
    first = d_ref[0] == 0
    own, other = own_ref[...], other_ref[...]
    low = jnp.where(first, own, other)
    high = jnp.where(first, other, own)
    a, b = (jnp.concatenate([x[0], x[1]], axis=1) for x in (low[:, :deep], high[:, :deep]))
    act = dot(f_ref[:, :deep], a, ((1,), (0,))) + dot(f_ref[:, deep:], b, ((1,), (0,)))
    phi = 0.5 * (1.0 + lax.erf(act * 0.7071067811865476))
    slope_ref[...] = phi + act * jnp.exp(-0.5 * act * act) * 0.3989422804014327
    width = w1_ref.shape[0]
    blocks = deep // width
    at = pl.multiple_of(lax.rem(p_ref[0], blocks) * width, width)
    mine = (p_ref[0] // blocks) == d_ref[0]
    rows = jnp.where(mine, own_ref[:, pl.ds(at, width)], other_ref[:, pl.ds(at, width)])
    w1_ref[...] = jnp.concatenate([rows[0], rows[1]], axis=1)
    half = hs // 2
    for k in range(2):
        for part, x in ((0, low), (1, high)):
            tail = jnp.concatenate([x[k, deep : deep + half], x[k, deep + half :]], axis=1)
            w2_ref[k * hs + part * half : k * hs + (part + 1) * half] = tail


def slopes_of(d, p, features, own, other, width):
    n, tall, hs = own.shape
    rows = features.shape[0]
    whole = lambda k, d, p: (0, 0)
    return pl.pallas_call(
        slopes_kernel,
        grid_spec=pltpu.PrefetchScalarGridSpec(
            num_scalar_prefetch=2,
            grid=(n // 2,),
            in_specs=[
                pl.BlockSpec(features.shape, whole),
                pl.BlockSpec((2, tall, hs), lambda k, d, p: (k, 0, 0)),
                pl.BlockSpec((2, tall, hs), lambda k, d, p: (k, 0, 0)),
            ],
            out_specs=(
                pl.BlockSpec((rows, 2 * hs), lambda k, d, p: (0, k)),
                pl.BlockSpec((2 * hs, 2 * hs), lambda k, d, p: (k, 0)),
                pl.BlockSpec((width, 2 * hs), lambda k, d, p: (0, k)),
            ),
        ),
        out_shape=(shape((rows, n * hs), F32), shape((n * hs, 2 * hs), BF16), shape((width, n * hs), BF16)),
        compiler_params=params(),
        cost_estimate=pl.CostEstimate(flops=10**10, bytes_accessed=3 * 10**7, transcendentals=0),
    )(d.reshape(1), p.reshape(1), features, own, other)


def unsort_kernel(got_ref, back_ref, out_ref):
    n, slot, bot = got_ref.shape
    rows = back_ref.shape[0]
    sr = rows // n
    got = got_ref[...].astype(F32)
    dz = got[:, :sr].reshape(rows, bot).astype(BF16)
    out_ref[:rows] = dot(back_ref[...], dz, ((1,), (0,))).astype(BF16)
    out_ref[rows:] = got[:, sr:].reshape(n * (slot - sr), bot).astype(BF16)


def features_kernel(dz_ref, slope_ref, w2_ref, w1_ref, out_ref, acc_ref):
    step = pl.program_id(0)

    @pl.when(step == 0)
    def _():
        acc_ref[...] = jnp.zeros_like(acc_ref)

    pre = dot(dz_ref[...], w2_ref[...], ((1,), (1,)))
    dhid = (pre * slope_ref[...]).astype(BF16)
    acc_ref[...] += dot(dhid, w1_ref[...], ((1,), (1,)))

    @pl.when(step == pl.num_programs(0) - 1)
    def _():
        out_ref[...] = acc_ref[...].astype(BF16)


def feature_grads(dz, slope, w2, w1_block):
    rows, hidden = slope.shape
    width, bot = w1_block.shape[0], w2.shape[1]
    step = bot
    return pl.pallas_call(
        features_kernel,
        grid=(hidden // step,),
        out_shape=shape((rows, width), BF16),
        in_specs=[
            pl.BlockSpec((rows, bot), lambda k: (0, 0)),
            pl.BlockSpec((rows, step), lambda k: (0, k)),
            pl.BlockSpec((step, bot), lambda k: (k, 0)),
            pl.BlockSpec((width, step), lambda k: (0, k)),
        ],
        out_specs=pl.BlockSpec((rows, width), lambda k: (0, 0)),
        scratch_shapes=[pltpu.VMEM((rows, width), F32)],
        compiler_params=params(),
    )(dz, slope, w2, w1_block)


def weights_kernel(f0_ref, f1_ref, dz0_ref, dz1_ref, h0_ref, h1_ref, s0_ref, s1_ref, w2_ref, g1_ref, g2_ref):
    g1, g2 = [], []
    rows = f0_ref.shape[0]
    for f, z, h, s in ((f0_ref, dz0_ref, h0_ref, s0_ref), (f1_ref, dz1_ref, h1_ref, s1_ref)):
        dz = z[:rows]
        g2.append(dot(h[...], dz, ((1,), (0,))))
        dhid = (dot(w2_ref[...], dz, ((1,), (1,))) * s[...]).astype(BF16)
        g1.append(dot(dhid, f[...], ((1,), (0,))))
    g1_ref[...] = (g1[0] + g1[1]).T
    g2_ref[...] = g2[0] + g2[1]


def protos_kernel(d_ref, protos_ref, own_ref, other_ref, left_ref, right_ref, lown_ref, lother_ref, out_ref):
    half = pl.program_id(0) // (pl.num_programs(0) // 2)
    mine = half == d_ref[0]
    first = d_ref[0] == 0
    a, b = left_ref[...].astype(F32), right_ref[...].astype(F32)
    scaled = jnp.concatenate([jnp.where(first, a, b), jnp.where(first, b, a)], axis=0).astype(BF16)

    def finish(dpn_ref, last_ref):
        mat = protos_ref[...].astype(F32)
        inv = lax.rsqrt(jnp.sum(mat * mat, axis=0, keepdims=True) + 1e-06)
        pn = mat * inv
        dpn = dpn_ref[...] - dot(scaled, last_ref[...], ((0,), (0,)))
        out_ref[...] = inv * (dpn - pn * jnp.sum(pn * dpn, axis=0, keepdims=True))

    @pl.when(mine)
    def _():
        finish(own_ref, lown_ref)

    @pl.when(jnp.logical_not(mine))
    def _():
        finish(other_ref, lother_ref)


def protos_grads(d, protos, own, other, mine, yours, lown, lother):
    bot, wide = protos.shape
    tile = 512
    steps = wide // tile
    halfsteps = steps // 2
    teach = lown.shape[0]

    def place(i, d_ref, same):
        at = d_ref[0] if same else 1 - d_ref[0]
        return (0, jnp.clip(i - at * halfsteps, 0, halfsteps - 1))

    own_map = lambda i, d_ref: place(i, d_ref, True)
    other_map = lambda i, d_ref: place(i, d_ref, False)
    return pl.pallas_call(
        protos_kernel,
        grid_spec=pltpu.PrefetchScalarGridSpec(
            num_scalar_prefetch=1,
            grid=(steps,),
            in_specs=[
                pl.BlockSpec((bot, tile), lambda i, d_ref: (0, i)),
                pl.BlockSpec((bot, tile), own_map),
                pl.BlockSpec((bot, tile), other_map),
                pl.BlockSpec((teach // 2, bot), lambda i, d_ref: (0, 0)),
                pl.BlockSpec((teach // 2, bot), lambda i, d_ref: (0, 0)),
                pl.BlockSpec((teach, tile), own_map),
                pl.BlockSpec((teach, tile), other_map),
            ],
            out_specs=pl.BlockSpec((bot, tile), lambda i, d_ref: (0, i)),
        ),
        out_shape=jax.ShapeDtypeStruct((bot, wide), F32),
        compiler_params=pltpu.CompilerParams(vmem_limit_bytes=32 * 1024 * 1024),
    )(d.reshape(1), protos, own, other, mine, yours, lown, lother)


def tied(*values):
    return lax.optimization_barrier(values)


def paired_body(
    features,
    teacher_features,
    crop_image,
    crop_view,
    head_w1,
    head_w2,
    protos,
    teacher_w1,
    teacher_w2,
    teacher_protos,
):
    nd, n = lax.axis_size("dp"), lax.axis_size("proto")
    d, p = lax.axis_index("dp"), lax.axis_index("proto")
    rows, teach = features.shape[0], teacher_features.shape[0]
    sr, tr = rows // n, teach // n
    wide, hs = head_w1.shape
    bot = head_w2.shape[1]
    everyone = nd * n
    factor = 10.0 / (9 * teach * nd)

    feat_other = swap(features, "dp", 1)
    parts, back, view = call(
        head_kernel,
        (shape((n, sr + tr, bot), BF16), shape((rows, rows), BF16), shape((rows, 1), F32)),
        [d],
        features, head_w1, head_w2, teacher_features, teacher_w1, teacher_w2,
        crop_image.reshape(1, -1), crop_view.reshape(1, -1),
        us=4,
    )
    parts_got = lax.all_to_all(parts, "proto", 0, 0)
    w1_late, w2_late, protos_late, tprotos_late, feat_late, _ = tied(
        head_w1, head_w2, protos, teacher_protos, features, parts
    )
    w2_half = lax.dynamic_slice_in_dim(w2_late, d * (hs // 2), hs // 2, 0)
    weights = jnp.concatenate(
        [lax.dynamic_slice_in_dim(w1_late, d * (wide // 2), wide // 2, 0), w2_half[:, :hs], w2_half[:, hs:]], axis=0
    )
    weights = lax.all_gather(weights, "proto")
    cols = protos.shape[1] // nd
    pnb = unit_cols(lax.dynamic_slice_in_dim(protos_late, d * cols, cols, 1))[0].astype(BF16)
    tpnb = unit_cols(lax.dynamic_slice_in_dim(tprotos_late, d * cols, cols, 1))[0].astype(BF16)
    view_other = swap(view, "dp", 1)

    got, zn, zinv = call(
        rows_kernel,
        (shape((n, sr + tr, bot), BF16), shape((sr + tr, bot), F32), shape((sr + tr, 1), F32)),
        [],
        parts_got,
    )
    feat_late, feat_other_late, w1_late, _ = tied(feat_late, feat_other, w1_late, got)
    got = lax.all_to_all(got, "proto", 0, 0)
    h0, h1, s0, s1 = call(
        hidden_kernel,
        (shape((hs, rows), BF16),) * 2 + (shape((hs, rows), F32),) * 2,
        [],
        feat_late, feat_other_late, w1_late,
        us=4,
    )
    got_other = swap(got, "dp", 1)
    kern, msg, student = call(
        kern_kernel,
        (shape((nd * teach, cols), F32), shape((everyone, nd * teach // 128, 128), F32), shape((nd * rows, bot), BF16)),
        [d],
        got, got_other, tpnb,
        us=3,
    )
    msg_got = lax.all_to_all(msg, ALL, 0, 0)
    student, _ = tied(student, msg)
    exb, sums, esum = student_sums(student, pnb)
    sums_other = swap(sums[rows:], "dp", 1)
    msg = call(
        second_kernel,
        shape((everyone, nd * (teach + rows) // 128, 128), F32),
        [d],
        msg_got, kern, esum,
    )
    msg_got = lax.all_to_all(msg, ALL, 0, 0)
    esum, last, mine, yours = call(
        third_kernel,
        (
            shape((nd * rows // 128, 128), F32),
            shape((nd * teach, cols), BF16),
            shape((teach, bot + 128), F32),
            shape((teach, bot + 128), F32),
        ),
        [d],
        msg_got, kern, pnb,
        us=2,
    )
    yours = swap(yours, "dp", 1)
    msg = call(message_kernel, shape((n, sr + 2 * tr, bot), BF16), [], sums[:rows], sums_other, mine, yours)
    msg_got = lax.all_to_all(msg, "proto", 0, 0)

    esum, view_late, view_other, student, exb, last, weights, _ = tied(
        esum, view, view_other, student, exb, last, weights, msg
    )
    esum = esum.reshape(nd, rows, 1)
    esum = jnp.concatenate([jnp.where(d == 0, esum[0], esum[1]), jnp.where(d == 0, esum[1], esum[0])], axis=0)
    count = jnp.where(jnp.concatenate([view_late, view_other], axis=0) == 2, 2.0, 1.0)
    crop_scale = count * factor / esum
    my_view = lax.dynamic_slice_in_dim(view_late, p * sr, sr, 0)
    my_scale = lax.dynamic_slice_in_dim(crop_scale, p * sr, sr, 0)
    dz = call(
        functools.partial(bottleneck_kernel, factor),
        shape((n, sr + tr, bot), BF16),
        [],
        msg_got, zn, zinv, my_view, my_scale,
    )
    got = lax.all_to_all(dz, "proto", 0, 0)
    left = (student.astype(F32) * crop_scale).astype(BF16)
    dpn = dot(left, exb, ((0,), (0,)))
    dpn_other, last_other = swap(dpn, "dp", 1), swap(last, "dp", 1)
    weights_other = swap(weights, "dp", 1)
    slope, w2_all, w1_block = slopes_of(d, p, features, weights, weights_other, wide // n)

    dz = call(unsort_kernel, shape((rows + teach, bot), BF16), [], got, back)
    dz_other = swap(dz, "dp", 1)
    grad_features = feature_grads(dz, slope, w2_all, w1_block)
    grad_w1, grad_w2 = call(
        weights_kernel,
        (shape(head_w1.shape, F32), shape(head_w2.shape, F32)),
        [],
        features, feat_other, dz, dz_other, h0, h1, s0, s1, head_w2,
    )
    grad_protos = protos_grads(d, protos, dpn, dpn_other, dz[rows:], dz_other[rows:], last, last_other)
    return (grad_features, grad_w1, grad_w2, grad_protos)


def body(features, teacher_features, *rest):
    n = lax.axis_size("proto")
    slot = (features.shape[0] // n, teacher_features.shape[0] // n)
    paired = lax.axis_size("dp") == 2 and n % 2 == 0 and slot[0] % 8 == 0 and slot[1] % 8 == 0
    return (paired_body if paired else general_body)(features, teacher_features, *rest)


def solution(mesh):
    in_specs = (
        P("dp", None),
        P("dp", None),
        P("dp"),
        P("dp"),
        P(None, "proto"),
        P("proto", None),
        P(None, "proto"),
        P(None, "proto"),
        P("proto", None),
        P(None, "proto"),
    )
    out_specs = (P("dp", "proto"), P(None, "proto"), P("proto", None), P(None, "proto"))
    return jax.shard_map(body, mesh=mesh, in_specs=in_specs, out_specs=out_specs, check_vma=False)
```

```python
import functools

import jax
import jax.numpy as jnp
from jax import lax
from jax.experimental import pallas as pl
from jax.experimental.pallas import tpu as pltpu
from jax.sharding import PartitionSpec as P

ITERS = 3
ALL = ("dp", "proto")
F32 = jnp.float32
BF16 = jnp.bfloat16


def gelu_parts(act):
    phi = 0.5 * (1.0 + lax.erf(act * 0.7071067811865476))
    slope = phi + act * jnp.exp(-0.5 * act * act) * 0.3989422804014327
    return (act * phi).astype(BF16), slope


def dot(a, b, dims):
    return lax.dot_general(a, b, (dims, ((), ())), preferred_element_type=F32)


def swap(value, axis, step):
    count = lax.axis_size(axis)
    return lax.ppermute(value, axis, [(i, i ^ step) for i in range(count)])


def over_dp(value):
    return [value] + [swap(value, "dp", s) for s in range(1, lax.axis_size("dp"))]


def tree_sum(parts):
    while len(parts) > 1:
        parts = [parts[i] + parts[i + 1] for i in range(0, len(parts), 2)]
    return parts[0]


def send_all(value, axes):
    count = lax.axis_size(axes)
    return lax.all_to_all(jnp.broadcast_to(value[None], (count,) + value.shape), axes, 0, 0)


def unit_cols(mat):
    matf = mat.astype(F32)
    inv = lax.rsqrt(jnp.sum(matf * matf, axis=0, keepdims=True) + 1e-06)
    return matf * inv, inv


def general_body(
    features,
    teacher_features,
    crop_image,
    crop_view,
    head_w1,
    head_w2,
    protos,
    teacher_w1,
    teacher_w2,
    teacher_protos,
):
    nd, n = lax.axis_size("dp"), lax.axis_size("proto")
    d, p = lax.axis_index("dp"), lax.axis_index("proto")
    rows, img = features.shape[0], teacher_features.shape[0] // 2
    per = rows // img
    sr, tr = rows // n, 2 * img // n
    bot = head_w2.shape[1]
    factor = 10.0 / (18 * img * nd)
    absolute = d ^ jnp.arange(nd)

    im = crop_image - d * img
    at = jnp.arange(rows, dtype=jnp.int32)
    rank = jnp.sum((im[:, None] == im[None, :]) & (at[None, :] < at[:, None]), axis=1)
    place = im * per + rank
    hit = at[:, None] == place[None, :]
    order = hit.astype(BF16)
    view = jnp.sum(jnp.where(hit, crop_view[None, :], 0), axis=1)
    views = jnp.stack(over_dp(view))[absolute]

    w1_block = lax.all_to_all(head_w1, "proto", split_axis=0, concat_axis=1, tiled=True)
    feats = over_dp(features)
    act = jnp.dot(features, head_w1, preferred_element_type=F32)
    hidden, slope = gelu_parts(act)
    zpart = jnp.dot(hidden, head_w2, preferred_element_type=F32).astype(BF16)
    zpart = jnp.dot(order, zpart, preferred_element_type=F32).astype(BF16)
    tact = jnp.dot(teacher_features, teacher_w1, preferred_element_type=F32)
    thidden, _ = gelu_parts(tact)
    tpart = jnp.dot(thidden, teacher_w2, preferred_element_type=F32).astype(BF16)
    parts = jnp.concatenate([zpart.reshape(n, sr, bot), tpart.reshape(n, tr, bot)], axis=1)
    parts = lax.all_to_all(parts, "proto", 0, 0)
    early = jnp.concatenate(
        [(slope - 0.5).astype(BF16)] + [head_w2[:, i : i + head_w1.shape[1]] for i in range(0, bot, head_w1.shape[1])],
        axis=0,
    )
    early = lax.all_gather(early, "proto")
    zrow = jnp.sum(parts.astype(F32), axis=0)
    zinv = lax.rsqrt(jnp.sum(zrow * zrow, axis=1, keepdims=True) + 1e-06)
    zn = zrow * zinv
    znb = send_all(zn.astype(BF16), "proto")
    znb = jnp.stack(over_dp(znb))[absolute]
    student = znb[:, :, :sr].reshape(nd * rows, bot)
    teacher = znb[:, :, sr:].reshape(nd * 2 * img, bot)

    cols = protos.shape[1] // nd
    pn, pinv = unit_cols(lax.dynamic_slice_in_dim(protos, d * cols, cols, 1))
    pnb = pn.astype(BF16)
    tpnb = unit_cols(lax.dynamic_slice_in_dim(teacher_protos, d * cols, cols, 1))[0].astype(BF16)

    kern = jnp.exp(jnp.dot(teacher, tpnb, preferred_element_type=F32) / 0.07)
    ex = jnp.exp(jnp.dot(student, pnb, preferred_element_type=F32) / 0.1)
    esum = jnp.sum(ex, axis=1)
    exb = ex.astype(BF16)
    sums = dot(exb, pnb, ((1,), (1,)))
    colscale = 1.0 / jnp.sum(kern, axis=0)
    for step in range(ITERS - 1):
        mass = jnp.sum(send_all(jnp.sum(kern * colscale[None, :], axis=1), ALL), axis=0)
        colscale = 1.0 / jnp.sum(kern / mass[:, None], axis=0)
    last = kern * colscale[None, :]
    lastb = last.astype(BF16)
    tsums = dot(lastb, pnb, ((1,), (1,)))
    tot = jnp.sum(send_all(jnp.concatenate([esum, jnp.sum(last, axis=1)]), ALL), axis=0)
    esum, mass = tot[: nd * rows], tot[nd * rows :]

    out = jnp.concatenate([sums.reshape(nd, n, sr, bot), tsums.reshape(nd, n, tr, bot)], axis=2)
    out = out[absolute]
    out = tree_sum([out[0]] + [swap(out[s], "dp", s) for s in range(1, nd)])
    out = jnp.sum(lax.all_to_all(out, "proto", 0, 0), axis=0)
    crop_scale = jnp.where(views == 2, 2.0, 1.0).reshape(-1) / esum * factor
    image_scale = factor / mass
    mine = (d * n + p)
    my_view = lax.dynamic_slice_in_dim(views.reshape(-1), mine * sr, sr)
    my_scale = lax.dynamic_slice_in_dim(crop_scale, mine * sr, sr)
    my_image = lax.dynamic_slice_in_dim(image_scale, mine * tr, tr)
    slot = jnp.arange(tr)
    pick = (slot[None, :] // 2 == jnp.arange(sr)[:, None] // per) & (slot[None, :] % 2 != my_view[:, None])
    target = jnp.sum(jnp.where(pick, my_image[None, :], 0.0)[:, :, None] * out[None, sr:], axis=1)
    dzn = my_scale[:, None] * out[:sr] - target
    zs, zi = zn[:sr], zinv[:sr]
    dz = (zi * (dzn - zs * jnp.sum(zs * dzn, axis=1, keepdims=True))).astype(BF16)
    dz = send_all(dz, "proto").reshape(rows, bot)
    dz = dot(order, dz, ((0,), (0,))).astype(BF16)
    dzs = over_dp(dz)

    tslot = jnp.arange(2 * img)
    picks = (tslot[None, None, :] // 2 == at[None, :, None] // per) & (tslot[None, None, :] % 2 != views[:, :, None])
    own = lax.dot_general(
        picks.astype(BF16), student.reshape(nd, rows, bot), (((1,), (1,)), ((0,), (0,))), preferred_element_type=F32
    ).reshape(nd * 2 * img, bot)
    left = (student.astype(F32) * crop_scale[:, None]).astype(BF16)
    right = (own * image_scale[:, None]).astype(BF16)
    dpn = dot(left, exb, ((0,), (0,))) - dot(right, lastb, ((0,), (0,)))
    gp = pinv * (dpn - pn * jnp.sum(pn * dpn, axis=0, keepdims=True))
    gps = over_dp(gp)
    grad_protos = jnp.zeros(protos.shape, F32)
    for s in range(nd):
        grad_protos = lax.dynamic_update_slice_in_dim(grad_protos, gps[s], (d ^ s) * cols, 1)

    w1_parts, w2_parts = [], []
    for s in range(nd):
        if s:
            hid, slp = gelu_parts(jnp.dot(feats[s], head_w1, preferred_element_type=F32))
        else:
            hid, slp = hidden, slope
        w2_parts.append(dot(hid, dzs[s], ((0,), (0,))))
        dhid = (dot(dzs[s], head_w2, ((1,), (1,))) * slp).astype(BF16)
        w1_parts.append(dot(feats[s], dhid, ((0,), (0,))))
    grad_w1, grad_w2 = tree_sum(w1_parts), tree_sum(w2_parts)
    slopes = 0.5 + early[:, :rows].astype(F32).transpose(1, 0, 2).reshape(rows, -1)
    w2_all = early[:, rows:].reshape(n, -1, head_w1.shape[1], head_w1.shape[1]).transpose(1, 3, 0, 2)
    w2_all = w2_all.reshape(bot, -1)
    dhid = (jnp.dot(dz, w2_all, preferred_element_type=F32) * slopes).astype(BF16)
    grad_features = dot(dhid, w1_block, ((1,), (1,))).astype(BF16)
    return (grad_features, grad_w1, grad_w2, grad_protos)


def params(mib=56):
    return pltpu.CompilerParams(vmem_limit_bytes=mib * 1024 * 1024)


def shape(dims, dtype):
    return jax.ShapeDtypeStruct(dims, dtype)


def kernel_name(kernel):
    return getattr(kernel, "func", kernel).__name__


def block(dims):
    return pl.BlockSpec(dims, lambda i: (0,) * len(dims))


def call(kernel, outs, scalars, *args, us=1, mib=56):
    smem = [jnp.asarray(s, jnp.int32).reshape(1) for s in scalars]
    return pl.pallas_call(
        kernel,
        grid=(1,),
        out_shape=outs,
        in_specs=[pl.BlockSpec(memory_space=pltpu.SMEM)] * len(smem) + [block(x.shape) for x in args],
        out_specs=jax.tree.map(lambda x: block(x.shape), outs),
        compiler_params=params(mib),
        name=kernel_name(kernel),
        cost_estimate=pl.CostEstimate(flops=us * 10**9, bytes_accessed=us * 10**6, transcendentals=0),
    )(*smem, *args)


def grids(dims):
    return lax.broadcasted_iota(jnp.int32, dims, 0), lax.broadcasted_iota(jnp.int32, dims, 1)


def to_row(col):
    down, along = grids((col.shape[0], col.shape[0]))
    return jnp.sum(jnp.where(down == along, col, jnp.zeros_like(col)), axis=0, keepdims=True)


def to_col(row):
    down, along = grids((row.shape[1], row.shape[1]))
    return jnp.sum(jnp.where(down == along, row, jnp.zeros_like(row)), axis=1, keepdims=True)


def head_kernel(d_ref, *refs):
    sources, im_ref, view_ref = refs[:6], refs[6], refs[7]
    parts_ref, back_ref, vs_ref = refs[8:11]
    held, sems = refs[11:17], refs[17]
    copies = [pltpu.make_async_copy(a, b, sems.at[k]) for k, (a, b) in enumerate(zip(sources, held))]
    for copy in copies:
        copy.start()
    f_ref, w1_ref, w2_ref, tf_ref, tw1_ref, tw2_ref = held
    rows, teach = f_ref.shape[0], tf_ref.shape[0]
    n = parts_ref.shape[0]
    img = teach // 2
    per = rows // img
    im = (im_ref[...].reshape(1, rows) - d_ref[0] * img).astype(F32)
    down, along = grids((rows, rows))
    imc = to_col(im)
    same = im == imc
    before = jnp.where(same & (along < down), 1.0, 0.0)
    after = jnp.where(same & (down < along), 1.0, 0.0)
    col = (imc * per + jnp.sum(before, axis=1, keepdims=True)).astype(jnp.int32)
    row = (im * per + jnp.sum(after, axis=0, keepdims=True)).astype(jnp.int32)
    back_ref[...] = jnp.where(col == along, 1.0, 0.0).astype(BF16)
    hit = row == down
    vs_ref[...] = jnp.sum(jnp.where(hit, view_ref[...].reshape(1, rows).astype(F32), 0.0), axis=1, keepdims=True)
    order = jnp.where(hit, 1.0, 0.0).astype(BF16)

    for copy in copies:
        copy.wait()

    def part(x, first, second):
        act = dot(x[...], first[...], ((1,), (0,)))
        hidden = (act * 0.5 * (1.0 + lax.erf(act * 0.7071067811865476))).astype(BF16)
        return dot(hidden, second[...], ((1,), (0,)))

    z = part(f_ref, w1_ref, w2_ref).astype(BF16)
    z = dot(order, z, ((1,), (0,))).reshape(n, rows // n, -1)
    t = part(tf_ref, tw1_ref, tw2_ref).reshape(n, teach // n, -1)
    parts_ref[...] = jnp.concatenate([z, t], axis=1).astype(BF16)


def rows_kernel(parts_ref, out_ref, zn_ref, zinv_ref):
    z = jnp.sum(parts_ref[...].astype(F32), axis=0)
    inv = lax.rsqrt(jnp.sum(z * z, axis=1, keepdims=True) + 1e-06)
    zn = z * inv
    zn_ref[...] = zn
    zinv_ref[...] = inv
    out_ref[...] = jnp.broadcast_to(zn[None], out_ref.shape).astype(BF16)


def row_mass(kern, mass):
    if mass is None:
        scale = 1.0 / jnp.sum(kern, axis=0, keepdims=True)
    else:
        scale = 1.0 / jnp.sum(kern * (1.0 / mass), axis=0, keepdims=True)
    return scale, jnp.sum(kern * scale, axis=1, keepdims=True)


def fold(col):
    row = to_row(col)
    return jnp.concatenate([row[:, k : k + 128] for k in range(0, row.shape[1], 128)], axis=0)


def unfold(block):
    return to_col(jnp.concatenate([block[k : k + 1] for k in range(block.shape[0])], axis=1))


def kern_kernel(d_ref, got_ref, other_ref, tpnb_ref, kern_ref, msg_ref, student_ref):
    n, slot, bot = got_ref.shape
    rows = student_ref.shape[0] // 2
    sr = rows // n
    own, other = got_ref[...].astype(F32), other_ref[...].astype(F32)
    student_ref[:rows] = own[:, :sr].reshape(rows, bot).astype(BF16)
    student_ref[rows:] = other[:, :sr].reshape(rows, bot).astype(BF16)
    own, other = own[:, sr:].reshape(-1, bot), other[:, sr:].reshape(-1, bot)
    first = d_ref[0] == 0
    teacher = jnp.concatenate([jnp.where(first, own, other), jnp.where(first, other, own)], axis=0).astype(BF16)
    kern = jnp.exp(dot(teacher, tpnb_ref[...], ((1,), (0,))) * (1.0 / 0.07))
    kern_ref[...] = kern
    _, mass = row_mass(kern, None)
    msg_ref[...] = jnp.broadcast_to(fold(mass)[None], msg_ref.shape)


def student_kernel(z_ref, pnb_ref, exb_ref, own_ref, other_ref, esum_ref):
    step = pl.program_id(0)
    ex = jnp.exp(dot(z_ref[...], pnb_ref[...], ((1,), (0,))) * 10.0)
    esum_ref[...] = jnp.sum(ex, axis=1, keepdims=True)
    exb = ex.astype(BF16)
    exb_ref[...] = exb
    sums = dot(exb, pnb_ref[...], ((1,), (1,)))

    @pl.when(step < pl.num_programs(0) // 2)
    def _():
        own_ref[...] = sums

    @pl.when(step >= pl.num_programs(0) // 2)
    def _():
        other_ref[...] = sums


def student_sums(student, pnb):
    total, bot = student.shape
    cols = pnb.shape[1]
    tile = total // 4
    return pl.pallas_call(
        student_kernel,
        name="student_kernel",
        grid=(4,),
        out_shape=(
            shape((total, cols), BF16),
            shape((total // 2, bot), F32),
            shape((total // 2, bot), F32),
            shape((total, 1), F32),
        ),
        in_specs=[pl.BlockSpec((tile, bot), lambda i: (i, 0)), pl.BlockSpec((bot, cols), lambda i: (0, 0))],
        out_specs=(
            pl.BlockSpec((tile, cols), lambda i: (i, 0)),
            pl.BlockSpec((tile, bot), lambda i: (jnp.minimum(i, 1), 0)),
            pl.BlockSpec((tile, bot), lambda i: (jnp.maximum(i - 2, 0), 0)),
            pl.BlockSpec((tile, 1), lambda i: (i, 0)),
        ),
        compiler_params=params(),
        cost_estimate=pl.CostEstimate(flops=5 * 10**9, bytes_accessed=10**7, transcendentals=0),
    )(student, pnb)


def second_kernel(d_ref, got_ref, kern_ref, esum_ref, msg_ref):
    mass = unfold(jnp.sum(got_ref[...], axis=0))
    _, mass = row_mass(kern_ref[...], mass)
    half = esum_ref.shape[0] // 2
    own, other = to_row(esum_ref[:half]), to_row(esum_ref[half:])
    first = d_ref[0] == 0
    mass = to_row(mass)
    mass = jnp.concatenate([mass, jnp.zeros((1, half - mass.shape[1]), F32)], axis=1)
    n = msg_ref.shape[0] // 2
    for k, row in enumerate((jnp.where(first, own, other), jnp.where(first, other, own))):
        part = jnp.concatenate([mass, row], axis=0)
        msg_ref[k * n : (k + 1) * n] = jnp.broadcast_to(part[None], (n,) + part.shape)


def third_kernel(d_ref, got_ref, kern_ref, pnb_ref, esum_ref, last_ref, mine_ref, yours_ref):
    teach = kern_ref.shape[0]
    got = jnp.sum(got_ref[...], axis=0)
    esum_ref[...] = to_col(got[1:])
    kern = kern_ref[...]
    scale, mass = row_mass(kern, to_col(got[:1, :teach]))
    last = (kern * scale).astype(BF16)
    last_ref[...] = last
    sums = dot(last, pnb_ref[...], ((1,), (1,)))
    sums = jnp.concatenate([sums, jnp.broadcast_to(mass, (teach, 128))], axis=1)
    half = teach // 2
    first = d_ref[0] == 0
    mine_ref[...] = jnp.where(first, sums[:half], sums[half:])
    yours_ref[...] = jnp.where(first, sums[half:], sums[:half])


def message_kernel(sums_ref, b0_ref, b1_ref, out_ref):
    n = out_ref.shape[0]
    rows, bot = sums_ref.shape
    sums = sums_ref[...].astype(F32).reshape(n, rows // n, bot)
    both = b0_ref[...] + b1_ref[...]
    mass = both[:, bot:]
    high = mass.astype(BF16).astype(F32)
    tail = jnp.concatenate([high, mass - high], axis=1)
    teach = both.shape[0]
    both = both[:, :bot].reshape(n, teach // n, bot)
    out_ref[...] = jnp.concatenate([sums, both, tail.reshape(n, teach // n, bot)], axis=1).astype(BF16)


def bottleneck_kernel(factor, got_ref, zn_ref, zinv_ref, view_ref, scale_ref, out_ref):
    sr = view_ref.shape[0]
    tr = zn_ref.shape[0] - sr
    per = sr // (tr // 2)
    out = jnp.sum(got_ref[...].astype(F32), axis=0)
    tail = out[sr + tr :]
    image = factor / (tail[:, :1] + tail[:, 128:129])
    sums = out[sr : sr + tr] * image
    zn, zinv = zn_ref[:sr], zinv_ref[:sr]
    znb = zn.astype(BF16).astype(F32)
    view = view_ref[...].astype(jnp.int32)
    which = lax.broadcasted_iota(jnp.int32, (sr, 1), 0)
    dzn = scale_ref[...] * out[:sr]
    own = []
    for t in range(tr):
        base = (t // 2) * per
        pick = (which >= base) & (which < base + per) & (view != t % 2)
        dzn = dzn - jnp.where(pick, sums[t : t + 1], 0.0)
        own.append(jnp.sum(jnp.where(pick, znb, 0.0), axis=0, keepdims=True) * image[t : t + 1])
    dz = zinv * (dzn - zn * jnp.sum(zn * dzn, axis=1, keepdims=True))
    both = jnp.concatenate([dz] + own, axis=0)
    out_ref[...] = jnp.broadcast_to(both[None], out_ref.shape).astype(BF16)


def hidden_kernel(f0_ref, f1_ref, w1_ref, h0_ref, h1_ref, s0_ref, s1_ref):
    for f, h, s in ((f0_ref, h0_ref, s0_ref), (f1_ref, h1_ref, s1_ref)):
        act = dot(f[...], w1_ref[...], ((1,), (0,))).T
        phi = 0.5 * (1.0 + lax.erf(act * 0.7071067811865476))
        h[...] = (act * phi).astype(BF16)
        s[...] = phi + act * jnp.exp(-0.5 * act * act) * 0.3989422804014327


def slopes_kernel(d_ref, p_ref, f_ref, own_ref, other_ref, slope_ref, w2_ref, w1_ref):
    hs = own_ref.shape[2]
    deep = f_ref.shape[1] // 2
    first = d_ref[0] == 0
    own, other = own_ref[...], other_ref[...]
    low = jnp.where(first, own, other)
    high = jnp.where(first, other, own)
    a, b = (jnp.concatenate([x[0], x[1]], axis=1) for x in (low[:, :deep], high[:, :deep]))
    act = dot(f_ref[:, :deep], a, ((1,), (0,))) + dot(f_ref[:, deep:], b, ((1,), (0,)))
    phi = 0.5 * (1.0 + lax.erf(act * 0.7071067811865476))
    slope_ref[...] = phi + act * jnp.exp(-0.5 * act * act) * 0.3989422804014327
    width = w1_ref.shape[0]
    blocks = deep // width
    at = pl.multiple_of(lax.rem(p_ref[0], blocks) * width, width)
    mine = (p_ref[0] // blocks) == d_ref[0]
    rows = jnp.where(mine, own_ref[:, pl.ds(at, width)], other_ref[:, pl.ds(at, width)])
    w1_ref[...] = jnp.concatenate([rows[0], rows[1]], axis=1)
    half = hs // 2
    for k in range(2):
        for part, x in ((0, low), (1, high)):
            tail = jnp.concatenate([x[k, deep : deep + half], x[k, deep + half :]], axis=1)
            w2_ref[k * hs + part * half : k * hs + (part + 1) * half] = tail


def slopes_of(d, p, features, own, other, width):
    n, tall, hs = own.shape
    rows = features.shape[0]
    whole = lambda k, d, p: (0, 0)
    return pl.pallas_call(
        slopes_kernel,
        name="slopes_kernel",
        grid_spec=pltpu.PrefetchScalarGridSpec(
            num_scalar_prefetch=2,
            grid=(n // 2,),
            in_specs=[
                pl.BlockSpec(features.shape, whole),
                pl.BlockSpec((2, tall, hs), lambda k, d, p: (k, 0, 0)),
                pl.BlockSpec((2, tall, hs), lambda k, d, p: (k, 0, 0)),
            ],
            out_specs=(
                pl.BlockSpec((rows, 2 * hs), lambda k, d, p: (0, k)),
                pl.BlockSpec((2 * hs, 2 * hs), lambda k, d, p: (k, 0)),
                pl.BlockSpec((width, 2 * hs), lambda k, d, p: (0, k)),
            ),
        ),
        out_shape=(shape((rows, n * hs), F32), shape((n * hs, 2 * hs), BF16), shape((width, n * hs), BF16)),
        compiler_params=params(20),
        cost_estimate=pl.CostEstimate(flops=10**10, bytes_accessed=3 * 10**7, transcendentals=0),
    )(d.reshape(1), p.reshape(1), features, own, other)


def unsort_kernel(got_ref, back_ref, out_ref):
    n, slot, bot = got_ref.shape
    rows = back_ref.shape[0]
    sr = rows // n
    got = got_ref[...].astype(F32)
    dz = got[:, :sr].reshape(rows, bot).astype(BF16)
    out_ref[:rows] = dot(back_ref[...], dz, ((1,), (0,))).astype(BF16)
    out_ref[rows:] = got[:, sr:].reshape(n * (slot - sr), bot).astype(BF16)


def features_kernel(dz_ref, slope_ref, w2_ref, w1_ref, out_ref, acc_ref):
    step = pl.program_id(0)

    @pl.when(step == 0)
    def _():
        acc_ref[...] = jnp.zeros_like(acc_ref)

    pre = dot(dz_ref[...], w2_ref[...], ((1,), (1,)))
    dhid = (pre * slope_ref[...]).astype(BF16)
    acc_ref[...] += dot(w1_ref[...], dhid, ((1,), (1,)))

    @pl.when(step == pl.num_programs(0) - 1)
    def _():
        out_ref[...] = acc_ref[...].astype(BF16)


def feature_grads(dz, slope, w2, w1_block):
    rows, hidden = slope.shape
    width, bot = w1_block.shape[0], w2.shape[1]
    step = 2 * bot
    return pl.pallas_call(
        features_kernel,
        name="features_kernel",
        grid=(hidden // step,),
        out_shape=shape((width, rows), BF16),
        in_specs=[
            pl.BlockSpec((rows, bot), lambda k: (0, 0)),
            pl.BlockSpec((rows, step), lambda k: (0, k)),
            pl.BlockSpec((step, bot), lambda k: (k, 0)),
            pl.BlockSpec((width, step), lambda k: (0, k)),
        ],
        out_specs=pl.BlockSpec((width, rows), lambda k: (0, 0)),
        scratch_shapes=[pltpu.VMEM((width, rows), F32)],
        compiler_params=params(12),
    )(dz, slope, w2, w1_block)


def weights_kernel(f0_ref, f1_ref, dz0_ref, dz1_ref, h0_ref, h1_ref, s0_ref, s1_ref, w2_ref, g1_ref, g2_ref):
    g1, g2 = [], []
    rows = f0_ref.shape[0]
    for f, z, h, s in ((f0_ref, dz0_ref, h0_ref, s0_ref), (f1_ref, dz1_ref, h1_ref, s1_ref)):
        dz = z[:rows]
        g2.append(dot(h[...], dz, ((1,), (0,))))
        dhid = (dot(w2_ref[...], dz, ((1,), (1,))) * s[...]).astype(BF16)
        g1.append(dot(dhid, f[...], ((1,), (0,))))
    g1_ref[...] = (g1[0] + g1[1]).T
    g2_ref[...] = g2[0] + g2[1]


def protos_kernel(d_ref, protos_ref, own_ref, other_ref, left_ref, right_ref, lown_ref, lother_ref, out_ref, turned_ref):
    half = pl.program_id(0) // (pl.num_programs(0) // 2)
    mine = half == d_ref[0]

    @pl.when(pl.program_id(0) == 0)
    def _():
        first = d_ref[0] == 0
        a, b = left_ref[...].astype(F32), right_ref[...].astype(F32)
        scaled = jnp.concatenate([jnp.where(first, a, b), jnp.where(first, b, a)], axis=0)
        turned_ref[...] = scaled.T.astype(BF16)

    def finish(dpn_ref, last_ref):
        mat = protos_ref[...].astype(F32)
        inv = lax.rsqrt(jnp.sum(mat * mat, axis=0, keepdims=True) + 1e-06)
        pn = mat * inv
        dpn = dpn_ref[...] - dot(turned_ref[...], last_ref[...], ((1,), (0,)))
        out_ref[...] = inv * (dpn - pn * jnp.sum(pn * dpn, axis=0, keepdims=True))

    @pl.when(mine)
    def _():
        finish(own_ref, lown_ref)

    @pl.when(jnp.logical_not(mine))
    def _():
        finish(other_ref, lother_ref)


def protos_grads(d, protos, own, other, mine, yours, lown, lother):
    bot, wide = protos.shape
    tile = 1024
    steps = wide // tile
    halfsteps = steps // 2
    teach = lown.shape[0]
    after = mine.shape[0] // (teach // 2) - 1

    def place(i, d_ref, same):
        at = d_ref[0] if same else 1 - d_ref[0]
        return (0, jnp.clip(i - at * halfsteps, 0, halfsteps - 1))

    own_map = lambda i, d_ref: place(i, d_ref, True)
    other_map = lambda i, d_ref: place(i, d_ref, False)
    return pl.pallas_call(
        protos_kernel,
        name="protos_kernel",
        grid_spec=pltpu.PrefetchScalarGridSpec(
            num_scalar_prefetch=1,
            grid=(steps,),
            in_specs=[
                pl.BlockSpec((bot, tile), lambda i, d_ref: (0, i)),
                pl.BlockSpec((bot, tile), own_map),
                pl.BlockSpec((bot, tile), other_map),
                pl.BlockSpec((teach // 2, bot), lambda i, d_ref: (after, 0)),
                pl.BlockSpec((teach // 2, bot), lambda i, d_ref: (after, 0)),
                pl.BlockSpec((teach, tile), own_map),
                pl.BlockSpec((teach, tile), other_map),
            ],
            out_specs=pl.BlockSpec((bot, tile), lambda i, d_ref: (0, i)),
            scratch_shapes=[pltpu.VMEM((bot, teach), BF16)],
        ),
        out_shape=jax.ShapeDtypeStruct((bot, wide), F32),
        compiler_params=params(16),
    )(d.reshape(1), protos, own, other, mine, yours, lown, lother)


def tied(*values):
    return lax.optimization_barrier(values)


def paired_body(
    features,
    teacher_features,
    crop_image,
    crop_view,
    head_w1,
    head_w2,
    protos,
    teacher_w1,
    teacher_w2,
    teacher_protos,
):
    nd, n = lax.axis_size("dp"), lax.axis_size("proto")
    d, p = lax.axis_index("dp"), lax.axis_index("proto")
    rows, teach = features.shape[0], teacher_features.shape[0]
    sr, tr = rows // n, teach // n
    wide, hs = head_w1.shape
    bot = head_w2.shape[1]
    everyone = nd * n
    factor = 10.0 / (9 * teach * nd)

    w2_half = lax.dynamic_slice_in_dim(head_w2, d * (hs // 2), hs // 2, 0)
    weights = jnp.concatenate(
        [lax.dynamic_slice_in_dim(head_w1, d * (wide // 2), wide // 2, 0), w2_half[:, :hs], w2_half[:, hs:]], axis=0
    )
    weights, head_w1_late = tied(weights, head_w1)
    weights = lax.all_gather(weights, "proto")
    feat_other = swap(features, "dp", 1)
    heads = (features, head_w1_late, head_w2, teacher_features, teacher_w1, teacher_w2)
    parts, back, view = pl.pallas_call(
        head_kernel,
        grid=(1,),
        out_shape=(shape((n, sr + tr, bot), BF16), shape((rows, rows), BF16), shape((rows, 1), F32)),
        in_specs=[pl.BlockSpec(memory_space=pltpu.SMEM)]
        + [pl.BlockSpec(memory_space=pl.ANY)] * 6
        + [block((rows,))] * 2,
        out_specs=(block((n, sr + tr, bot)), block((rows, rows)), block((rows, 1))),
        scratch_shapes=[pltpu.VMEM(x.shape, x.dtype) for x in heads] + [pltpu.SemaphoreType.DMA((6,))],
        compiler_params=params(),
        name="head_kernel",
    )(d.reshape(1), *heads, crop_image, crop_view)
    parts_got = lax.all_to_all(parts, "proto", 0, 0)
    w1_late, protos_late, tprotos_late, feat_late, feat_other_late, _ = tied(
        head_w1, protos, teacher_protos, features, feat_other, parts
    )
    h0, h1, s0, s1 = call(
        hidden_kernel,
        (shape((hs, rows), BF16),) * 2 + (shape((hs, rows), F32),) * 2,
        [],
        feat_late, feat_other_late, w1_late,
        us=4,
    )
    cols = protos.shape[1] // nd
    pnb = unit_cols(lax.dynamic_slice_in_dim(protos_late, d * cols, cols, 1))[0].astype(BF16)
    tpnb = unit_cols(lax.dynamic_slice_in_dim(tprotos_late, d * cols, cols, 1))[0].astype(BF16)
    parts_got, h0, h1, s0, s1, pnb, tpnb = tied(parts_got, h0, h1, s0, s1, pnb, tpnb)

    got, zn, zinv = call(
        rows_kernel,
        (shape((n, sr + tr, bot), BF16), shape((sr + tr, bot), F32), shape((sr + tr, 1), F32)),
        [],
        parts_got,
    )
    got = lax.all_to_all(got, "proto", 0, 0)
    got_other = swap(got, "dp", 1)
    kern, msg, student = call(
        kern_kernel,
        (shape((nd * teach, cols), F32), shape((everyone, nd * teach // 128, 128), F32), shape((nd * rows, bot), BF16)),
        [d],
        got, got_other, tpnb,
        us=3,
    )
    msg_got = lax.all_to_all(msg, ALL, 0, 0)
    student, _ = tied(student, msg)
    exb, sums, sums_other, esum = student_sums(student, pnb)
    msg = call(
        second_kernel,
        shape((everyone, 2, rows), F32),
        [d],
        msg_got, kern, esum,
    )
    msg_got = lax.all_to_all(msg, ALL, 0, 0)
    sums, sums_other, _ = tied(sums, sums_other, msg)
    sums_other = swap(sums_other, "dp", 1)
    sums = (sums + sums_other).astype(BF16)
    msg_got, sums = tied(msg_got, sums)
    esum, last, mine, yours = call(
        third_kernel,
        (
            shape((rows, 1), F32),
            shape((nd * teach, cols), BF16),
            shape((teach, bot + 128), F32),
            shape((teach, bot + 128), F32),
        ),
        [d],
        msg_got, kern, pnb,
        us=2,
    )
    yours = swap(yours, "dp", 1)
    msg = call(message_kernel, shape((n, sr + 2 * tr, bot), BF16), [], sums, mine, yours)
    msg_got = lax.all_to_all(msg, "proto", 0, 0)

    esum, view_late, weights, last, _ = tied(esum, view, weights, last, msg)
    weights_other, last_other = swap(weights, "dp", 1), swap(last, "dp", 1)
    crop_scale = jnp.where(view_late == 2, 2.0, 1.0) * factor / esum
    scale_other = swap(crop_scale, "dp", 1)
    my_view = lax.dynamic_slice_in_dim(view_late, p * sr, sr, 0)
    my_scale = lax.dynamic_slice_in_dim(crop_scale, p * sr, sr, 0)
    left = (student.astype(F32) * jnp.concatenate([crop_scale, scale_other], axis=0)).astype(BF16)
    dpn = dot(left, exb, ((0,), (0,)))
    msg_got, dpn = tied(msg_got, dpn)
    dpn_other = swap(dpn, "dp", 1)
    dz = call(
        functools.partial(bottleneck_kernel, factor),
        shape((n, sr + tr, bot), BF16),
        [],
        msg_got, zn, zinv, my_view, my_scale,
    )
    got = lax.all_to_all(dz, "proto", 0, 0)
    weights, feat_late, _ = tied(weights, features, dz)
    slope, w2_all, w1_block = slopes_of(d, p, feat_late, weights, weights_other, wide // n)
    got, slope, w2_all, w1_block = tied(got, slope, w2_all, w1_block)

    dz = call(unsort_kernel, shape((rows + teach, bot), BF16), [], got, back, mib=8)
    dz_other = swap(dz, "dp", 1)
    grad_features = feature_grads(dz, slope, w2_all, w1_block).T
    grad_w1, grad_w2 = call(
        weights_kernel,
        (shape(head_w1.shape, F32), shape(head_w2.shape, F32)),
        [],
        features, feat_other, dz, dz_other, h0, h1, s0, s1, head_w2,
        mib=16,
    )
    grad_protos = protos_grads(d, protos, dpn, dpn_other, dz, dz_other, last, last_other)
    return (grad_features, grad_w1, grad_w2, grad_protos)


def body(features, teacher_features, *rest):
    n = lax.axis_size("proto")
    slot = (features.shape[0] // n, teacher_features.shape[0] // n)
    paired = lax.axis_size("dp") == 2 and n % 2 == 0 and slot[0] % 8 == 0 and slot[1] % 8 == 0
    paired = paired and features.shape[0] % teacher_features.shape[0] == 0
    return (paired_body if paired else general_body)(features, teacher_features, *rest)


def solution(mesh):
    in_specs = (
        P("dp", None),
        P("dp", None),
        P("dp"),
        P("dp"),
        P(None, "proto"),
        P("proto", None),
        P(None, "proto"),
        P(None, "proto"),
        P("proto", None),
        P(None, "proto"),
    )
    out_specs = (P("dp", "proto"), P(None, "proto"), P("proto", None), P(None, "proto"))
    return jax.shard_map(body, mesh=mesh, in_specs=in_specs, out_specs=out_specs, check_vma=False)
```

```python
import functools

import jax
import jax.numpy as jnp
from jax import lax
from jax.experimental import pallas as pl
from jax.experimental.pallas import tpu as pltpu
from jax.sharding import PartitionSpec as P

ITERS = 3
ALL = ("dp", "proto")
F32 = jnp.float32
BF16 = jnp.bfloat16


def gelu_parts(act):
    phi = 0.5 * (1.0 + lax.erf(act * 0.7071067811865476))
    slope = phi + act * jnp.exp(-0.5 * act * act) * 0.3989422804014327
    return (act * phi).astype(BF16), slope


def dot(a, b, dims):
    return lax.dot_general(a, b, (dims, ((), ())), preferred_element_type=F32)


def swap(value, axis, step):
    count = lax.axis_size(axis)
    return lax.ppermute(value, axis, [(i, i ^ step) for i in range(count)])


def over_dp(value):
    return [value] + [swap(value, "dp", s) for s in range(1, lax.axis_size("dp"))]


def tree_sum(parts):
    while len(parts) > 1:
        parts = [parts[i] + parts[i + 1] for i in range(0, len(parts), 2)]
    return parts[0]


def send_all(value, axes):
    count = lax.axis_size(axes)
    return lax.all_to_all(jnp.broadcast_to(value[None], (count,) + value.shape), axes, 0, 0)


def unit_cols(mat):
    matf = mat.astype(F32)
    inv = lax.rsqrt(jnp.sum(matf * matf, axis=0, keepdims=True) + 1e-06)
    return matf * inv, inv


def general_body(
    features,
    teacher_features,
    crop_image,
    crop_view,
    head_w1,
    head_w2,
    protos,
    teacher_w1,
    teacher_w2,
    teacher_protos,
):
    nd, n = lax.axis_size("dp"), lax.axis_size("proto")
    d, p = lax.axis_index("dp"), lax.axis_index("proto")
    rows, img = features.shape[0], teacher_features.shape[0] // 2
    per = rows // img
    sr, tr = rows // n, 2 * img // n
    bot = head_w2.shape[1]
    factor = 10.0 / (18 * img * nd)
    absolute = d ^ jnp.arange(nd)

    im = crop_image - d * img
    at = jnp.arange(rows, dtype=jnp.int32)
    rank = jnp.sum((im[:, None] == im[None, :]) & (at[None, :] < at[:, None]), axis=1)
    place = im * per + rank
    hit = at[:, None] == place[None, :]
    order = hit.astype(BF16)
    view = jnp.sum(jnp.where(hit, crop_view[None, :], 0), axis=1)
    views = jnp.stack(over_dp(view))[absolute]

    w1_block = lax.all_to_all(head_w1, "proto", split_axis=0, concat_axis=1, tiled=True)
    feats = over_dp(features)
    act = jnp.dot(features, head_w1, preferred_element_type=F32)
    hidden, slope = gelu_parts(act)
    zpart = jnp.dot(hidden, head_w2, preferred_element_type=F32).astype(BF16)
    zpart = jnp.dot(order, zpart, preferred_element_type=F32).astype(BF16)
    tact = jnp.dot(teacher_features, teacher_w1, preferred_element_type=F32)
    thidden, _ = gelu_parts(tact)
    tpart = jnp.dot(thidden, teacher_w2, preferred_element_type=F32).astype(BF16)
    parts = jnp.concatenate([zpart.reshape(n, sr, bot), tpart.reshape(n, tr, bot)], axis=1)
    parts = lax.all_to_all(parts, "proto", 0, 0)
    early = jnp.concatenate(
        [(slope - 0.5).astype(BF16)] + [head_w2[:, i : i + head_w1.shape[1]] for i in range(0, bot, head_w1.shape[1])],
        axis=0,
    )
    early = lax.all_gather(early, "proto")
    zrow = jnp.sum(parts.astype(F32), axis=0)
    zinv = lax.rsqrt(jnp.sum(zrow * zrow, axis=1, keepdims=True) + 1e-06)
    zn = zrow * zinv
    znb = send_all(zn.astype(BF16), "proto")
    znb = jnp.stack(over_dp(znb))[absolute]
    student = znb[:, :, :sr].reshape(nd * rows, bot)
    teacher = znb[:, :, sr:].reshape(nd * 2 * img, bot)

    cols = protos.shape[1] // nd
    pn, pinv = unit_cols(lax.dynamic_slice_in_dim(protos, d * cols, cols, 1))
    pnb = pn.astype(BF16)
    tpnb = unit_cols(lax.dynamic_slice_in_dim(teacher_protos, d * cols, cols, 1))[0].astype(BF16)

    kern = jnp.exp(jnp.dot(teacher, tpnb, preferred_element_type=F32) / 0.07)
    ex = jnp.exp(jnp.dot(student, pnb, preferred_element_type=F32) / 0.1)
    esum = jnp.sum(ex, axis=1)
    exb = ex.astype(BF16)
    sums = dot(exb, pnb, ((1,), (1,)))
    colscale = 1.0 / jnp.sum(kern, axis=0)
    for step in range(ITERS - 1):
        mass = jnp.sum(send_all(jnp.sum(kern * colscale[None, :], axis=1), ALL), axis=0)
        colscale = 1.0 / jnp.sum(kern / mass[:, None], axis=0)
    last = kern * colscale[None, :]
    lastb = last.astype(BF16)
    tsums = dot(lastb, pnb, ((1,), (1,)))
    tot = jnp.sum(send_all(jnp.concatenate([esum, jnp.sum(last, axis=1)]), ALL), axis=0)
    esum, mass = tot[: nd * rows], tot[nd * rows :]

    out = jnp.concatenate([sums.reshape(nd, n, sr, bot), tsums.reshape(nd, n, tr, bot)], axis=2)
    out = out[absolute]
    out = tree_sum([out[0]] + [swap(out[s], "dp", s) for s in range(1, nd)])
    out = jnp.sum(lax.all_to_all(out, "proto", 0, 0), axis=0)
    crop_scale = jnp.where(views == 2, 2.0, 1.0).reshape(-1) / esum * factor
    image_scale = factor / mass
    mine = (d * n + p)
    my_view = lax.dynamic_slice_in_dim(views.reshape(-1), mine * sr, sr)
    my_scale = lax.dynamic_slice_in_dim(crop_scale, mine * sr, sr)
    my_image = lax.dynamic_slice_in_dim(image_scale, mine * tr, tr)
    slot = jnp.arange(tr)
    pick = (slot[None, :] // 2 == jnp.arange(sr)[:, None] // per) & (slot[None, :] % 2 != my_view[:, None])
    target = jnp.sum(jnp.where(pick, my_image[None, :], 0.0)[:, :, None] * out[None, sr:], axis=1)
    dzn = my_scale[:, None] * out[:sr] - target
    zs, zi = zn[:sr], zinv[:sr]
    dz = (zi * (dzn - zs * jnp.sum(zs * dzn, axis=1, keepdims=True))).astype(BF16)
    dz = send_all(dz, "proto").reshape(rows, bot)
    dz = dot(order, dz, ((0,), (0,))).astype(BF16)
    dzs = over_dp(dz)

    tslot = jnp.arange(2 * img)
    picks = (tslot[None, None, :] // 2 == at[None, :, None] // per) & (tslot[None, None, :] % 2 != views[:, :, None])
    own = lax.dot_general(
        picks.astype(BF16), student.reshape(nd, rows, bot), (((1,), (1,)), ((0,), (0,))), preferred_element_type=F32
    ).reshape(nd * 2 * img, bot)
    left = (student.astype(F32) * crop_scale[:, None]).astype(BF16)
    right = (own * image_scale[:, None]).astype(BF16)
    dpn = dot(left, exb, ((0,), (0,))) - dot(right, lastb, ((0,), (0,)))
    gp = pinv * (dpn - pn * jnp.sum(pn * dpn, axis=0, keepdims=True))
    gps = over_dp(gp)
    grad_protos = jnp.zeros(protos.shape, F32)
    for s in range(nd):
        grad_protos = lax.dynamic_update_slice_in_dim(grad_protos, gps[s], (d ^ s) * cols, 1)

    w1_parts, w2_parts = [], []
    for s in range(nd):
        if s:
            hid, slp = gelu_parts(jnp.dot(feats[s], head_w1, preferred_element_type=F32))
        else:
            hid, slp = hidden, slope
        w2_parts.append(dot(hid, dzs[s], ((0,), (0,))))
        dhid = (dot(dzs[s], head_w2, ((1,), (1,))) * slp).astype(BF16)
        w1_parts.append(dot(feats[s], dhid, ((0,), (0,))))
    grad_w1, grad_w2 = tree_sum(w1_parts), tree_sum(w2_parts)
    slopes = 0.5 + early[:, :rows].astype(F32).transpose(1, 0, 2).reshape(rows, -1)
    w2_all = early[:, rows:].reshape(n, -1, head_w1.shape[1], head_w1.shape[1]).transpose(1, 3, 0, 2)
    w2_all = w2_all.reshape(bot, -1)
    dhid = (jnp.dot(dz, w2_all, preferred_element_type=F32) * slopes).astype(BF16)
    grad_features = dot(dhid, w1_block, ((1,), (1,))).astype(BF16)
    return (grad_features, grad_w1, grad_w2, grad_protos)


def params(mib=56):
    return pltpu.CompilerParams(vmem_limit_bytes=mib * 1024 * 1024)


def shape(dims, dtype):
    return jax.ShapeDtypeStruct(dims, dtype)


def kernel_name(kernel):
    return getattr(kernel, "func", kernel).__name__


def block(dims):
    return pl.BlockSpec(dims, lambda i: (0,) * len(dims))


def call(kernel, outs, scalars, *args, us=1, mib=56):
    smem = [jnp.asarray(s, jnp.int32).reshape(1) for s in scalars]
    return pl.pallas_call(
        kernel,
        grid=(1,),
        out_shape=outs,
        in_specs=[pl.BlockSpec(memory_space=pltpu.SMEM)] * len(smem) + [block(x.shape) for x in args],
        out_specs=jax.tree.map(lambda x: block(x.shape), outs),
        compiler_params=params(mib),
        name=kernel_name(kernel),
        cost_estimate=pl.CostEstimate(flops=us * 10**9, bytes_accessed=us * 10**6, transcendentals=0),
    )(*smem, *args)


def grids(dims):
    return lax.broadcasted_iota(jnp.int32, dims, 0), lax.broadcasted_iota(jnp.int32, dims, 1)


def to_row(col):
    down, along = grids((col.shape[0], col.shape[0]))
    return jnp.sum(jnp.where(down == along, col, jnp.zeros_like(col)), axis=0, keepdims=True)


def to_col(row):
    down, along = grids((row.shape[1], row.shape[1]))
    return jnp.sum(jnp.where(down == along, row, jnp.zeros_like(row)), axis=1, keepdims=True)


def head_kernel(d_ref, *refs):
    sources, im_ref, view_ref = refs[:6], refs[6], refs[7]
    parts_ref, place_ref, vs_ref, pack_ref = refs[8:12]
    held, sems = refs[12:18], refs[18]
    copies = [pltpu.make_async_copy(a, b, sems.at[k]) for k, (a, b) in enumerate(zip(sources, held))]
    for copy in copies:
        copy.start()
    f_ref, w1_ref, w2_ref, tf_ref, tw1_ref, tw2_ref = held
    rows, teach = f_ref.shape[0], tf_ref.shape[0]
    n = parts_ref.shape[0]
    img = teach // 2
    per = rows // img
    im = (im_ref[...].reshape(1, rows) - d_ref[0] * img).astype(F32)
    down, along = grids((rows, rows))
    imc = to_col(im)
    same = im == imc
    after = jnp.where(same & (down < along), 1.0, 0.0)
    row = im * per + jnp.sum(after, axis=0, keepdims=True)
    place_ref[...] = row
    hit = row.astype(jnp.int32) == down
    vs_ref[...] = jnp.sum(jnp.where(hit, view_ref[...].reshape(1, rows).astype(F32), 0.0), axis=1, keepdims=True)
    order = jnp.where(hit, 1.0, 0.0).astype(BF16)

    for copy in copies:
        copy.wait()

    deep, hs = w1_ref.shape[0] // 2, w1_ref.shape[1]
    half = hs // 2
    pack_ref[:deep] = w1_ref[pl.ds(pl.multiple_of(d_ref[0] * deep, deep), deep)]
    w2_half = w2_ref[pl.ds(pl.multiple_of(d_ref[0] * half, half), half)]
    pack_ref[deep : deep + half] = w2_half[:, :hs]
    pack_ref[deep + half :] = w2_half[:, hs:]

    def part(x, first, second):
        act = dot(x[...], first[...], ((1,), (0,)))
        hidden = (act * 0.5 * (1.0 + lax.erf(act * 0.7071067811865476))).astype(BF16)
        return dot(hidden, second[...], ((1,), (0,)))

    z = part(f_ref, w1_ref, w2_ref).astype(BF16)
    z = dot(order, z, ((1,), (0,))).reshape(n, rows // n, -1)
    t = part(tf_ref, tw1_ref, tw2_ref).reshape(n, teach // n, -1)
    parts_ref[...] = jnp.concatenate([z, t], axis=1).astype(BF16)


def rows_kernel(parts_ref, out_ref, zn_ref, zinv_ref):
    z = jnp.sum(parts_ref[...].astype(F32), axis=0)
    inv = lax.rsqrt(jnp.sum(z * z, axis=1, keepdims=True) + 1e-06)
    zn = z * inv
    zn_ref[...] = zn
    zinv_ref[...] = inv
    out_ref[...] = jnp.broadcast_to(zn[None], out_ref.shape).astype(BF16)


def row_mass(kern, mass):
    if mass is None:
        scale = 1.0 / jnp.sum(kern, axis=0, keepdims=True)
    else:
        scale = 1.0 / jnp.sum(kern * (1.0 / mass), axis=0, keepdims=True)
    return scale, jnp.sum(kern * scale, axis=1, keepdims=True)


def fold(col):
    row = to_row(col)
    return jnp.concatenate([row[:, k : k + 128] for k in range(0, row.shape[1], 128)], axis=0)


def unfold(block):
    return to_col(jnp.concatenate([block[k : k + 1] for k in range(block.shape[0])], axis=1))


def kern_kernel(d_ref, got_ref, other_ref, tpnb_ref, kern_ref, msg_ref, student_ref):
    n, slot, bot = got_ref.shape
    rows = student_ref.shape[0] // 2
    sr = rows // n
    own, other = got_ref[...].astype(F32), other_ref[...].astype(F32)
    student_ref[:rows] = own[:, :sr].reshape(rows, bot).astype(BF16)
    student_ref[rows:] = other[:, :sr].reshape(rows, bot).astype(BF16)
    own, other = own[:, sr:].reshape(-1, bot), other[:, sr:].reshape(-1, bot)
    first = d_ref[0] == 0
    teacher = jnp.concatenate([jnp.where(first, own, other), jnp.where(first, other, own)], axis=0).astype(BF16)
    kern = jnp.exp(dot(teacher, tpnb_ref[...], ((1,), (0,))) * (1.0 / 0.07))
    kern_ref[...] = kern
    _, mass = row_mass(kern, None)
    msg_ref[...] = jnp.broadcast_to(fold(mass)[None], msg_ref.shape)


def student_kernel(z_ref, pnb_ref, exb_ref, own_ref, other_ref, esum_ref):
    step = pl.program_id(0)
    ex = jnp.exp(dot(z_ref[...], pnb_ref[...], ((1,), (0,))) * 10.0)
    esum_ref[...] = jnp.sum(ex, axis=1, keepdims=True)
    exb = ex.astype(BF16)
    exb_ref[...] = exb
    sums = dot(exb, pnb_ref[...], ((1,), (1,)))

    @pl.when(step < pl.num_programs(0) // 2)
    def _():
        own_ref[...] = sums

    @pl.when(step >= pl.num_programs(0) // 2)
    def _():
        other_ref[...] = sums


def student_sums(student, pnb):
    total, bot = student.shape
    cols = pnb.shape[1]
    tile = total // 4
    return pl.pallas_call(
        student_kernel,
        name="student_kernel",
        grid=(4,),
        out_shape=(
            shape((total, cols), BF16),
            shape((total // 2, bot), F32),
            shape((total // 2, bot), F32),
            shape((total, 1), F32),
        ),
        in_specs=[pl.BlockSpec((tile, bot), lambda i: (i, 0)), pl.BlockSpec((bot, cols), lambda i: (0, 0))],
        out_specs=(
            pl.BlockSpec((tile, cols), lambda i: (i, 0)),
            pl.BlockSpec((tile, bot), lambda i: (jnp.minimum(i, 1), 0)),
            pl.BlockSpec((tile, bot), lambda i: (jnp.maximum(i - 2, 0), 0)),
            pl.BlockSpec((tile, 1), lambda i: (i, 0)),
        ),
        compiler_params=params(),
        cost_estimate=pl.CostEstimate(flops=5 * 10**9, bytes_accessed=10**7, transcendentals=0),
    )(student, pnb)


def second_kernel(d_ref, got_ref, kern_ref, esum_ref, msg_ref):
    mass = unfold(jnp.sum(got_ref[...], axis=0))
    _, mass = row_mass(kern_ref[...], mass)
    half = esum_ref.shape[0] // 2
    own, other = to_row(esum_ref[:half]), to_row(esum_ref[half:])
    first = d_ref[0] == 0
    mass = to_row(mass)
    n = msg_ref.shape[0] // 2
    for k, row in enumerate((jnp.where(first, own, other), jnp.where(first, other, own))):
        part = jnp.concatenate([mass, row], axis=1)
        msg_ref[k * n : (k + 1) * n] = jnp.broadcast_to(part[None], (n,) + part.shape)


def third_kernel(d_ref, got_ref, kern_ref, pnb_ref, esum_ref, last_ref, mine_ref, yours_ref):
    teach = kern_ref.shape[0]
    got = jnp.sum(got_ref[...], axis=0)
    esum_ref[...] = to_col(got[:, teach:])
    kern = kern_ref[...]
    scale, mass = row_mass(kern, to_col(got[:, :teach]))
    last = (kern * scale).astype(BF16)
    last_ref[...] = last
    sums = dot(last, pnb_ref[...], ((1,), (1,)))
    sums = jnp.concatenate([sums, jnp.broadcast_to(mass, (teach, 128))], axis=1)
    half = teach // 2
    first = d_ref[0] == 0
    mine_ref[...] = jnp.where(first, sums[:half], sums[half:])
    yours_ref[...] = jnp.where(first, sums[half:], sums[:half])


def message_kernel(sums_ref, b0_ref, b1_ref, out_ref):
    n = out_ref.shape[0]
    rows, bot = sums_ref.shape
    sums = sums_ref[...].astype(F32).reshape(n, rows // n, bot)
    both = b0_ref[...] + b1_ref[...]
    mass = both[:, bot:]
    high = mass.astype(BF16).astype(F32)
    tail = jnp.concatenate([high, mass - high], axis=1)
    teach = both.shape[0]
    both = both[:, :bot].reshape(n, teach // n, bot)
    out_ref[...] = jnp.concatenate([sums, both, tail.reshape(n, teach // n, bot)], axis=1).astype(BF16)


def bottleneck_kernel(factor, p_ref, got_ref, zn_ref, zinv_ref, view_ref, scale_ref, out_ref):
    sr = view_ref.shape[0] // out_ref.shape[0]
    mine = pl.ds(pl.multiple_of(p_ref[0] * sr, sr), sr)
    tr = zn_ref.shape[0] - sr
    per = sr // (tr // 2)
    out = jnp.sum(got_ref[...].astype(F32), axis=0)
    tail = out[sr + tr :]
    image = factor / (tail[:, :1] + tail[:, 128:129])
    sums = out[sr : sr + tr] * image
    zn, zinv = zn_ref[:sr], zinv_ref[:sr]
    znb = zn.astype(BF16).astype(F32)
    view = view_ref[mine].astype(jnp.int32)
    which = lax.broadcasted_iota(jnp.int32, (sr, 1), 0)
    dzn = scale_ref[mine] * out[:sr]
    own = []
    for t in range(tr):
        base = (t // 2) * per
        pick = (which >= base) & (which < base + per) & (view != t % 2)
        dzn = dzn - jnp.where(pick, sums[t : t + 1], 0.0)
        own.append(jnp.sum(jnp.where(pick, znb, 0.0), axis=0, keepdims=True) * image[t : t + 1])
    dz = zinv * (dzn - zn * jnp.sum(zn * dzn, axis=1, keepdims=True))
    both = jnp.concatenate([dz] + own, axis=0)
    out_ref[...] = jnp.broadcast_to(both[None], out_ref.shape).astype(BF16)


def hidden_kernel(f0_ref, f1_ref, w1_ref, h0_ref, h1_ref, s0_ref, s1_ref):
    for f, h, s in ((f0_ref, h0_ref, s0_ref), (f1_ref, h1_ref, s1_ref)):
        act = dot(f[...], w1_ref[...], ((1,), (0,))).T
        phi = 0.5 * (1.0 + lax.erf(act * 0.7071067811865476))
        h[...] = (act * phi).astype(BF16)
        s[...] = phi + act * jnp.exp(-0.5 * act * act) * 0.3989422804014327


def slopes_kernel(d_ref, p_ref, f_ref, own_ref, other_ref, slope_ref, w2_ref, w1_ref):
    hs = own_ref.shape[2]
    deep = f_ref.shape[1] // 2
    first = d_ref[0] == 0
    own, other = own_ref[...], other_ref[...]
    low = jnp.where(first, own, other)
    high = jnp.where(first, other, own)
    a, b = (jnp.concatenate([x[0], x[1]], axis=1) for x in (low[:, :deep], high[:, :deep]))
    act = dot(f_ref[:, :deep], a, ((1,), (0,))) + dot(f_ref[:, deep:], b, ((1,), (0,)))
    phi = 0.5 * (1.0 + lax.erf(act * 0.7071067811865476))
    slope_ref[...] = phi + act * jnp.exp(-0.5 * act * act) * 0.3989422804014327
    width = w1_ref.shape[0]
    blocks = deep // width
    at = pl.multiple_of(lax.rem(p_ref[0], blocks) * width, width)
    mine = (p_ref[0] // blocks) == d_ref[0]
    rows = jnp.where(mine, own_ref[:, pl.ds(at, width)], other_ref[:, pl.ds(at, width)])
    w1_ref[...] = jnp.concatenate([rows[0], rows[1]], axis=1)
    half = hs // 2
    for k in range(2):
        for part, x in ((0, low), (1, high)):
            tail = jnp.concatenate([x[k, deep : deep + half], x[k, deep + half :]], axis=1)
            w2_ref[k * hs + part * half : k * hs + (part + 1) * half] = tail


def slopes_of(d, p, features, own, other, width):
    n, tall, hs = own.shape
    rows = features.shape[0]
    whole = lambda k, d, p: (0, 0)
    return pl.pallas_call(
        slopes_kernel,
        name="slopes_kernel",
        grid_spec=pltpu.PrefetchScalarGridSpec(
            num_scalar_prefetch=2,
            grid=(n // 2,),
            in_specs=[
                pl.BlockSpec(features.shape, whole),
                pl.BlockSpec((2, tall, hs), lambda k, d, p: (k, 0, 0)),
                pl.BlockSpec((2, tall, hs), lambda k, d, p: (k, 0, 0)),
            ],
            out_specs=(
                pl.BlockSpec((rows, 2 * hs), lambda k, d, p: (0, k)),
                pl.BlockSpec((2 * hs, 2 * hs), lambda k, d, p: (k, 0)),
                pl.BlockSpec((width, 2 * hs), lambda k, d, p: (0, k)),
            ),
        ),
        out_shape=(shape((rows, n * hs), F32), shape((n * hs, 2 * hs), BF16), shape((width, n * hs), BF16)),
        compiler_params=params(),
        cost_estimate=pl.CostEstimate(flops=10**10, bytes_accessed=3 * 10**7, transcendentals=0),
    )(d.reshape(1), p.reshape(1), features, own, other)


def fetch(pairs, sems):
    copies = [pltpu.make_async_copy(x, y, sems.at[k]) for k, (x, y) in enumerate(pairs)]
    for copy in copies:
        copy.start()
    return copies


def put_back(got, place):
    n, _, bot = got.shape
    rows = place.shape[1]
    _, along = grids((rows, rows))
    back = jnp.where(to_col(place).astype(jnp.int32) == along, 1.0, 0.0).astype(BF16)
    dz = got.astype(F32)[:, : rows // n].reshape(rows, bot).astype(BF16)
    return dot(back, dz, ((1,), (0,))).astype(BF16)


def features_kernel(step, *refs):
    ins, (dz_ref, out_ref), held, sems = refs[:5], refs[5:7], refs[7:12], refs[12]
    got, place, slope, w2, w1 = held
    pieces = [pl.ds(k, step) for k in range(0, slope.shape[1], step)]
    small = fetch([(ins[k], held[k]) for k in (0, 1, 4)], sems.at[pl.ds(0, 3)])
    large = []
    for k, piece in enumerate(pieces):
        pairs = [(ins[2].at[:, piece], slope.at[:, piece]), (ins[3].at[piece], w2.at[piece])]
        large.append(fetch(pairs, sems.at[pl.ds(3 + 2 * k, 2)]))
    for copy in small:
        copy.wait()
    dz = put_back(got[...], place[...])
    dz_ref[...] = dz
    total = None
    for piece, copies in zip(pieces, large):
        for copy in copies:
            copy.wait()
        dhid = (dot(dz, w2[piece], ((1,), (1,))) * slope[:, piece]).astype(BF16)
        part = dot(w1[:, piece], dhid, ((1,), (1,)))
        total = part if total is None else total + part
    out_ref[...] = total.astype(BF16)


def feature_grads(got, place, slope, w2, w1):
    args = (got, place, slope, w2, w1)
    rows, hidden = slope.shape
    bot, step = got.shape[2], 512
    return pl.pallas_call(
        functools.partial(features_kernel, step),
        name="features_kernel",
        grid=(1,),
        out_shape=(shape((rows, bot), BF16), shape((w1.shape[0], rows), BF16)),
        in_specs=[pl.BlockSpec(memory_space=pl.ANY)] * len(args),
        out_specs=(block((rows, bot)), block((w1.shape[0], rows))),
        scratch_shapes=[pltpu.VMEM(x.shape, x.dtype) for x in args]
        + [pltpu.SemaphoreType.DMA((3 + 2 * (hidden // step),))],
        compiler_params=params(),
    )(*args)


def last_kernel(tile, d_ref, *refs):
    ins, (gp_hbm, g1_hbm, g2_hbm) = refs[:16], refs[16:19]
    held, (gp, g1, g2, sems, tile_sems, out_sems) = refs[19:35], refs[35:]
    dz0, got0, got1, place1, protos, down, dother, lown, lother, f0, f1, h0, h1, s0, s1, w2 = held
    cols = protos.shape[1] // 2
    steps = cols // tile
    rows = dz0.shape[0]
    n, slot, bot = got0.shape
    early = fetch([(ins[k], held[k]) for k in range(4)], sems)
    tiles = []
    for k in range(2 * steps):
        own = k < steps
        here = pl.multiple_of((d_ref[0] if own else 1 - d_ref[0]) * cols + (k % steps) * tile, tile)
        there = pl.ds((k % steps) * tile, tile)
        a, b = (5, 7) if own else (6, 8)
        pairs = [
            (ins[4].at[:, pl.ds(here, tile)], protos.at[:, pl.ds(here, tile)]),
            (ins[a].at[:, there], held[a].at[:, there]),
            (ins[b].at[:, there], held[b].at[:, there]),
        ]
        tiles.append((here, there, a, b, fetch(pairs, tile_sems.at[k])))
    late = fetch([(ins[k], held[k]) for k in range(9, 16)], sems.at[pl.ds(4, 7)])
    for copy in early:
        copy.wait()
    first = d_ref[0] == 0
    right0 = got0[...].astype(F32)[:, rows // n :].reshape(-1, bot)
    right1 = got1[...].astype(F32)[:, rows // n :].reshape(-1, bot)
    right = jnp.concatenate([jnp.where(first, right0, right1), jnp.where(first, right1, right0)], axis=0)
    right = right.T.astype(BF16)
    dz1 = put_back(got1[...], place1[...])
    outs = []
    for k, (here, there, a, b, copies) in enumerate(tiles):
        for copy in copies:
            copy.wait()
        mat = protos[:, pl.ds(here, tile)].astype(F32)
        inv = lax.rsqrt(jnp.sum(mat * mat, axis=0, keepdims=True) + 1e-06)
        pn = mat * inv
        dpn = held[a][:, there].astype(F32) - dot(right, held[b][:, there], ((1,), (0,)))
        gp[:, pl.ds(here, tile)] = inv * (dpn - pn * jnp.sum(pn * dpn, axis=0, keepdims=True))
        out = pltpu.make_async_copy(gp.at[:, pl.ds(here, tile)], gp_hbm.at[:, pl.ds(here, tile)], out_sems.at[k])
        out.start()
        outs.append(out)
    for copy in late:
        copy.wait()
    sums1, sums2 = [], []
    for f, dz, h, sl in ((f0, dz0[...], h0, s0), (f1, dz1, h1, s1)):
        sums2.append(dot(h[...], dz, ((1,), (0,))))
        dhid = (dot(w2[...], dz, ((1,), (1,))) * sl[...]).astype(BF16)
        sums1.append(dot(dhid, f[...], ((1,), (0,))))
    g1[...] = (sums1[0] + sums1[1]).T
    g2[...] = sums2[0] + sums2[1]
    for k, (x, y) in enumerate(((g1, g1_hbm), (g2, g2_hbm))):
        out = pltpu.make_async_copy(x, y, out_sems.at[2 * steps + k])
        out.start()
        outs.append(out)
    for out in outs:
        out.wait()


def last_grads(d, head_w1, *args):
    tile = 512
    protos, head_w2 = args[4], args[15]
    tiles = protos.shape[1] // tile
    outs = (shape(protos.shape, F32), shape(head_w1.shape, F32), shape(head_w2.shape, F32))
    anywhere = pl.BlockSpec(memory_space=pl.ANY)
    return pl.pallas_call(
        functools.partial(last_kernel, tile),
        name="last_kernel",
        out_shape=outs,
        in_specs=[pl.BlockSpec(memory_space=pltpu.SMEM)] + [anywhere] * len(args),
        out_specs=(anywhere,) * 3,
        scratch_shapes=[pltpu.VMEM(x.shape, x.dtype) for x in args + outs]
        + [
            pltpu.SemaphoreType.DMA((11,)),
            pltpu.SemaphoreType.DMA((tiles, 3)),
            pltpu.SemaphoreType.DMA((tiles + 2,)),
        ],
        compiler_params=params(),
    )(d.reshape(1), *args)


def tied(*values):
    return lax.optimization_barrier(values)


def paired_body(
    features,
    teacher_features,
    crop_image,
    crop_view,
    head_w1,
    head_w2,
    protos,
    teacher_w1,
    teacher_w2,
    teacher_protos,
):
    nd, n = lax.axis_size("dp"), lax.axis_size("proto")
    d, p = lax.axis_index("dp"), lax.axis_index("proto")
    rows, teach = features.shape[0], teacher_features.shape[0]
    sr, tr = rows // n, teach // n
    wide, hs = head_w1.shape
    bot = head_w2.shape[1]
    everyone = nd * n
    factor = 10.0 / (9 * teach * nd)

    feat_other = swap(features, "dp", 1)
    heads = (features, head_w1, head_w2, teacher_features, teacher_w1, teacher_w2)
    parts, place, view, weights = pl.pallas_call(
        head_kernel,
        grid=(1,),
        out_shape=(
            shape((n, sr + tr, bot), BF16),
            shape((1, rows), F32),
            shape((rows, 1), F32),
            shape((wide // 2 + hs, hs), BF16),
        ),
        in_specs=[pl.BlockSpec(memory_space=pltpu.SMEM)]
        + [pl.BlockSpec(memory_space=pl.ANY)] * 6
        + [block((rows,))] * 2,
        out_specs=(block((n, sr + tr, bot)), block((1, rows)), block((rows, 1)), block((wide // 2 + hs, hs))),
        scratch_shapes=[pltpu.VMEM(x.shape, x.dtype) for x in heads] + [pltpu.SemaphoreType.DMA((6,))],
        compiler_params=params(),
        name="head_kernel",
    )(d.reshape(1), *heads, crop_image, crop_view)
    weights = lax.all_gather(weights, "proto")
    parts_got = lax.all_to_all(parts, "proto", 0, 0)
    w1_late, protos_late, tprotos_late, feat_late, feat_other_late, _ = tied(
        head_w1, protos, teacher_protos, features, feat_other, parts
    )
    h0, h1, s0, s1 = call(
        hidden_kernel,
        (shape((hs, rows), BF16),) * 2 + (shape((hs, rows), F32),) * 2,
        [],
        feat_late, feat_other_late, w1_late,
        us=4,
    )
    cols = protos.shape[1] // nd
    pnb = unit_cols(lax.dynamic_slice_in_dim(protos_late, d * cols, cols, 1))[0].astype(BF16)
    tpnb = unit_cols(lax.dynamic_slice_in_dim(tprotos_late, d * cols, cols, 1))[0].astype(BF16)
    parts_got, h0, h1, s0, s1, pnb, tpnb = tied(parts_got, h0, h1, s0, s1, pnb, tpnb)

    got, zn, zinv = call(
        rows_kernel,
        (shape((n, sr + tr, bot), BF16), shape((sr + tr, bot), F32), shape((sr + tr, 1), F32)),
        [],
        parts_got,
    )
    got = lax.all_to_all(got, "proto", 0, 0)
    got_other = swap(got, "dp", 1)
    kern, msg, student = call(
        kern_kernel,
        (shape((nd * teach, cols), F32), shape((everyone, nd * teach // 128, 128), F32), shape((nd * rows, bot), BF16)),
        [d],
        got, got_other, tpnb,
        us=3,
    )
    msg_got = lax.all_to_all(msg, ALL, 0, 0)
    student, _ = tied(student, msg)
    exb, sums, sums_other, esum = student_sums(student, pnb)
    msg = call(
        second_kernel,
        shape((everyone, 1, nd * teach + rows), F32),
        [d],
        msg_got, kern, esum,
    )
    msg_got = lax.all_to_all(msg, ALL, 0, 0)
    sums, sums_other, _ = tied(sums, sums_other, msg)
    sums_other = swap(sums_other, "dp", 1)
    sums = (sums + sums_other).astype(BF16)
    msg_got, sums = tied(msg_got, sums)
    esum, last, mine, yours = call(
        third_kernel,
        (
            shape((rows, 1), F32),
            shape((nd * teach, cols), BF16),
            shape((teach, bot + 128), F32),
            shape((teach, bot + 128), F32),
        ),
        [d],
        msg_got, kern, pnb,
        us=2,
    )
    yours = swap(yours, "dp", 1)
    msg = call(message_kernel, shape((n, sr + 2 * tr, bot), BF16), [], sums, mine, yours)
    msg_got = lax.all_to_all(msg, "proto", 0, 0)

    esum, view_late, last, weights, place, _ = tied(esum, view, last, weights, place, msg)
    weights_other, last_other = swap(weights, "dp", 1), swap(last, "dp", 1)
    place_other = swap(place, "dp", 1)
    crop_scale = jnp.where(view_late == 2, 2.0, 1.0) * factor / esum
    scale_other = swap(crop_scale, "dp", 1)
    left = (student.astype(F32) * jnp.concatenate([crop_scale, scale_other], axis=0)).astype(BF16)
    dpn = dot(left, exb, ((0,), (0,))).astype(BF16)
    msg_got, dpn = tied(msg_got, dpn)
    dpn_other = swap(dpn, "dp", 1)
    dz = call(
        functools.partial(bottleneck_kernel, factor),
        shape((n, sr + tr, bot), BF16),
        [p],
        msg_got, zn, zinv, view_late, crop_scale,
    )
    got = lax.all_to_all(dz, "proto", 0, 0)
    weights, feat_late, _ = tied(weights, features, dz)
    slopes = slopes_of(d, p, feat_late, weights, weights_other, wide // n)
    got, slopes = tied(got, slopes)

    got_other = swap(got, "dp", 1)
    dz, grad_features = feature_grads(got, place, *slopes)
    grad_protos, grad_w1, grad_w2 = last_grads(
        d, head_w1, dz, got, got_other, place_other, protos, dpn, dpn_other, last, last_other,
        features, feat_other, h0, h1, s0, s1, head_w2,
    )
    grad_features = grad_features.T
    return (grad_features, grad_w1, grad_w2, grad_protos)


def body(features, teacher_features, *rest):
    n = lax.axis_size("proto")
    slot = (features.shape[0] // n, teacher_features.shape[0] // n)
    paired = lax.axis_size("dp") == 2 and n % 2 == 0 and slot[0] % 8 == 0 and slot[1] % 8 == 0
    paired = paired and features.shape[0] % teacher_features.shape[0] == 0
    return (paired_body if paired else general_body)(features, teacher_features, *rest)


def solution(mesh):
    in_specs = (
        P("dp", None),
        P("dp", None),
        P("dp"),
        P("dp"),
        P(None, "proto"),
        P("proto", None),
        P(None, "proto"),
        P(None, "proto"),
        P("proto", None),
        P(None, "proto"),
    )
    out_specs = (P("dp", "proto"), P(None, "proto"), P("proto", None), P(None, "proto"))
    return jax.shard_map(body, mesh=mesh, in_specs=in_specs, out_specs=out_specs, check_vma=False)
```

```python
import functools

import jax
import jax.numpy as jnp
from jax import lax
from jax.experimental import pallas as pl
from jax.experimental.pallas import tpu as pltpu
from jax.sharding import PartitionSpec as P

ITERS = 3
ALL = ("dp", "proto")
NEAR = 4
F32 = jnp.float32
BF16 = jnp.bfloat16


def gelu_parts(act):
    phi = 0.5 * (1.0 + lax.erf(act * 0.7071067811865476))
    slope = phi + act * jnp.exp(-0.5 * act * act) * 0.3989422804014327
    return (act * phi).astype(BF16), slope


def dot(a, b, dims):
    return lax.dot_general(a, b, (dims, ((), ())), preferred_element_type=F32)


def swap(value, axis, step):
    count = lax.axis_size(axis)
    return lax.ppermute(value, axis, [(i, i ^ step) for i in range(count)])


def over_dp(value):
    return [value] + [swap(value, "dp", s) for s in range(1, lax.axis_size("dp"))]


def tree_sum(parts):
    while len(parts) > 1:
        parts = [parts[i] + parts[i + 1] for i in range(0, len(parts), 2)]
    return parts[0]


def send_all(value, axes):
    count = lax.axis_size(axes)
    return lax.all_to_all(jnp.broadcast_to(value[None], (count,) + value.shape), axes, 0, 0)


def unit_cols(mat):
    matf = mat.astype(F32)
    inv = lax.rsqrt(jnp.sum(matf * matf, axis=0, keepdims=True) + 1e-06)
    return matf * inv, inv


def general_body(
    features,
    teacher_features,
    crop_image,
    crop_view,
    head_w1,
    head_w2,
    protos,
    teacher_w1,
    teacher_w2,
    teacher_protos,
):
    nd, n = lax.axis_size("dp"), lax.axis_size("proto")
    d, p = lax.axis_index("dp"), lax.axis_index("proto")
    rows, img = features.shape[0], teacher_features.shape[0] // 2
    per = rows // img
    sr, tr = rows // n, 2 * img // n
    bot = head_w2.shape[1]
    factor = 10.0 / (18 * img * nd)
    absolute = d ^ jnp.arange(nd)

    im = crop_image - d * img
    at = jnp.arange(rows, dtype=jnp.int32)
    rank = jnp.sum((im[:, None] == im[None, :]) & (at[None, :] < at[:, None]), axis=1)
    place = im * per + rank
    hit = at[:, None] == place[None, :]
    order = hit.astype(BF16)
    view = jnp.sum(jnp.where(hit, crop_view[None, :], 0), axis=1)
    views = jnp.stack(over_dp(view))[absolute]

    w1_block = lax.all_to_all(head_w1, "proto", split_axis=0, concat_axis=1, tiled=True)
    feats = over_dp(features)
    act = jnp.dot(features, head_w1, preferred_element_type=F32)
    hidden, slope = gelu_parts(act)
    zpart = jnp.dot(hidden, head_w2, preferred_element_type=F32).astype(BF16)
    zpart = jnp.dot(order, zpart, preferred_element_type=F32).astype(BF16)
    tact = jnp.dot(teacher_features, teacher_w1, preferred_element_type=F32)
    thidden, _ = gelu_parts(tact)
    tpart = jnp.dot(thidden, teacher_w2, preferred_element_type=F32).astype(BF16)
    parts = jnp.concatenate([zpart.reshape(n, sr, bot), tpart.reshape(n, tr, bot)], axis=1)
    parts = lax.all_to_all(parts, "proto", 0, 0)
    early = jnp.concatenate(
        [(slope - 0.5).astype(BF16)] + [head_w2[:, i : i + head_w1.shape[1]] for i in range(0, bot, head_w1.shape[1])],
        axis=0,
    )
    early = lax.all_gather(early, "proto")
    zrow = jnp.sum(parts.astype(F32), axis=0)
    zinv = lax.rsqrt(jnp.sum(zrow * zrow, axis=1, keepdims=True) + 1e-06)
    zn = zrow * zinv
    znb = send_all(zn.astype(BF16), "proto")
    znb = jnp.stack(over_dp(znb))[absolute]
    student = znb[:, :, :sr].reshape(nd * rows, bot)
    teacher = znb[:, :, sr:].reshape(nd * 2 * img, bot)

    cols = protos.shape[1] // nd
    pn, pinv = unit_cols(lax.dynamic_slice_in_dim(protos, d * cols, cols, 1))
    pnb = pn.astype(BF16)
    tpnb = unit_cols(lax.dynamic_slice_in_dim(teacher_protos, d * cols, cols, 1))[0].astype(BF16)

    kern = jnp.exp(jnp.dot(teacher, tpnb, preferred_element_type=F32) / 0.07)
    ex = jnp.exp(jnp.dot(student, pnb, preferred_element_type=F32) / 0.1)
    esum = jnp.sum(ex, axis=1)
    exb = ex.astype(BF16)
    sums = dot(exb, pnb, ((1,), (1,)))
    colscale = 1.0 / jnp.sum(kern, axis=0)
    for step in range(ITERS - 1):
        mass = jnp.sum(send_all(jnp.sum(kern * colscale[None, :], axis=1), ALL), axis=0)
        colscale = 1.0 / jnp.sum(kern / mass[:, None], axis=0)
    last = kern * colscale[None, :]
    lastb = last.astype(BF16)
    tsums = dot(lastb, pnb, ((1,), (1,)))
    tot = jnp.sum(send_all(jnp.concatenate([esum, jnp.sum(last, axis=1)]), ALL), axis=0)
    esum, mass = tot[: nd * rows], tot[nd * rows :]

    out = jnp.concatenate([sums.reshape(nd, n, sr, bot), tsums.reshape(nd, n, tr, bot)], axis=2)
    out = out[absolute]
    out = tree_sum([out[0]] + [swap(out[s], "dp", s) for s in range(1, nd)])
    out = jnp.sum(lax.all_to_all(out, "proto", 0, 0), axis=0)
    crop_scale = jnp.where(views == 2, 2.0, 1.0).reshape(-1) / esum * factor
    image_scale = factor / mass
    mine = (d * n + p)
    my_view = lax.dynamic_slice_in_dim(views.reshape(-1), mine * sr, sr)
    my_scale = lax.dynamic_slice_in_dim(crop_scale, mine * sr, sr)
    my_image = lax.dynamic_slice_in_dim(image_scale, mine * tr, tr)
    slot = jnp.arange(tr)
    pick = (slot[None, :] // 2 == jnp.arange(sr)[:, None] // per) & (slot[None, :] % 2 != my_view[:, None])
    target = jnp.sum(jnp.where(pick, my_image[None, :], 0.0)[:, :, None] * out[None, sr:], axis=1)
    dzn = my_scale[:, None] * out[:sr] - target
    zs, zi = zn[:sr], zinv[:sr]
    dz = (zi * (dzn - zs * jnp.sum(zs * dzn, axis=1, keepdims=True))).astype(BF16)
    dz = send_all(dz, "proto").reshape(rows, bot)
    dz = dot(order, dz, ((0,), (0,))).astype(BF16)
    dzs = over_dp(dz)

    tslot = jnp.arange(2 * img)
    picks = (tslot[None, None, :] // 2 == at[None, :, None] // per) & (tslot[None, None, :] % 2 != views[:, :, None])
    own = lax.dot_general(
        picks.astype(BF16), student.reshape(nd, rows, bot), (((1,), (1,)), ((0,), (0,))), preferred_element_type=F32
    ).reshape(nd * 2 * img, bot)
    left = (student.astype(F32) * crop_scale[:, None]).astype(BF16)
    right = (own * image_scale[:, None]).astype(BF16)
    dpn = dot(left, exb, ((0,), (0,))) - dot(right, lastb, ((0,), (0,)))
    gp = pinv * (dpn - pn * jnp.sum(pn * dpn, axis=0, keepdims=True))
    gps = over_dp(gp)
    grad_protos = jnp.zeros(protos.shape, F32)
    for s in range(nd):
        grad_protos = lax.dynamic_update_slice_in_dim(grad_protos, gps[s], (d ^ s) * cols, 1)

    w1_parts, w2_parts = [], []
    for s in range(nd):
        if s:
            hid, slp = gelu_parts(jnp.dot(feats[s], head_w1, preferred_element_type=F32))
        else:
            hid, slp = hidden, slope
        w2_parts.append(dot(hid, dzs[s], ((0,), (0,))))
        dhid = (dot(dzs[s], head_w2, ((1,), (1,))) * slp).astype(BF16)
        w1_parts.append(dot(feats[s], dhid, ((0,), (0,))))
    grad_w1, grad_w2 = tree_sum(w1_parts), tree_sum(w2_parts)
    slopes = 0.5 + early[:, :rows].astype(F32).transpose(1, 0, 2).reshape(rows, -1)
    w2_all = early[:, rows:].reshape(n, -1, head_w1.shape[1], head_w1.shape[1]).transpose(1, 3, 0, 2)
    w2_all = w2_all.reshape(bot, -1)
    dhid = (jnp.dot(dz, w2_all, preferred_element_type=F32) * slopes).astype(BF16)
    grad_features = dot(dhid, w1_block, ((1,), (1,))).astype(BF16)
    return (grad_features, grad_w1, grad_w2, grad_protos)


def params(mib=56):
    return pltpu.CompilerParams(vmem_limit_bytes=mib * 1024 * 1024)


def shape(dims, dtype):
    return jax.ShapeDtypeStruct(dims, dtype)


def kernel_name(kernel):
    return getattr(kernel, "func", kernel).__name__


def block(dims):
    return pl.BlockSpec(dims, lambda i: (0,) * len(dims))


def call(kernel, outs, scalars, *args, us=1, mib=56):
    smem = [jnp.asarray(s, jnp.int32).reshape(1) for s in scalars]
    return pl.pallas_call(
        kernel,
        grid=(1,),
        out_shape=outs,
        in_specs=[pl.BlockSpec(memory_space=pltpu.SMEM)] * len(smem) + [block(x.shape) for x in args],
        out_specs=jax.tree.map(lambda x: block(x.shape), outs),
        compiler_params=params(mib),
        name=kernel_name(kernel),
        cost_estimate=pl.CostEstimate(flops=us * 10**9, bytes_accessed=us * 10**6, transcendentals=0),
    )(*smem, *args)


def grids(dims):
    return lax.broadcasted_iota(jnp.int32, dims, 0), lax.broadcasted_iota(jnp.int32, dims, 1)


def to_row(col):
    down, along = grids((col.shape[0], col.shape[0]))
    return jnp.sum(jnp.where(down == along, col, jnp.zeros_like(col)), axis=0, keepdims=True)


def to_col(row):
    down, along = grids((row.shape[1], row.shape[1]))
    return jnp.sum(jnp.where(down == along, row, jnp.zeros_like(row)), axis=1, keepdims=True)


def head_kernel(d_ref, *refs):
    sources, im_ref, view_ref = refs[:6], refs[6], refs[7]
    parts_ref, place_ref, vs_ref, pack_ref = refs[8:12]
    held, sems = refs[12:18], refs[18]
    copies = [pltpu.make_async_copy(a, b, sems.at[k]) for k, (a, b) in enumerate(zip(sources, held))]
    for copy in copies:
        copy.start()
    f_ref, w1_ref, w2_ref, tf_ref, tw1_ref, tw2_ref = held
    rows, teach = f_ref.shape[0], tf_ref.shape[0]
    n = parts_ref.shape[0]
    img = teach // 2
    per = rows // img
    im = (im_ref[...].reshape(1, rows) - d_ref[0] * img).astype(F32)
    down, along = grids((rows, rows))
    imc = to_col(im)
    same = im == imc
    after = jnp.where(same & (down < along), 1.0, 0.0)
    row = im * per + jnp.sum(after, axis=0, keepdims=True)
    place_ref[...] = row
    hit = row.astype(jnp.int32) == down
    vs_ref[...] = jnp.sum(jnp.where(hit, view_ref[...].reshape(1, rows).astype(F32), 0.0), axis=1, keepdims=True)
    order = jnp.where(hit, 1.0, 0.0).astype(BF16)

    for copy in copies:
        copy.wait()

    deep, hs = w1_ref.shape[0] // 2, w1_ref.shape[1]
    half = hs // 2
    pack_ref[:deep] = w1_ref[pl.ds(pl.multiple_of(d_ref[0] * deep, deep), deep)]
    w2_half = w2_ref[pl.ds(pl.multiple_of(d_ref[0] * half, half), half)]
    pack_ref[deep : deep + half] = w2_half[:, :hs]
    pack_ref[deep + half :] = w2_half[:, hs:]

    def part(x, first, second):
        act = dot(x[...], first[...], ((1,), (0,)))
        hidden = (act * 0.5 * (1.0 + lax.erf(act * 0.7071067811865476))).astype(BF16)
        return dot(hidden, second[...], ((1,), (0,)))

    z = part(f_ref, w1_ref, w2_ref).astype(BF16)
    z = dot(order, z, ((1,), (0,))).reshape(n, rows // n, -1)
    t = part(tf_ref, tw1_ref, tw2_ref).reshape(n, teach // n, -1)
    parts_ref[...] = jnp.concatenate([z, t], axis=1).astype(BF16)


def rows_kernel(parts_ref, out_ref, zn_ref, zinv_ref):
    z = jnp.sum(parts_ref[...].astype(F32), axis=0)
    inv = lax.rsqrt(jnp.sum(z * z, axis=1, keepdims=True) + 1e-06)
    zn = z * inv
    zn_ref[...] = zn
    zinv_ref[...] = inv
    out_ref[...] = jnp.broadcast_to(zn[None], out_ref.shape).astype(BF16)


def row_mass(kern, mass):
    if mass is None:
        scale = 1.0 / jnp.sum(kern, axis=0, keepdims=True)
    else:
        scale = 1.0 / jnp.sum(kern * (1.0 / mass), axis=0, keepdims=True)
    return scale, jnp.sum(kern * scale, axis=1, keepdims=True)


def fold(col):
    row = to_row(col)
    return jnp.concatenate([row[:, k : k + 128] for k in range(0, row.shape[1], 128)], axis=0)


def unfold(block):
    return to_col(jnp.concatenate([block[k : k + 1] for k in range(block.shape[0])], axis=1))


def kern_kernel(d_ref, got_ref, other_ref, tpnb_ref, kern_ref, msg_ref, student_ref):
    n, slot, bot = got_ref.shape
    rows = student_ref.shape[0] // 2
    sr = rows // n
    own, other = got_ref[...].astype(F32), other_ref[...].astype(F32)
    student_ref[:rows] = own[:, :sr].reshape(rows, bot).astype(BF16)
    student_ref[rows:] = other[:, :sr].reshape(rows, bot).astype(BF16)
    own, other = own[:, sr:].reshape(-1, bot), other[:, sr:].reshape(-1, bot)
    first = d_ref[0] == 0
    teacher = jnp.concatenate([jnp.where(first, own, other), jnp.where(first, other, own)], axis=0).astype(BF16)
    kern = jnp.exp(dot(teacher, tpnb_ref[...], ((1,), (0,))) * (1.0 / 0.07))
    kern_ref[...] = kern
    _, mass = row_mass(kern, None)
    msg_ref[...] = jnp.broadcast_to(fold(mass)[None], msg_ref.shape)


def student_kernel(z_ref, pnb_ref, exb_ref, own_ref, other_ref, esum_ref):
    step = pl.program_id(0)
    ex = jnp.exp(dot(z_ref[...], pnb_ref[...], ((1,), (0,))) * 10.0)
    esum_ref[...] = jnp.sum(ex, axis=1, keepdims=True)
    exb = ex.astype(BF16)
    exb_ref[...] = exb
    sums = dot(exb, pnb_ref[...], ((1,), (1,)))

    @pl.when(step < pl.num_programs(0) // 2)
    def _():
        own_ref[...] = sums

    @pl.when(step >= pl.num_programs(0) // 2)
    def _():
        other_ref[...] = sums


def student_sums(student, pnb):
    total, bot = student.shape
    cols = pnb.shape[1]
    tile = total // 4
    return pl.pallas_call(
        student_kernel,
        name="student_kernel",
        grid=(4,),
        out_shape=(
            shape((total, cols), BF16),
            shape((total // 2, bot), F32),
            shape((total // 2, bot), F32),
            shape((total, 1), F32),
        ),
        in_specs=[pl.BlockSpec((tile, bot), lambda i: (i, 0)), pl.BlockSpec((bot, cols), lambda i: (0, 0))],
        out_specs=(
            pl.BlockSpec((tile, cols), lambda i: (i, 0)),
            pl.BlockSpec((tile, bot), lambda i: (jnp.minimum(i, 1), 0)),
            pl.BlockSpec((tile, bot), lambda i: (jnp.maximum(i - 2, 0), 0)),
            pl.BlockSpec((tile, 1), lambda i: (i, 0)),
        ),
        compiler_params=params(),
        cost_estimate=pl.CostEstimate(flops=5 * 10**9, bytes_accessed=10**7, transcendentals=0),
    )(student, pnb)


def second_kernel(d_ref, got_ref, kern_ref, esum_ref, msg_ref):
    mass = unfold(jnp.sum(got_ref[...], axis=0))
    _, mass = row_mass(kern_ref[...], mass)
    half = esum_ref.shape[0] // 2
    own, other = to_row(esum_ref[:half]), to_row(esum_ref[half:])
    first = d_ref[0] == 0
    mass = to_row(mass)
    n = msg_ref.shape[0] // 2
    for k, row in enumerate((jnp.where(first, own, other), jnp.where(first, other, own))):
        part = jnp.concatenate([mass, row], axis=1)
        msg_ref[k * n : (k + 1) * n] = jnp.broadcast_to(part[None], (n,) + part.shape)


def third_kernel(d_ref, got_ref, kern_ref, pnb_ref, esum_ref, last_ref, mine_ref, yours_ref):
    teach = kern_ref.shape[0]
    got = jnp.sum(got_ref[...], axis=0)
    esum_ref[...] = to_col(got[:, teach:])
    kern = kern_ref[...]
    scale, mass = row_mass(kern, to_col(got[:, :teach]))
    last = (kern * scale).astype(BF16)
    last_ref[...] = last
    sums = dot(last, pnb_ref[...], ((1,), (1,)))
    sums = jnp.concatenate([sums, jnp.broadcast_to(mass, (teach, 128))], axis=1)
    half = teach // 2
    first = d_ref[0] == 0
    mine_ref[...] = jnp.where(first, sums[:half], sums[half:])
    yours_ref[...] = jnp.where(first, sums[half:], sums[:half])


def message_kernel(sums_ref, b0_ref, b1_ref, out_ref):
    n = out_ref.shape[0]
    rows, bot = sums_ref.shape
    sums = sums_ref[...].astype(F32).reshape(n, rows // n, bot)
    both = b0_ref[...] + b1_ref[...]
    mass = both[:, bot:]
    high = mass.astype(BF16).astype(F32)
    tail = jnp.concatenate([high, mass - high], axis=1)
    teach = both.shape[0]
    both = both[:, :bot].reshape(n, teach // n, bot)
    out_ref[...] = jnp.concatenate([sums, both, tail.reshape(n, teach // n, bot)], axis=1).astype(BF16)


def bottleneck_kernel(factor, p_ref, got_ref, zn_ref, zinv_ref, view_ref, scale_ref, out_ref):
    sr = view_ref.shape[0] // out_ref.shape[0]
    mine = pl.ds(pl.multiple_of(p_ref[0] * sr, sr), sr)
    tr = zn_ref.shape[0] - sr
    per = sr // (tr // 2)
    out = jnp.sum(got_ref[...].astype(F32), axis=0)
    tail = out[sr + tr :]
    image = factor / (tail[:, :1] + tail[:, 128:129])
    sums = out[sr : sr + tr] * image
    zn, zinv = zn_ref[:sr], zinv_ref[:sr]
    znb = zn.astype(BF16).astype(F32)
    view = view_ref[mine].astype(jnp.int32)
    which = lax.broadcasted_iota(jnp.int32, (sr, 1), 0)
    dzn = scale_ref[mine] * out[:sr]
    own = []
    for t in range(tr):
        base = (t // 2) * per
        pick = (which >= base) & (which < base + per) & (view != t % 2)
        dzn = dzn - jnp.where(pick, sums[t : t + 1], 0.0)
        own.append(jnp.sum(jnp.where(pick, znb, 0.0), axis=0, keepdims=True) * image[t : t + 1])
    dz = zinv * (dzn - zn * jnp.sum(zn * dzn, axis=1, keepdims=True))
    both = jnp.concatenate([dz] + own, axis=0)
    out_ref[...] = jnp.broadcast_to(both[None], out_ref.shape).astype(BF16)


def hidden_kernel(f0_ref, f1_ref, w1_ref, h0_ref, h1_ref, s0_ref, s1_ref):
    for f, h, s in ((f0_ref, h0_ref, s0_ref), (f1_ref, h1_ref, s1_ref)):
        act = dot(f[...], w1_ref[...], ((1,), (0,))).T
        phi = 0.5 * (1.0 + lax.erf(act * 0.7071067811865476))
        h[...] = (act * phi).astype(BF16)
        s[...] = phi + act * jnp.exp(-0.5 * act * act) * 0.3989422804014327


def slopes_kernel(d_ref, p_ref, f_ref, own_ref, other_ref, slope_ref, w2_ref, w1_ref):
    hs = own_ref.shape[2]
    deep = f_ref.shape[1] // 2
    first = d_ref[0] == 0
    own, other = own_ref[...], other_ref[...]
    low = jnp.where(first, own, other)
    high = jnp.where(first, other, own)
    a, b = (jnp.concatenate([x[0], x[1]], axis=1) for x in (low[:, :deep], high[:, :deep]))
    act = dot(f_ref[:, :deep], a, ((1,), (0,))) + dot(f_ref[:, deep:], b, ((1,), (0,)))
    phi = 0.5 * (1.0 + lax.erf(act * 0.7071067811865476))
    slope_ref[...] = phi + act * jnp.exp(-0.5 * act * act) * 0.3989422804014327
    groups, width = w1_ref.shape[0], w1_ref.shape[1]
    blocks = deep // width
    for k in range(groups):
        chip = p_ref[0] ^ (k * NEAR)
        at = pl.multiple_of(lax.rem(chip, blocks) * width, width)
        mine = (chip // blocks) == d_ref[0]
        rows = jnp.where(mine, own_ref[:, pl.ds(at, width)], other_ref[:, pl.ds(at, width)])
        w1_ref[k] = jnp.concatenate([rows[0], rows[1]], axis=1)
    half = hs // 2
    for k in range(2):
        for part, x in ((0, low), (1, high)):
            tail = jnp.concatenate([x[k, deep : deep + half], x[k, deep + half :]], axis=1)
            w2_ref[k * hs + part * half : k * hs + (part + 1) * half] = tail


def slopes_of(d, p, features, own, other, width, groups):
    n, tall, hs = own.shape
    rows = features.shape[0]
    whole = lambda k, d, p: (0, 0)
    return pl.pallas_call(
        slopes_kernel,
        name="slopes_kernel",
        grid_spec=pltpu.PrefetchScalarGridSpec(
            num_scalar_prefetch=2,
            grid=(n // 2,),
            in_specs=[
                pl.BlockSpec(features.shape, whole),
                pl.BlockSpec((2, tall, hs), lambda k, d, p: (k, 0, 0)),
                pl.BlockSpec((2, tall, hs), lambda k, d, p: (k, 0, 0)),
            ],
            out_specs=(
                pl.BlockSpec((rows, 2 * hs), lambda k, d, p: (0, k)),
                pl.BlockSpec((2 * hs, 2 * hs), lambda k, d, p: (k, 0)),
                pl.BlockSpec((groups, width, 2 * hs), lambda k, d, p: (0, 0, k)),
            ),
        ),
        out_shape=(shape((rows, n * hs), F32), shape((n * hs, 2 * hs), BF16), shape((groups, width, n * hs), BF16)),
        compiler_params=params(),
        cost_estimate=pl.CostEstimate(flops=4 * 10**9, bytes_accessed=3 * 10**7, transcendentals=0),
    )(d.reshape(1), p.reshape(1), features, own, other)


def fetch(pairs, sems):
    copies = [pltpu.make_async_copy(x, y, sems.at[k]) for k, (x, y) in enumerate(pairs)]
    for copy in copies:
        copy.start()
    return copies


def put_back(got, place):
    n, _, bot = got.shape
    rows = place.shape[1]
    _, along = grids((rows, rows))
    back = jnp.where(to_col(place).astype(jnp.int32) == along, 1.0, 0.0).astype(BF16)
    dz = got.astype(F32)[:, : rows // n].reshape(rows, bot).astype(BF16)
    return dot(back, dz, ((1,), (0,))).astype(BF16)


def features_kernel(step, *refs):
    ins, (dz_ref, own_ref, far_ref), held, sems = refs[:5], refs[5:8], refs[8:13], refs[13]
    got, place, slope, w2, w1 = held
    groups, width = w1.shape[:2]
    pieces = [pl.ds(k, step) for k in range(0, slope.shape[1], step)]
    small = fetch([(ins[k], held[k]) for k in (0, 1, 4)], sems.at[pl.ds(0, 3)])
    large = []
    for k, piece in enumerate(pieces):
        pairs = [(ins[2].at[:, piece], slope.at[:, piece]), (ins[3].at[piece], w2.at[piece])]
        large.append(fetch(pairs, sems.at[pl.ds(3 + 2 * k, 2)]))
    for copy in small:
        copy.wait()
    dz = put_back(got[...], place[...])
    dz_ref[...] = dz
    total = None
    for piece, copies in zip(pieces, large):
        for copy in copies:
            copy.wait()
        dhid = (dot(dz, w2[piece], ((1,), (1,))) * slope[:, piece]).astype(BF16)
        part = dot(w1[:, :, piece].reshape(groups * width, step), dhid, ((1,), (1,)))
        total = part if total is None else total + part
    own_ref[...] = total[:width]
    for k in range(1, groups):
        far_ref[k - 1] = total[k * width : (k + 1) * width].astype(BF16)


def feature_grads(got, place, slope, w2, w1):
    args = (got, place, slope, w2, w1)
    rows, hidden = slope.shape
    bot, step = got.shape[2], 256
    groups, width = w1.shape[:2]
    outs = (shape((rows, bot), BF16), shape((width, rows), F32), shape((groups - 1, width, rows), BF16))
    return pl.pallas_call(
        functools.partial(features_kernel, step),
        name="features_kernel",
        grid=(1,),
        out_shape=outs,
        in_specs=[pl.BlockSpec(memory_space=pl.ANY)] * len(args),
        out_specs=tuple(block(x.shape) for x in outs),
        scratch_shapes=[pltpu.VMEM(x.shape, x.dtype) for x in args]
        + [pltpu.SemaphoreType.DMA((3 + 2 * (hidden // step),))],
        compiler_params=params(),
    )(*args)


def last_kernel(tile, d_ref, *refs):
    ins, (gp_hbm, g1_hbm, g2_hbm) = refs[:16], refs[16:19]
    held, (gp, g1, g2, sems, tile_sems, out_sems) = refs[19:35], refs[35:]
    dz0, got0, got1, place1, protos, down, dother, lown, lother, f0, f1, h0, h1, s0, s1, w2 = held
    cols = protos.shape[1] // 2
    steps = cols // tile
    rows = dz0.shape[0]
    n, slot, bot = got0.shape
    early = fetch([(ins[k], held[k]) for k in range(4)], sems)
    tiles = []
    for k in range(2 * steps):
        own = k < steps
        here = pl.multiple_of((d_ref[0] if own else 1 - d_ref[0]) * cols + (k % steps) * tile, tile)
        there = pl.ds((k % steps) * tile, tile)
        a, b = (5, 7) if own else (6, 8)
        pairs = [
            (ins[4].at[:, pl.ds(here, tile)], protos.at[:, pl.ds(here, tile)]),
            (ins[a].at[:, there], held[a].at[:, there]),
            (ins[b].at[:, there], held[b].at[:, there]),
        ]
        tiles.append((here, there, a, b, fetch(pairs, tile_sems.at[k])))
    late = fetch([(ins[k], held[k]) for k in range(9, 16)], sems.at[pl.ds(4, 7)])
    for copy in early:
        copy.wait()
    first = d_ref[0] == 0
    right0 = got0[...].astype(F32)[:, rows // n :].reshape(-1, bot)
    right1 = got1[...].astype(F32)[:, rows // n :].reshape(-1, bot)
    right = jnp.concatenate([jnp.where(first, right0, right1), jnp.where(first, right1, right0)], axis=0)
    right = right.T.astype(BF16)
    dz1 = put_back(got1[...], place1[...])
    outs = []
    for k, (here, there, a, b, copies) in enumerate(tiles):
        for copy in copies:
            copy.wait()
        mat = protos[:, pl.ds(here, tile)].astype(F32)
        inv = lax.rsqrt(jnp.sum(mat * mat, axis=0, keepdims=True) + 1e-06)
        pn = mat * inv
        dpn = held[a][:, there].astype(F32) - dot(right, held[b][:, there], ((1,), (0,)))
        gp[:, pl.ds(here, tile)] = inv * (dpn - pn * jnp.sum(pn * dpn, axis=0, keepdims=True))
        out = pltpu.make_async_copy(gp.at[:, pl.ds(here, tile)], gp_hbm.at[:, pl.ds(here, tile)], out_sems.at[k])
        out.start()
        outs.append(out)
    for copy in late:
        copy.wait()
    sums1, sums2 = [], []
    for f, dz, h, sl in ((f0, dz0[...], h0, s0), (f1, dz1, h1, s1)):
        sums2.append(dot(h[...], dz, ((1,), (0,))))
        dhid = (dot(w2[...], dz, ((1,), (1,))) * sl[...]).astype(BF16)
        sums1.append(dot(dhid, f[...], ((1,), (0,))))
    g1[...] = (sums1[0] + sums1[1]).T
    g2[...] = sums2[0] + sums2[1]
    for k, (x, y) in enumerate(((g1, g1_hbm), (g2, g2_hbm))):
        out = pltpu.make_async_copy(x, y, out_sems.at[2 * steps + k])
        out.start()
        outs.append(out)
    for out in outs:
        out.wait()


def last_grads(d, head_w1, *args):
    tile = 512
    protos, head_w2 = args[4], args[15]
    tiles = protos.shape[1] // tile
    outs = (shape(protos.shape, F32), shape(head_w1.shape, F32), shape(head_w2.shape, F32))
    anywhere = pl.BlockSpec(memory_space=pl.ANY)
    return pl.pallas_call(
        functools.partial(last_kernel, tile),
        name="last_kernel",
        out_shape=outs,
        in_specs=[pl.BlockSpec(memory_space=pltpu.SMEM)] + [anywhere] * len(args),
        out_specs=(anywhere,) * 3,
        scratch_shapes=[pltpu.VMEM(x.shape, x.dtype) for x in args + outs]
        + [
            pltpu.SemaphoreType.DMA((11,)),
            pltpu.SemaphoreType.DMA((tiles, 3)),
            pltpu.SemaphoreType.DMA((tiles + 2,)),
        ],
        compiler_params=params(),
    )(d.reshape(1), *args)


def tied(*values):
    return lax.optimization_barrier(values)


def paired_body(
    features,
    teacher_features,
    crop_image,
    crop_view,
    head_w1,
    head_w2,
    protos,
    teacher_w1,
    teacher_w2,
    teacher_protos,
):
    nd, n = lax.axis_size("dp"), lax.axis_size("proto")
    d, p = lax.axis_index("dp"), lax.axis_index("proto")
    rows, teach = features.shape[0], teacher_features.shape[0]
    sr, tr = rows // n, teach // n
    wide, hs = head_w1.shape
    bot = head_w2.shape[1]
    everyone = nd * n
    factor = 10.0 / (9 * teach * nd)

    feat_other = swap(features, "dp", 1)
    heads = (features, head_w1, head_w2, teacher_features, teacher_w1, teacher_w2)
    parts, place, view, weights = pl.pallas_call(
        head_kernel,
        grid=(1,),
        out_shape=(
            shape((n, sr + tr, bot), BF16),
            shape((1, rows), F32),
            shape((rows, 1), F32),
            shape((wide // 2 + hs, hs), BF16),
        ),
        in_specs=[pl.BlockSpec(memory_space=pltpu.SMEM)]
        + [pl.BlockSpec(memory_space=pl.ANY)] * 6
        + [block((rows,))] * 2,
        out_specs=(block((n, sr + tr, bot)), block((1, rows)), block((rows, 1)), block((wide // 2 + hs, hs))),
        scratch_shapes=[pltpu.VMEM(x.shape, x.dtype) for x in heads] + [pltpu.SemaphoreType.DMA((6,))],
        compiler_params=params(),
        name="head_kernel",
    )(d.reshape(1), *heads, crop_image, crop_view)
    weights = [weights] + [swap(weights, "proto", k) for k in range(1, NEAR)]
    parts_got = lax.all_to_all(parts, "proto", 0, 0)
    w1_late, protos_late, tprotos_late, feat_late, feat_other_late, _ = tied(
        head_w1, protos, teacher_protos, features, feat_other, parts
    )
    h0, h1, s0, s1 = call(
        hidden_kernel,
        (shape((hs, rows), BF16),) * 2 + (shape((hs, rows), F32),) * 2,
        [],
        feat_late, feat_other_late, w1_late,
        us=4,
    )
    cols = protos.shape[1] // nd
    pnb = unit_cols(lax.dynamic_slice_in_dim(protos_late, d * cols, cols, 1))[0].astype(BF16)
    tpnb = unit_cols(lax.dynamic_slice_in_dim(tprotos_late, d * cols, cols, 1))[0].astype(BF16)
    weights = jnp.stack(weights)
    parts_got, h0, h1, s0, s1, pnb, tpnb, weights = tied(parts_got, h0, h1, s0, s1, pnb, tpnb, weights)

    got, zn, zinv = call(
        rows_kernel,
        (shape((n, sr + tr, bot), BF16), shape((sr + tr, bot), F32), shape((sr + tr, 1), F32)),
        [],
        parts_got,
    )
    got = lax.all_to_all(got, "proto", 0, 0)
    got_other = swap(got, "dp", 1)
    kern, msg, student = call(
        kern_kernel,
        (shape((nd * teach, cols), F32), shape((everyone, nd * teach // 128, 128), F32), shape((nd * rows, bot), BF16)),
        [d],
        got, got_other, tpnb,
        us=3,
    )
    msg_got = lax.all_to_all(msg, ALL, 0, 0)
    student, _ = tied(student, msg)
    exb, sums, sums_other, esum = student_sums(student, pnb)
    msg = call(
        second_kernel,
        shape((everyone, 1, nd * teach + rows), F32),
        [d],
        msg_got, kern, esum,
    )
    msg_got = lax.all_to_all(msg, ALL, 0, 0)
    sums, sums_other, _ = tied(sums, sums_other, msg)
    sums_other = swap(sums_other, "dp", 1)
    sums = (sums + sums_other).astype(BF16)
    msg_got, sums = tied(msg_got, sums)
    esum, last, mine, yours = call(
        third_kernel,
        (
            shape((rows, 1), F32),
            shape((nd * teach, cols), BF16),
            shape((teach, bot + 128), F32),
            shape((teach, bot + 128), F32),
        ),
        [d],
        msg_got, kern, pnb,
        us=2,
    )
    yours = swap(yours, "dp", 1)
    msg = call(message_kernel, shape((n, sr + 2 * tr, bot), BF16), [], sums, mine, yours)
    msg_got = lax.all_to_all(msg, "proto", 0, 0)

    esum, view_late, last, weights, place, _ = tied(esum, view, last, weights, place, msg)
    weights_other, last_other = swap(weights, "dp", 1), swap(last, "dp", 1)
    place_other = swap(place, "dp", 1)
    crop_scale = jnp.where(view_late == 2, 2.0, 1.0) * factor / esum
    scale_other = swap(crop_scale, "dp", 1)
    left = (student.astype(F32) * jnp.concatenate([crop_scale, scale_other], axis=0)).astype(BF16)
    dpn = dot(left, exb, ((0,), (0,))).astype(BF16)
    msg_got, dpn = tied(msg_got, dpn)
    dpn_other = swap(dpn, "dp", 1)
    dz = call(
        functools.partial(bottleneck_kernel, factor),
        shape((n, sr + tr, bot), BF16),
        [p],
        msg_got, zn, zinv, view_late, crop_scale,
    )
    got = lax.all_to_all(dz, "proto", 0, 0)
    weights, feat_late, _ = tied(weights, features, dz)
    slopes = slopes_of(d, p, feat_late, weights, weights_other, wide // n, n // NEAR)
    got, slopes = tied(got, slopes)

    got_other = swap(got, "dp", 1)
    dz, grad_features, far = feature_grads(got, place, *slopes)
    far = [swap(far[k - 1], "proto", k * NEAR) for k in range(1, n // NEAR)]
    grad_protos, grad_w1, grad_w2 = last_grads(
        d, head_w1, dz, got, got_other, place_other, protos, dpn, dpn_other, last, last_other,
        features, feat_other, h0, h1, s0, s1, head_w2,
    )
    grad_protos, *far = tied(grad_protos, *far)
    grad_features = (grad_features + sum(x.astype(F32) for x in far)).astype(BF16).T
    return (grad_features, grad_w1, grad_w2, grad_protos)


def body(features, teacher_features, *rest):
    n = lax.axis_size("proto")
    slot = (features.shape[0] // n, teacher_features.shape[0] // n)
    paired = lax.axis_size("dp") == 2 and n == 4 * NEAR and slot[0] % 8 == 0 and slot[1] % 8 == 0
    paired = paired and features.shape[0] % teacher_features.shape[0] == 0
    return (paired_body if paired else general_body)(features, teacher_features, *rest)


def solution(mesh):
    in_specs = (
        P("dp", None),
        P("dp", None),
        P("dp"),
        P("dp"),
        P(None, "proto"),
        P("proto", None),
        P(None, "proto"),
        P(None, "proto"),
        P("proto", None),
        P(None, "proto"),
    )
    out_specs = (P("dp", "proto"), P(None, "proto"), P("proto", None), P(None, "proto"))
    return jax.shard_map(body, mesh=mesh, in_specs=in_specs, out_specs=out_specs, check_vma=False)
```

```python
import functools

import jax
import jax.numpy as jnp
from jax import lax
from jax.experimental import pallas as pl
from jax.experimental.pallas import tpu as pltpu
from jax.sharding import PartitionSpec as P

ITERS = 3
ALL = ("dp", "proto")
NEAR = 4
F32 = jnp.float32
BF16 = jnp.bfloat16


def gelu_parts(act):
    phi = 0.5 * (1.0 + lax.erf(act * 0.7071067811865476))
    slope = phi + act * jnp.exp(-0.5 * act * act) * 0.3989422804014327
    return (act * phi).astype(BF16), slope


def dot(a, b, dims):
    return lax.dot_general(a, b, (dims, ((), ())), preferred_element_type=F32)


def swap(value, axis, step):
    count = lax.axis_size(axis)
    return lax.ppermute(value, axis, [(i, i ^ step) for i in range(count)])


def over_dp(value):
    return [value] + [swap(value, "dp", s) for s in range(1, lax.axis_size("dp"))]


def tree_sum(parts):
    while len(parts) > 1:
        parts = [parts[i] + parts[i + 1] for i in range(0, len(parts), 2)]
    return parts[0]


def send_all(value, axes):
    count = lax.axis_size(axes)
    return lax.all_to_all(jnp.broadcast_to(value[None], (count,) + value.shape), axes, 0, 0)


def unit_cols(mat):
    matf = mat.astype(F32)
    inv = lax.rsqrt(jnp.sum(matf * matf, axis=0, keepdims=True) + 1e-06)
    return matf * inv, inv


def general_body(
    features,
    teacher_features,
    crop_image,
    crop_view,
    head_w1,
    head_w2,
    protos,
    teacher_w1,
    teacher_w2,
    teacher_protos,
):
    nd, n = lax.axis_size("dp"), lax.axis_size("proto")
    d, p = lax.axis_index("dp"), lax.axis_index("proto")
    rows, img = features.shape[0], teacher_features.shape[0] // 2
    per = rows // img
    sr, tr = rows // n, 2 * img // n
    bot = head_w2.shape[1]
    factor = 10.0 / (18 * img * nd)
    absolute = d ^ jnp.arange(nd)

    im = crop_image - d * img
    at = jnp.arange(rows, dtype=jnp.int32)
    rank = jnp.sum((im[:, None] == im[None, :]) & (at[None, :] < at[:, None]), axis=1)
    place = im * per + rank
    hit = at[:, None] == place[None, :]
    order = hit.astype(BF16)
    view = jnp.sum(jnp.where(hit, crop_view[None, :], 0), axis=1)
    views = jnp.stack(over_dp(view))[absolute]

    w1_block = lax.all_to_all(head_w1, "proto", split_axis=0, concat_axis=1, tiled=True)
    feats = over_dp(features)
    act = jnp.dot(features, head_w1, preferred_element_type=F32)
    hidden, slope = gelu_parts(act)
    zpart = jnp.dot(hidden, head_w2, preferred_element_type=F32).astype(BF16)
    zpart = jnp.dot(order, zpart, preferred_element_type=F32).astype(BF16)
    tact = jnp.dot(teacher_features, teacher_w1, preferred_element_type=F32)
    thidden, _ = gelu_parts(tact)
    tpart = jnp.dot(thidden, teacher_w2, preferred_element_type=F32).astype(BF16)
    parts = jnp.concatenate([zpart.reshape(n, sr, bot), tpart.reshape(n, tr, bot)], axis=1)
    parts = lax.all_to_all(parts, "proto", 0, 0)
    early = jnp.concatenate(
        [(slope - 0.5).astype(BF16)] + [head_w2[:, i : i + head_w1.shape[1]] for i in range(0, bot, head_w1.shape[1])],
        axis=0,
    )
    early = lax.all_gather(early, "proto")
    zrow = jnp.sum(parts.astype(F32), axis=0)
    zinv = lax.rsqrt(jnp.sum(zrow * zrow, axis=1, keepdims=True) + 1e-06)
    zn = zrow * zinv
    znb = send_all(zn.astype(BF16), "proto")
    znb = jnp.stack(over_dp(znb))[absolute]
    student = znb[:, :, :sr].reshape(nd * rows, bot)
    teacher = znb[:, :, sr:].reshape(nd * 2 * img, bot)

    cols = protos.shape[1] // nd
    pn, pinv = unit_cols(lax.dynamic_slice_in_dim(protos, d * cols, cols, 1))
    pnb = pn.astype(BF16)
    tpnb = unit_cols(lax.dynamic_slice_in_dim(teacher_protos, d * cols, cols, 1))[0].astype(BF16)

    kern = jnp.exp(jnp.dot(teacher, tpnb, preferred_element_type=F32) / 0.07)
    ex = jnp.exp(jnp.dot(student, pnb, preferred_element_type=F32) / 0.1)
    esum = jnp.sum(ex, axis=1)
    exb = ex.astype(BF16)
    sums = dot(exb, pnb, ((1,), (1,)))
    colscale = 1.0 / jnp.sum(kern, axis=0)
    for step in range(ITERS - 1):
        mass = jnp.sum(send_all(jnp.sum(kern * colscale[None, :], axis=1), ALL), axis=0)
        colscale = 1.0 / jnp.sum(kern / mass[:, None], axis=0)
    last = kern * colscale[None, :]
    lastb = last.astype(BF16)
    tsums = dot(lastb, pnb, ((1,), (1,)))
    tot = jnp.sum(send_all(jnp.concatenate([esum, jnp.sum(last, axis=1)]), ALL), axis=0)
    esum, mass = tot[: nd * rows], tot[nd * rows :]

    out = jnp.concatenate([sums.reshape(nd, n, sr, bot), tsums.reshape(nd, n, tr, bot)], axis=2)
    out = out[absolute]
    out = tree_sum([out[0]] + [swap(out[s], "dp", s) for s in range(1, nd)])
    out = jnp.sum(lax.all_to_all(out, "proto", 0, 0), axis=0)
    crop_scale = jnp.where(views == 2, 2.0, 1.0).reshape(-1) / esum * factor
    image_scale = factor / mass
    mine = (d * n + p)
    my_view = lax.dynamic_slice_in_dim(views.reshape(-1), mine * sr, sr)
    my_scale = lax.dynamic_slice_in_dim(crop_scale, mine * sr, sr)
    my_image = lax.dynamic_slice_in_dim(image_scale, mine * tr, tr)
    slot = jnp.arange(tr)
    pick = (slot[None, :] // 2 == jnp.arange(sr)[:, None] // per) & (slot[None, :] % 2 != my_view[:, None])
    target = jnp.sum(jnp.where(pick, my_image[None, :], 0.0)[:, :, None] * out[None, sr:], axis=1)
    dzn = my_scale[:, None] * out[:sr] - target
    zs, zi = zn[:sr], zinv[:sr]
    dz = (zi * (dzn - zs * jnp.sum(zs * dzn, axis=1, keepdims=True))).astype(BF16)
    dz = send_all(dz, "proto").reshape(rows, bot)
    dz = dot(order, dz, ((0,), (0,))).astype(BF16)
    dzs = over_dp(dz)

    tslot = jnp.arange(2 * img)
    picks = (tslot[None, None, :] // 2 == at[None, :, None] // per) & (tslot[None, None, :] % 2 != views[:, :, None])
    own = lax.dot_general(
        picks.astype(BF16), student.reshape(nd, rows, bot), (((1,), (1,)), ((0,), (0,))), preferred_element_type=F32
    ).reshape(nd * 2 * img, bot)
    left = (student.astype(F32) * crop_scale[:, None]).astype(BF16)
    right = (own * image_scale[:, None]).astype(BF16)
    dpn = dot(left, exb, ((0,), (0,))) - dot(right, lastb, ((0,), (0,)))
    gp = pinv * (dpn - pn * jnp.sum(pn * dpn, axis=0, keepdims=True))
    gps = over_dp(gp)
    grad_protos = jnp.zeros(protos.shape, F32)
    for s in range(nd):
        grad_protos = lax.dynamic_update_slice_in_dim(grad_protos, gps[s], (d ^ s) * cols, 1)

    w1_parts, w2_parts = [], []
    for s in range(nd):
        if s:
            hid, slp = gelu_parts(jnp.dot(feats[s], head_w1, preferred_element_type=F32))
        else:
            hid, slp = hidden, slope
        w2_parts.append(dot(hid, dzs[s], ((0,), (0,))))
        dhid = (dot(dzs[s], head_w2, ((1,), (1,))) * slp).astype(BF16)
        w1_parts.append(dot(feats[s], dhid, ((0,), (0,))))
    grad_w1, grad_w2 = tree_sum(w1_parts), tree_sum(w2_parts)
    slopes = 0.5 + early[:, :rows].astype(F32).transpose(1, 0, 2).reshape(rows, -1)
    w2_all = early[:, rows:].reshape(n, -1, head_w1.shape[1], head_w1.shape[1]).transpose(1, 3, 0, 2)
    w2_all = w2_all.reshape(bot, -1)
    dhid = (jnp.dot(dz, w2_all, preferred_element_type=F32) * slopes).astype(BF16)
    grad_features = dot(dhid, w1_block, ((1,), (1,))).astype(BF16)
    return (grad_features, grad_w1, grad_w2, grad_protos)


def params(mib=56):
    return pltpu.CompilerParams(vmem_limit_bytes=mib * 1024 * 1024)


def shape(dims, dtype):
    return jax.ShapeDtypeStruct(dims, dtype)


def kernel_name(kernel):
    return getattr(kernel, "func", kernel).__name__


def block(dims):
    return pl.BlockSpec(dims, lambda i: (0,) * len(dims))


def call(kernel, outs, scalars, *args, us=1, mib=56):
    smem = [jnp.asarray(s, jnp.int32).reshape(1) for s in scalars]
    return pl.pallas_call(
        kernel,
        grid=(1,),
        out_shape=outs,
        in_specs=[pl.BlockSpec(memory_space=pltpu.SMEM)] * len(smem) + [block(x.shape) for x in args],
        out_specs=jax.tree.map(lambda x: block(x.shape), outs),
        compiler_params=params(mib),
        name=kernel_name(kernel),
        cost_estimate=pl.CostEstimate(flops=us * 10**9, bytes_accessed=us * 10**6, transcendentals=0),
    )(*smem, *args)


def grids(dims):
    return lax.broadcasted_iota(jnp.int32, dims, 0), lax.broadcasted_iota(jnp.int32, dims, 1)


def to_row(col):
    down, along = grids((col.shape[0], col.shape[0]))
    return jnp.sum(jnp.where(down == along, col, jnp.zeros_like(col)), axis=0, keepdims=True)


def to_col(row):
    down, along = grids((row.shape[1], row.shape[1]))
    return jnp.sum(jnp.where(down == along, row, jnp.zeros_like(row)), axis=1, keepdims=True)


def head_kernel(d_ref, *refs):
    sources, im_ref, view_ref = refs[:6], refs[6], refs[7]
    parts_ref, place_ref, vs_ref, pack_ref = refs[8:12]
    held, sems = refs[12:18], refs[18]
    copies = [pltpu.make_async_copy(a, b, sems.at[k]) for k, (a, b) in enumerate(zip(sources, held))]
    for copy in copies:
        copy.start()
    f_ref, w1_ref, w2_ref, tf_ref, tw1_ref, tw2_ref = held
    rows, teach = f_ref.shape[0], tf_ref.shape[0]
    n = parts_ref.shape[0]
    img = teach // 2
    per = rows // img
    im = (im_ref[...].reshape(1, rows) - d_ref[0] * img).astype(F32)
    down, along = grids((rows, rows))
    imc = to_col(im)
    same = im == imc
    after = jnp.where(same & (down < along), 1.0, 0.0)
    row = im * per + jnp.sum(after, axis=0, keepdims=True)
    place_ref[...] = row
    hit = row.astype(jnp.int32) == down
    vs_ref[...] = jnp.sum(jnp.where(hit, view_ref[...].reshape(1, rows).astype(F32), 0.0), axis=1, keepdims=True)
    order = jnp.where(hit, 1.0, 0.0).astype(BF16)

    for copy in copies:
        copy.wait()

    deep, hs = w1_ref.shape[0] // 2, w1_ref.shape[1]
    half = hs // 2
    pack_ref[:deep] = w1_ref[pl.ds(pl.multiple_of(d_ref[0] * deep, deep), deep)]
    w2_half = w2_ref[pl.ds(pl.multiple_of(d_ref[0] * half, half), half)]
    pack_ref[deep : deep + half] = w2_half[:, :hs]
    pack_ref[deep + half :] = w2_half[:, hs:]

    def part(x, first, second):
        act = dot(x[...], first[...], ((1,), (0,)))
        hidden = (act * 0.5 * (1.0 + lax.erf(act * 0.7071067811865476))).astype(BF16)
        return dot(hidden, second[...], ((1,), (0,)))

    z = part(f_ref, w1_ref, w2_ref).astype(BF16)
    z = dot(order, z, ((1,), (0,))).reshape(n, rows // n, -1)
    t = part(tf_ref, tw1_ref, tw2_ref).reshape(n, teach // n, -1)
    parts_ref[...] = jnp.concatenate([z, t], axis=1).astype(BF16)


def rows_kernel(parts_ref, out_ref, zn_ref, zinv_ref):
    z = jnp.sum(parts_ref[...].astype(F32), axis=0)
    inv = lax.rsqrt(jnp.sum(z * z, axis=1, keepdims=True) + 1e-06)
    zn = z * inv
    zn_ref[...] = zn
    zinv_ref[...] = inv
    out_ref[...] = jnp.broadcast_to(zn[None], out_ref.shape).astype(BF16)


def row_mass(kern, mass):
    if mass is None:
        scale = 1.0 / jnp.sum(kern, axis=0, keepdims=True)
    else:
        scale = 1.0 / jnp.sum(kern * (1.0 / mass), axis=0, keepdims=True)
    return scale, jnp.sum(kern * scale, axis=1, keepdims=True)


def fold(col):
    row = to_row(col)
    return jnp.concatenate([row[:, k : k + 128] for k in range(0, row.shape[1], 128)], axis=0)


def unfold(block):
    return to_col(jnp.concatenate([block[k : k + 1] for k in range(block.shape[0])], axis=1))


def kern_kernel(d_ref, got_ref, other_ref, tpnb_ref, kern_ref, msg_ref, student_ref):
    n, slot, bot = got_ref.shape
    rows = student_ref.shape[0] // 2
    sr = rows // n
    own, other = got_ref[...].astype(F32), other_ref[...].astype(F32)
    student_ref[:rows] = own[:, :sr].reshape(rows, bot).astype(BF16)
    student_ref[rows:] = other[:, :sr].reshape(rows, bot).astype(BF16)
    own, other = own[:, sr:].reshape(-1, bot), other[:, sr:].reshape(-1, bot)
    first = d_ref[0] == 0
    teacher = jnp.concatenate([jnp.where(first, own, other), jnp.where(first, other, own)], axis=0).astype(BF16)
    kern = jnp.exp(dot(teacher, tpnb_ref[...], ((1,), (0,))) * (1.0 / 0.07))
    kern_ref[...] = kern
    _, mass = row_mass(kern, None)
    msg_ref[...] = jnp.broadcast_to(fold(mass)[None], msg_ref.shape)


def student_kernel(z_ref, pnb_ref, exb_ref, own_ref, other_ref, esum_ref):
    step = pl.program_id(0)
    ex = jnp.exp(dot(z_ref[...], pnb_ref[...], ((1,), (0,))) * 10.0)
    esum_ref[...] = jnp.sum(ex, axis=1, keepdims=True)
    exb = ex.astype(BF16)
    exb_ref[...] = exb
    sums = dot(exb, pnb_ref[...], ((1,), (1,)))

    @pl.when(step < pl.num_programs(0) // 2)
    def _():
        own_ref[...] = sums

    @pl.when(step >= pl.num_programs(0) // 2)
    def _():
        other_ref[...] = sums


def student_sums(student, pnb):
    total, bot = student.shape
    cols = pnb.shape[1]
    tile = total // 4
    return pl.pallas_call(
        student_kernel,
        name="student_kernel",
        grid=(4,),
        out_shape=(
            shape((total, cols), BF16),
            shape((total // 2, bot), F32),
            shape((total // 2, bot), F32),
            shape((total, 1), F32),
        ),
        in_specs=[pl.BlockSpec((tile, bot), lambda i: (i, 0)), pl.BlockSpec((bot, cols), lambda i: (0, 0))],
        out_specs=(
            pl.BlockSpec((tile, cols), lambda i: (i, 0)),
            pl.BlockSpec((tile, bot), lambda i: (jnp.minimum(i, 1), 0)),
            pl.BlockSpec((tile, bot), lambda i: (jnp.maximum(i - 2, 0), 0)),
            pl.BlockSpec((tile, 1), lambda i: (i, 0)),
        ),
        compiler_params=params(),
        cost_estimate=pl.CostEstimate(flops=5 * 10**9, bytes_accessed=10**7, transcendentals=0),
    )(student, pnb)


def second_kernel(d_ref, got_ref, kern_ref, esum_ref, msg_ref):
    mass = unfold(jnp.sum(got_ref[...], axis=0))
    _, mass = row_mass(kern_ref[...], mass)
    half = esum_ref.shape[0] // 2
    own, other = to_row(esum_ref[:half]), to_row(esum_ref[half:])
    first = d_ref[0] == 0
    mass = to_row(mass)
    n = msg_ref.shape[0] // 2
    for k, row in enumerate((jnp.where(first, own, other), jnp.where(first, other, own))):
        part = jnp.concatenate([mass, row], axis=1)
        msg_ref[k * n : (k + 1) * n] = jnp.broadcast_to(part[None], (n,) + part.shape)


def third_kernel(d_ref, got_ref, kern_ref, pnb_ref, esum_ref, last_ref, mine_ref, yours_ref):
    teach = kern_ref.shape[0]
    got = jnp.sum(got_ref[...], axis=0)
    esum_ref[...] = to_col(got[:, teach:])
    kern = kern_ref[...]
    scale, mass = row_mass(kern, to_col(got[:, :teach]))
    last = (kern * scale).astype(BF16)
    last_ref[...] = last
    sums = dot(last, pnb_ref[...], ((1,), (1,)))
    sums = jnp.concatenate([sums, jnp.broadcast_to(mass, (teach, 128))], axis=1)
    half = teach // 2
    first = d_ref[0] == 0
    mine_ref[...] = jnp.where(first, sums[:half], sums[half:])
    yours_ref[...] = jnp.where(first, sums[half:], sums[:half])


def message_kernel(sums_ref, b0_ref, b1_ref, out_ref):
    n = out_ref.shape[0]
    rows, bot = sums_ref.shape
    sums = sums_ref[...].astype(F32).reshape(n, rows // n, bot)
    both = b0_ref[...] + b1_ref[...]
    mass = both[:, bot:]
    high = mass.astype(BF16).astype(F32)
    tail = jnp.concatenate([high, mass - high], axis=1)
    teach = both.shape[0]
    both = both[:, :bot].reshape(n, teach // n, bot)
    out_ref[...] = jnp.concatenate([sums, both, tail.reshape(n, teach // n, bot)], axis=1).astype(BF16)


def bottleneck_kernel(factor, p_ref, got_ref, zn_ref, zinv_ref, view_ref, scale_ref, out_ref):
    sr = view_ref.shape[0] // out_ref.shape[0]
    mine = pl.ds(pl.multiple_of(p_ref[0] * sr, sr), sr)
    tr = zn_ref.shape[0] - sr
    per = sr // (tr // 2)
    out = jnp.sum(got_ref[...].astype(F32), axis=0)
    tail = out[sr + tr :]
    image = factor / (tail[:, :1] + tail[:, 128:129])
    sums = out[sr : sr + tr] * image
    zn, zinv = zn_ref[:sr], zinv_ref[:sr]
    znb = zn.astype(BF16).astype(F32)
    view = view_ref[mine].astype(jnp.int32)
    which = lax.broadcasted_iota(jnp.int32, (sr, 1), 0)
    dzn = scale_ref[mine] * out[:sr]
    own = []
    for t in range(tr):
        base = (t // 2) * per
        pick = (which >= base) & (which < base + per) & (view != t % 2)
        dzn = dzn - jnp.where(pick, sums[t : t + 1], 0.0)
        own.append(jnp.sum(jnp.where(pick, znb, 0.0), axis=0, keepdims=True) * image[t : t + 1])
    dz = zinv * (dzn - zn * jnp.sum(zn * dzn, axis=1, keepdims=True))
    both = jnp.concatenate([dz] + own, axis=0)
    out_ref[...] = jnp.broadcast_to(both[None], out_ref.shape).astype(BF16)


def hidden_kernel(f0_ref, f1_ref, w1_ref, h0_ref, h1_ref, s0_ref, s1_ref):
    for f, h, s in ((f0_ref, h0_ref, s0_ref), (f1_ref, h1_ref, s1_ref)):
        act = dot(f[...], w1_ref[...], ((1,), (0,))).T
        phi = 0.5 * (1.0 + lax.erf(act * 0.7071067811865476))
        h[...] = (act * phi).astype(BF16)
        s[...] = phi + act * jnp.exp(-0.5 * act * act) * 0.3989422804014327


def slopes_kernel(d_ref, p_ref, f_ref, own_ref, other_ref, slope_ref, w2_ref, w1_ref):
    hs = own_ref.shape[2]
    deep = f_ref.shape[1] // 2
    first = d_ref[0] == 0
    own, other = own_ref[...], other_ref[...]
    low = jnp.where(first, own, other)
    high = jnp.where(first, other, own)
    a, b = (jnp.concatenate([x[0], x[1]], axis=1) for x in (low[:, :deep], high[:, :deep]))
    act = dot(f_ref[:, :deep], a, ((1,), (0,))) + dot(f_ref[:, deep:], b, ((1,), (0,)))
    phi = 0.5 * (1.0 + lax.erf(act * 0.7071067811865476))
    slope_ref[...] = phi + act * jnp.exp(-0.5 * act * act) * 0.3989422804014327
    groups, width = w1_ref.shape[0], w1_ref.shape[1]
    blocks = deep // width
    for k in range(groups):
        chip = p_ref[0] ^ (k * NEAR)
        at = pl.multiple_of(lax.rem(chip, blocks) * width, width)
        mine = (chip // blocks) == d_ref[0]
        rows = jnp.where(mine, own_ref[:, pl.ds(at, width)], other_ref[:, pl.ds(at, width)])
        w1_ref[k] = jnp.concatenate([rows[0], rows[1]], axis=1)
    half = hs // 2
    for k in range(2):
        for part, x in ((0, low), (1, high)):
            tail = jnp.concatenate([x[k, deep : deep + half], x[k, deep + half :]], axis=1)
            w2_ref[k * hs + part * half : k * hs + (part + 1) * half] = tail


def slopes_of(d, p, features, own, other, width, groups):
    n, tall, hs = own.shape
    rows = features.shape[0]
    whole = lambda k, d, p: (0, 0)
    return pl.pallas_call(
        slopes_kernel,
        name="slopes_kernel",
        grid_spec=pltpu.PrefetchScalarGridSpec(
            num_scalar_prefetch=2,
            grid=(n // 2,),
            in_specs=[
                pl.BlockSpec(features.shape, whole),
                pl.BlockSpec((2, tall, hs), lambda k, d, p: (k, 0, 0)),
                pl.BlockSpec((2, tall, hs), lambda k, d, p: (k, 0, 0)),
            ],
            out_specs=(
                pl.BlockSpec((rows, 2 * hs), lambda k, d, p: (0, k)),
                pl.BlockSpec((2 * hs, 2 * hs), lambda k, d, p: (k, 0)),
                pl.BlockSpec((groups, width, 2 * hs), lambda k, d, p: (0, 0, k)),
            ),
        ),
        out_shape=(shape((rows, n * hs), F32), shape((n * hs, 2 * hs), BF16), shape((groups, width, n * hs), BF16)),
        compiler_params=params(),
        cost_estimate=pl.CostEstimate(flops=4 * 10**9, bytes_accessed=3 * 10**7, transcendentals=0),
    )(d.reshape(1), p.reshape(1), features, own, other)


def fetch(pairs, sems):
    copies = [pltpu.make_async_copy(x, y, sems.at[k]) for k, (x, y) in enumerate(pairs)]
    for copy in copies:
        copy.start()
    return copies


def put_back(got, place):
    n, _, bot = got.shape
    rows = place.shape[1]
    _, along = grids((rows, rows))
    back = jnp.where(to_col(place).astype(jnp.int32) == along, 1.0, 0.0).astype(BF16)
    dz = got.astype(F32)[:, : rows // n].reshape(rows, bot).astype(BF16)
    return dot(back, dz, ((1,), (0,))).astype(BF16)


def features_kernel(step, *refs):
    ins, held, sems = refs[:5], refs[-6:-1], refs[-1]
    dz_ref, own_ref, *far_refs = refs[5:-6]
    got, place, slope, w2, w1 = held
    groups, width = w1.shape[:2]
    pieces = [pl.ds(k, step) for k in range(0, slope.shape[1], step)]
    small = fetch([(ins[k], held[k]) for k in (0, 1, 4)], sems.at[pl.ds(0, 3)])
    large = []
    for k, piece in enumerate(pieces):
        pairs = [(ins[2].at[:, piece], slope.at[:, piece]), (ins[3].at[piece], w2.at[piece])]
        large.append(fetch(pairs, sems.at[pl.ds(3 + 2 * k, 2)]))
    for copy in small:
        copy.wait()
    dz = put_back(got[...], place[...])
    dz_ref[...] = dz
    total = None
    for piece, copies in zip(pieces, large):
        for copy in copies:
            copy.wait()
        dhid = (dot(dz, w2[piece], ((1,), (1,))) * slope[:, piece]).astype(BF16)
        part = dot(w1[:, :, piece].reshape(groups * width, step), dhid, ((1,), (1,)))
        total = part if total is None else total + part
    own_ref[...] = total[:width]
    for k, far_ref in enumerate(far_refs, 1):
        far_ref[...] = total[k * width : (k + 1) * width].astype(BF16)


def feature_grads(got, place, slope, w2, w1):
    args = (got, place, slope, w2, w1)
    rows, hidden = slope.shape
    bot, step = got.shape[2], 256
    groups, width = w1.shape[:2]
    outs = (shape((rows, bot), BF16), shape((width, rows), F32)) + (shape((width, rows), BF16),) * (groups - 1)
    return pl.pallas_call(
        functools.partial(features_kernel, step),
        name="features_kernel",
        grid=(1,),
        out_shape=outs,
        in_specs=[pl.BlockSpec(memory_space=pl.ANY)] * len(args),
        out_specs=tuple(block(x.shape) for x in outs),
        scratch_shapes=[pltpu.VMEM(x.shape, x.dtype) for x in args]
        + [pltpu.SemaphoreType.DMA((3 + 2 * (hidden // step),))],
        compiler_params=params(),
    )(*args)


def last_kernel(tile, d_ref, *refs):
    ins, (gp_hbm, g1_hbm, g2_hbm) = refs[:16], refs[16:19]
    held, (gp, g1, g2, sems, tile_sems, out_sems) = refs[19:35], refs[35:]
    dz0, got0, got1, place1, protos, down, dother, lown, lother, f0, f1, h0, h1, s0, s1, w2 = held
    cols = protos.shape[1] // 2
    steps = cols // tile
    rows = dz0.shape[0]
    n, slot, bot = got0.shape
    early = fetch([(ins[k], held[k]) for k in range(4)], sems)
    tiles = []
    for k in range(2 * steps):
        own = k < steps
        here = pl.multiple_of((d_ref[0] if own else 1 - d_ref[0]) * cols + (k % steps) * tile, tile)
        there = pl.ds((k % steps) * tile, tile)
        a, b = (5, 7) if own else (6, 8)
        pairs = [
            (ins[4].at[:, pl.ds(here, tile)], protos.at[:, pl.ds(here, tile)]),
            (ins[a].at[:, there], held[a].at[:, there]),
            (ins[b].at[:, there], held[b].at[:, there]),
        ]
        tiles.append((here, there, a, b, fetch(pairs, tile_sems.at[k])))
    late = fetch([(ins[k], held[k]) for k in range(9, 16)], sems.at[pl.ds(4, 7)])
    for copy in early:
        copy.wait()
    first = d_ref[0] == 0
    right0 = got0[...].astype(F32)[:, rows // n :].reshape(-1, bot)
    right1 = got1[...].astype(F32)[:, rows // n :].reshape(-1, bot)
    right = jnp.concatenate([jnp.where(first, right0, right1), jnp.where(first, right1, right0)], axis=0)
    right = right.T.astype(BF16)
    dz1 = put_back(got1[...], place1[...])
    outs = []
    for k, (here, there, a, b, copies) in enumerate(tiles):
        for copy in copies:
            copy.wait()
        mat = protos[:, pl.ds(here, tile)].astype(F32)
        inv = lax.rsqrt(jnp.sum(mat * mat, axis=0, keepdims=True) + 1e-06)
        pn = mat * inv
        dpn = held[a][:, there].astype(F32) - dot(right, held[b][:, there], ((1,), (0,)))
        gp[:, pl.ds(here, tile)] = inv * (dpn - pn * jnp.sum(pn * dpn, axis=0, keepdims=True))
        out = pltpu.make_async_copy(gp.at[:, pl.ds(here, tile)], gp_hbm.at[:, pl.ds(here, tile)], out_sems.at[k])
        out.start()
        outs.append(out)
    for copy in late:
        copy.wait()
    sums1, sums2 = [], []
    for f, dz, h, sl in ((f0, dz0[...], h0, s0), (f1, dz1, h1, s1)):
        sums2.append(dot(h[...], dz, ((1,), (0,))))
        dhid = (dot(w2[...], dz, ((1,), (1,))) * sl[...]).astype(BF16)
        sums1.append(dot(dhid, f[...], ((1,), (0,))))
    g1[...] = (sums1[0] + sums1[1]).T
    g2[...] = sums2[0] + sums2[1]
    for k, (x, y) in enumerate(((g1, g1_hbm), (g2, g2_hbm))):
        out = pltpu.make_async_copy(x, y, out_sems.at[2 * steps + k])
        out.start()
        outs.append(out)
    for out in outs:
        out.wait()


def last_grads(d, head_w1, *args):
    tile = 512
    protos, head_w2 = args[4], args[15]
    tiles = protos.shape[1] // tile
    outs = (shape(protos.shape, F32), shape(head_w1.shape, F32), shape(head_w2.shape, F32))
    anywhere = pl.BlockSpec(memory_space=pl.ANY)
    return pl.pallas_call(
        functools.partial(last_kernel, tile),
        name="last_kernel",
        out_shape=outs,
        in_specs=[pl.BlockSpec(memory_space=pltpu.SMEM)] + [anywhere] * len(args),
        out_specs=(anywhere,) * 3,
        scratch_shapes=[pltpu.VMEM(x.shape, x.dtype) for x in args + outs]
        + [
            pltpu.SemaphoreType.DMA((11,)),
            pltpu.SemaphoreType.DMA((tiles, 3)),
            pltpu.SemaphoreType.DMA((tiles + 2,)),
        ],
        compiler_params=params(),
    )(d.reshape(1), *args)


def tied(*values):
    return lax.optimization_barrier(values)


def paired_body(
    features,
    teacher_features,
    crop_image,
    crop_view,
    head_w1,
    head_w2,
    protos,
    teacher_w1,
    teacher_w2,
    teacher_protos,
):
    nd, n = lax.axis_size("dp"), lax.axis_size("proto")
    d, p = lax.axis_index("dp"), lax.axis_index("proto")
    rows, teach = features.shape[0], teacher_features.shape[0]
    sr, tr = rows // n, teach // n
    wide, hs = head_w1.shape
    bot = head_w2.shape[1]
    everyone = nd * n
    factor = 10.0 / (9 * teach * nd)

    feat_other = swap(features, "dp", 1)
    heads = (features, head_w1, head_w2, teacher_features, teacher_w1, teacher_w2)
    parts, place, view, weights = pl.pallas_call(
        head_kernel,
        grid=(1,),
        out_shape=(
            shape((n, sr + tr, bot), BF16),
            shape((1, rows), F32),
            shape((rows, 1), F32),
            shape((wide // 2 + hs, hs), BF16),
        ),
        in_specs=[pl.BlockSpec(memory_space=pltpu.SMEM)]
        + [pl.BlockSpec(memory_space=pl.ANY)] * 6
        + [block((rows,))] * 2,
        out_specs=(block((n, sr + tr, bot)), block((1, rows)), block((rows, 1)), block((wide // 2 + hs, hs))),
        scratch_shapes=[pltpu.VMEM(x.shape, x.dtype) for x in heads] + [pltpu.SemaphoreType.DMA((6,))],
        compiler_params=params(),
        name="head_kernel",
    )(d.reshape(1), *heads, crop_image, crop_view)
    weights = [weights] + [swap(weights, "proto", k) for k in range(1, NEAR)]
    parts_got = lax.all_to_all(parts, "proto", 0, 0)
    protos_late, tprotos_late, _ = tied(protos, teacher_protos, parts)
    cols = protos.shape[1] // nd
    pnb = unit_cols(lax.dynamic_slice_in_dim(protos_late, d * cols, cols, 1))[0].astype(BF16)
    tpnb = unit_cols(lax.dynamic_slice_in_dim(tprotos_late, d * cols, cols, 1))[0].astype(BF16)
    parts_got, pnb, tpnb = tied(parts_got, pnb, tpnb)

    got, zn, zinv = call(
        rows_kernel,
        (shape((n, sr + tr, bot), BF16), shape((sr + tr, bot), F32), shape((sr + tr, 1), F32)),
        [],
        parts_got,
    )
    sent = got
    got = lax.all_to_all(got, "proto", 0, 0)
    w1_late, feat_late, feat_other_late, weights, _ = tied(head_w1, features, feat_other, weights, sent)
    h0, h1, s0, s1 = call(
        hidden_kernel,
        (shape((hs, rows), BF16),) * 2 + (shape((hs, rows), F32),) * 2,
        [],
        feat_late, feat_other_late, w1_late,
        us=4,
    )
    weights = jnp.stack(weights)
    got, h0, h1, s0, s1, weights = tied(got, h0, h1, s0, s1, weights)
    got_other = swap(got, "dp", 1)
    kern, msg, student = call(
        kern_kernel,
        (shape((nd * teach, cols), F32), shape((everyone, nd * teach // 128, 128), F32), shape((nd * rows, bot), BF16)),
        [d],
        got, got_other, tpnb,
        us=3,
    )
    msg_got = lax.all_to_all(msg, ALL, 0, 0)
    student, _ = tied(student, msg)
    exb, sums, sums_other, esum = student_sums(student, pnb)
    msg = call(
        second_kernel,
        shape((everyone, 1, nd * teach + rows), F32),
        [d],
        msg_got, kern, esum,
    )
    msg_got = lax.all_to_all(msg, ALL, 0, 0)
    sums, sums_other, _ = tied(sums, sums_other, msg)
    sums_other = swap(sums_other, "dp", 1)
    sums = (sums + sums_other).astype(BF16)
    msg_got, sums = tied(msg_got, sums)
    esum, last, mine, yours = call(
        third_kernel,
        (
            shape((rows, 1), F32),
            shape((nd * teach, cols), BF16),
            shape((teach, bot + 128), F32),
            shape((teach, bot + 128), F32),
        ),
        [d],
        msg_got, kern, pnb,
        us=2,
    )
    yours = swap(yours, "dp", 1)
    msg = call(message_kernel, shape((n, sr + 2 * tr, bot), BF16), [], sums, mine, yours)
    msg_got = lax.all_to_all(msg, "proto", 0, 0)

    esum, view_late, last, weights, place, _ = tied(esum, view, last, weights, place, msg)
    weights_other, last_other = swap(weights, "dp", 1), swap(last, "dp", 1)
    place_other = swap(place, "dp", 1)
    crop_scale = jnp.where(view_late == 2, 2.0, 1.0) * factor / esum
    scale_other = swap(crop_scale, "dp", 1)
    left = (student.astype(F32) * jnp.concatenate([crop_scale, scale_other], axis=0)).astype(BF16)
    dpn = dot(left, exb, ((0,), (0,))).astype(BF16)
    msg_got, dpn = tied(msg_got, dpn)
    dpn_other = swap(dpn, "dp", 1)
    dz = call(
        functools.partial(bottleneck_kernel, factor),
        shape((n, sr + tr, bot), BF16),
        [p],
        msg_got, zn, zinv, view_late, crop_scale,
    )
    got = lax.all_to_all(dz, "proto", 0, 0)
    weights, feat_late, _ = tied(weights, features, dz)
    slopes = slopes_of(d, p, feat_late, weights, weights_other, wide // n, n // NEAR)
    got, slopes = tied(got, slopes)

    got_other = swap(got, "dp", 1)
    dz, grad_features, *far = feature_grads(got, place, *slopes)
    far = [swap(x, "proto", k * NEAR) for k, x in enumerate(far, 1)]
    grad_protos, grad_w1, grad_w2 = last_grads(
        d, head_w1, dz, got, got_other, place_other, protos, dpn, dpn_other, last, last_other,
        features, feat_other, h0, h1, s0, s1, head_w2,
    )
    grad_protos, *far = tied(grad_protos, *far)
    grad_features = (grad_features + sum(x.astype(F32) for x in far)).astype(BF16).T
    return (grad_features, grad_w1, grad_w2, grad_protos)


def body(features, teacher_features, *rest):
    n = lax.axis_size("proto")
    slot = (features.shape[0] // n, teacher_features.shape[0] // n)
    paired = lax.axis_size("dp") == 2 and n == 4 * NEAR and slot[0] % 8 == 0 and slot[1] % 8 == 0
    paired = paired and features.shape[0] % teacher_features.shape[0] == 0
    return (paired_body if paired else general_body)(features, teacher_features, *rest)


def solution(mesh):
    in_specs = (
        P("dp", None),
        P("dp", None),
        P("dp"),
        P("dp"),
        P(None, "proto"),
        P("proto", None),
        P(None, "proto"),
        P(None, "proto"),
        P("proto", None),
        P(None, "proto"),
    )
    out_specs = (P("dp", "proto"), P(None, "proto"), P("proto", None), P(None, "proto"))
    return jax.shard_map(body, mesh=mesh, in_specs=in_specs, out_specs=out_specs, check_vma=False)
```

```python
import functools

import jax
import jax.numpy as jnp
from jax import lax
from jax.experimental import pallas as pl
from jax.experimental.pallas import tpu as pltpu
from jax.sharding import PartitionSpec as P

ITERS = 3
ALL = ("dp", "proto")
NEAR = 4
F32 = jnp.float32
BF16 = jnp.bfloat16


def gelu_parts(act):
    phi = 0.5 * (1.0 + lax.erf(act * 0.7071067811865476))
    slope = phi + act * jnp.exp(-0.5 * act * act) * 0.3989422804014327
    return (act * phi).astype(BF16), slope


def dot(a, b, dims):
    return lax.dot_general(a, b, (dims, ((), ())), preferred_element_type=F32)


def swap(value, axis, step):
    count = lax.axis_size(axis)
    return lax.ppermute(value, axis, [(i, i ^ step) for i in range(count)])


def over_dp(value):
    return [value] + [swap(value, "dp", s) for s in range(1, lax.axis_size("dp"))]


def tree_sum(parts):
    while len(parts) > 1:
        parts = [parts[i] + parts[i + 1] for i in range(0, len(parts), 2)]
    return parts[0]


def send_all(value, axes):
    count = lax.axis_size(axes)
    return lax.all_to_all(jnp.broadcast_to(value[None], (count,) + value.shape), axes, 0, 0)


def unit_cols(mat):
    matf = mat.astype(F32)
    inv = lax.rsqrt(jnp.sum(matf * matf, axis=0, keepdims=True) + 1e-06)
    return matf * inv, inv


def general_body(
    features,
    teacher_features,
    crop_image,
    crop_view,
    head_w1,
    head_w2,
    protos,
    teacher_w1,
    teacher_w2,
    teacher_protos,
):
    nd, n = lax.axis_size("dp"), lax.axis_size("proto")
    d, p = lax.axis_index("dp"), lax.axis_index("proto")
    rows, img = features.shape[0], teacher_features.shape[0] // 2
    per = rows // img
    sr, tr = rows // n, 2 * img // n
    bot = head_w2.shape[1]
    factor = 10.0 / (18 * img * nd)
    absolute = d ^ jnp.arange(nd)

    im = crop_image - d * img
    at = jnp.arange(rows, dtype=jnp.int32)
    rank = jnp.sum((im[:, None] == im[None, :]) & (at[None, :] < at[:, None]), axis=1)
    place = im * per + rank
    hit = at[:, None] == place[None, :]
    order = hit.astype(BF16)
    view = jnp.sum(jnp.where(hit, crop_view[None, :], 0), axis=1)
    views = jnp.stack(over_dp(view))[absolute]

    w1_block = lax.all_to_all(head_w1, "proto", split_axis=0, concat_axis=1, tiled=True)
    feats = over_dp(features)
    act = jnp.dot(features, head_w1, preferred_element_type=F32)
    hidden, slope = gelu_parts(act)
    zpart = jnp.dot(hidden, head_w2, preferred_element_type=F32).astype(BF16)
    zpart = jnp.dot(order, zpart, preferred_element_type=F32).astype(BF16)
    tact = jnp.dot(teacher_features, teacher_w1, preferred_element_type=F32)
    thidden, _ = gelu_parts(tact)
    tpart = jnp.dot(thidden, teacher_w2, preferred_element_type=F32).astype(BF16)
    parts = jnp.concatenate([zpart.reshape(n, sr, bot), tpart.reshape(n, tr, bot)], axis=1)
    parts = lax.all_to_all(parts, "proto", 0, 0)
    early = jnp.concatenate(
        [(slope - 0.5).astype(BF16)] + [head_w2[:, i : i + head_w1.shape[1]] for i in range(0, bot, head_w1.shape[1])],
        axis=0,
    )
    early = lax.all_gather(early, "proto")
    zrow = jnp.sum(parts.astype(F32), axis=0)
    zinv = lax.rsqrt(jnp.sum(zrow * zrow, axis=1, keepdims=True) + 1e-06)
    zn = zrow * zinv
    znb = send_all(zn.astype(BF16), "proto")
    znb = jnp.stack(over_dp(znb))[absolute]
    student = znb[:, :, :sr].reshape(nd * rows, bot)
    teacher = znb[:, :, sr:].reshape(nd * 2 * img, bot)

    cols = protos.shape[1] // nd
    pn, pinv = unit_cols(lax.dynamic_slice_in_dim(protos, d * cols, cols, 1))
    pnb = pn.astype(BF16)
    tpnb = unit_cols(lax.dynamic_slice_in_dim(teacher_protos, d * cols, cols, 1))[0].astype(BF16)

    kern = jnp.exp(jnp.dot(teacher, tpnb, preferred_element_type=F32) / 0.07)
    ex = jnp.exp(jnp.dot(student, pnb, preferred_element_type=F32) / 0.1)
    esum = jnp.sum(ex, axis=1)
    exb = ex.astype(BF16)
    sums = dot(exb, pnb, ((1,), (1,)))
    colscale = 1.0 / jnp.sum(kern, axis=0)
    for step in range(ITERS - 1):
        mass = jnp.sum(send_all(jnp.sum(kern * colscale[None, :], axis=1), ALL), axis=0)
        colscale = 1.0 / jnp.sum(kern / mass[:, None], axis=0)
    last = kern * colscale[None, :]
    lastb = last.astype(BF16)
    tsums = dot(lastb, pnb, ((1,), (1,)))
    tot = jnp.sum(send_all(jnp.concatenate([esum, jnp.sum(last, axis=1)]), ALL), axis=0)
    esum, mass = tot[: nd * rows], tot[nd * rows :]

    out = jnp.concatenate([sums.reshape(nd, n, sr, bot), tsums.reshape(nd, n, tr, bot)], axis=2)
    out = out[absolute]
    out = tree_sum([out[0]] + [swap(out[s], "dp", s) for s in range(1, nd)])
    out = jnp.sum(lax.all_to_all(out, "proto", 0, 0), axis=0)
    crop_scale = jnp.where(views == 2, 2.0, 1.0).reshape(-1) / esum * factor
    image_scale = factor / mass
    mine = (d * n + p)
    my_view = lax.dynamic_slice_in_dim(views.reshape(-1), mine * sr, sr)
    my_scale = lax.dynamic_slice_in_dim(crop_scale, mine * sr, sr)
    my_image = lax.dynamic_slice_in_dim(image_scale, mine * tr, tr)
    slot = jnp.arange(tr)
    pick = (slot[None, :] // 2 == jnp.arange(sr)[:, None] // per) & (slot[None, :] % 2 != my_view[:, None])
    target = jnp.sum(jnp.where(pick, my_image[None, :], 0.0)[:, :, None] * out[None, sr:], axis=1)
    dzn = my_scale[:, None] * out[:sr] - target
    zs, zi = zn[:sr], zinv[:sr]
    dz = (zi * (dzn - zs * jnp.sum(zs * dzn, axis=1, keepdims=True))).astype(BF16)
    dz = send_all(dz, "proto").reshape(rows, bot)
    dz = dot(order, dz, ((0,), (0,))).astype(BF16)
    dzs = over_dp(dz)

    tslot = jnp.arange(2 * img)
    picks = (tslot[None, None, :] // 2 == at[None, :, None] // per) & (tslot[None, None, :] % 2 != views[:, :, None])
    own = lax.dot_general(
        picks.astype(BF16), student.reshape(nd, rows, bot), (((1,), (1,)), ((0,), (0,))), preferred_element_type=F32
    ).reshape(nd * 2 * img, bot)
    left = (student.astype(F32) * crop_scale[:, None]).astype(BF16)
    right = (own * image_scale[:, None]).astype(BF16)
    dpn = dot(left, exb, ((0,), (0,))) - dot(right, lastb, ((0,), (0,)))
    gp = pinv * (dpn - pn * jnp.sum(pn * dpn, axis=0, keepdims=True))
    gps = over_dp(gp)
    grad_protos = jnp.zeros(protos.shape, F32)
    for s in range(nd):
        grad_protos = lax.dynamic_update_slice_in_dim(grad_protos, gps[s], (d ^ s) * cols, 1)

    w1_parts, w2_parts = [], []
    for s in range(nd):
        if s:
            hid, slp = gelu_parts(jnp.dot(feats[s], head_w1, preferred_element_type=F32))
        else:
            hid, slp = hidden, slope
        w2_parts.append(dot(hid, dzs[s], ((0,), (0,))))
        dhid = (dot(dzs[s], head_w2, ((1,), (1,))) * slp).astype(BF16)
        w1_parts.append(dot(feats[s], dhid, ((0,), (0,))))
    grad_w1, grad_w2 = tree_sum(w1_parts), tree_sum(w2_parts)
    slopes = 0.5 + early[:, :rows].astype(F32).transpose(1, 0, 2).reshape(rows, -1)
    w2_all = early[:, rows:].reshape(n, -1, head_w1.shape[1], head_w1.shape[1]).transpose(1, 3, 0, 2)
    w2_all = w2_all.reshape(bot, -1)
    dhid = (jnp.dot(dz, w2_all, preferred_element_type=F32) * slopes).astype(BF16)
    grad_features = dot(dhid, w1_block, ((1,), (1,))).astype(BF16)
    return (grad_features, grad_w1, grad_w2, grad_protos)


def params(mib=50):
    return pltpu.CompilerParams(vmem_limit_bytes=mib * 1024 * 1024)


def shape(dims, dtype):
    return jax.ShapeDtypeStruct(dims, dtype)


def kernel_name(kernel):
    return getattr(kernel, "func", kernel).__name__


def block(dims):
    return pl.BlockSpec(dims, lambda i: (0,) * len(dims))


def call(kernel, outs, scalars, *args, us=1, mib=50):
    smem = [jnp.asarray(s, jnp.int32).reshape(1) for s in scalars]
    return pl.pallas_call(
        kernel,
        grid=(1,),
        out_shape=outs,
        in_specs=[pl.BlockSpec(memory_space=pltpu.SMEM)] * len(smem) + [block(x.shape) for x in args],
        out_specs=jax.tree.map(lambda x: block(x.shape), outs),
        compiler_params=params(mib),
        name=kernel_name(kernel),
        cost_estimate=pl.CostEstimate(flops=us * 10**9, bytes_accessed=us * 10**6, transcendentals=0),
    )(*smem, *args)


def grids(dims):
    return lax.broadcasted_iota(jnp.int32, dims, 0), lax.broadcasted_iota(jnp.int32, dims, 1)


def to_row(col):
    down, along = grids((col.shape[0], col.shape[0]))
    return jnp.sum(jnp.where(down == along, col, jnp.zeros_like(col)), axis=0, keepdims=True)


def to_col(row):
    down, along = grids((row.shape[1], row.shape[1]))
    return jnp.sum(jnp.where(down == along, row, jnp.zeros_like(row)), axis=1, keepdims=True)


def head_kernel(d_ref, *refs):
    sources, im_ref, view_ref = refs[:6], refs[6], refs[7]
    parts_ref, place_ref, vs_ref, pack_ref = refs[8:12]
    held, sems = refs[12:18], refs[18]
    copies = [pltpu.make_async_copy(a, b, sems.at[k]) for k, (a, b) in enumerate(zip(sources, held))]
    for copy in copies:
        copy.start()
    f_ref, w1_ref, w2_ref, tf_ref, tw1_ref, tw2_ref = held
    rows, teach = f_ref.shape[0], tf_ref.shape[0]
    n = parts_ref.shape[0]
    img = teach // 2
    per = rows // img
    im = (im_ref[...].reshape(1, rows) - d_ref[0] * img).astype(F32)
    down, along = grids((rows, rows))
    imc = to_col(im)
    same = im == imc
    after = jnp.where(same & (down < along), 1.0, 0.0)
    row = im * per + jnp.sum(after, axis=0, keepdims=True)
    place_ref[...] = row
    hit = row.astype(jnp.int32) == down
    vs_ref[...] = jnp.sum(jnp.where(hit, view_ref[...].reshape(1, rows).astype(F32), 0.0), axis=1, keepdims=True)
    order = jnp.where(hit, 1.0, 0.0).astype(BF16)

    for copy in copies:
        copy.wait()

    deep, hs = w1_ref.shape[0] // 2, w1_ref.shape[1]
    half = hs // 2
    pack_ref[:deep] = w1_ref[pl.ds(pl.multiple_of(d_ref[0] * deep, deep), deep)]
    w2_half = w2_ref[pl.ds(pl.multiple_of(d_ref[0] * half, half), half)]
    pack_ref[deep : deep + half] = w2_half[:, :hs]
    pack_ref[deep + half :] = w2_half[:, hs:]

    def part(x, first, second):
        act = dot(x[...], first[...], ((1,), (0,)))
        hidden = (act * 0.5 * (1.0 + lax.erf(act * 0.7071067811865476))).astype(BF16)
        return dot(hidden, second[...], ((1,), (0,)))

    z = part(f_ref, w1_ref, w2_ref).astype(BF16)
    z = dot(order, z, ((1,), (0,))).reshape(n, rows // n, -1)
    t = part(tf_ref, tw1_ref, tw2_ref).reshape(n, teach // n, -1)
    parts_ref[...] = jnp.concatenate([z, t], axis=1).astype(BF16)


def rows_kernel(parts_ref, out_ref, zn_ref):
    z = jnp.sum(parts_ref[...].astype(F32), axis=0)
    inv = lax.rsqrt(jnp.sum(z * z, axis=1, keepdims=True) + 1e-06)
    zn = z * inv
    zn_ref[...] = jnp.concatenate([zn, jnp.broadcast_to(inv, (zn.shape[0], 128))], axis=1)
    out_ref[...] = jnp.broadcast_to(zn[None], out_ref.shape).astype(BF16)


def row_mass(kern, mass):
    if mass is None:
        scale = 1.0 / jnp.sum(kern, axis=0, keepdims=True)
    else:
        scale = 1.0 / jnp.sum(kern * (1.0 / mass), axis=0, keepdims=True)
    return scale, jnp.sum(kern * scale, axis=1, keepdims=True)


def fold(col):
    row = to_row(col)
    return jnp.concatenate([row[:, k : k + 128] for k in range(0, row.shape[1], 128)], axis=0)


def unfold(block):
    return to_col(jnp.concatenate([block[k : k + 1] for k in range(block.shape[0])], axis=1))


def kern_kernel(d_ref, got_ref, other_ref, tpnb_ref, kern_ref, msg_ref, student_ref):
    n, slot, bot = got_ref.shape
    rows = student_ref.shape[0] // 2
    sr = rows // n
    own, other = got_ref[...].astype(F32), other_ref[...].astype(F32)
    student_ref[:rows] = own[:, :sr].reshape(rows, bot).astype(BF16)
    student_ref[rows:] = other[:, :sr].reshape(rows, bot).astype(BF16)
    own, other = own[:, sr:].reshape(-1, bot), other[:, sr:].reshape(-1, bot)
    first = d_ref[0] == 0
    teacher = jnp.concatenate([jnp.where(first, own, other), jnp.where(first, other, own)], axis=0).astype(BF16)
    kern = jnp.exp(dot(teacher, tpnb_ref[...], ((1,), (0,))) * (1.0 / 0.07))
    kern_ref[...] = kern
    _, mass = row_mass(kern, None)
    msg_ref[...] = jnp.broadcast_to(fold(mass)[None], msg_ref.shape)


def student_kernel(z_ref, pnb_ref, exb_ref, own_ref, other_ref, esum_ref):
    step = pl.program_id(0)
    ex = jnp.exp(dot(z_ref[...], pnb_ref[...], ((1,), (0,))) * 10.0)
    esum_ref[...] = jnp.sum(ex, axis=1, keepdims=True)
    exb = ex.astype(BF16)
    exb_ref[...] = exb
    sums = dot(exb, pnb_ref[...], ((1,), (1,)))

    @pl.when(step < pl.num_programs(0) // 2)
    def _():
        own_ref[...] = sums

    @pl.when(step >= pl.num_programs(0) // 2)
    def _():
        other_ref[...] = sums


def student_sums(student, pnb):
    total, bot = student.shape
    cols = pnb.shape[1]
    tile = total // 4
    return pl.pallas_call(
        student_kernel,
        name="student_kernel",
        grid=(4,),
        out_shape=(
            shape((total, cols), BF16),
            shape((total // 2, bot), F32),
            shape((total // 2, bot), F32),
            shape((total, 1), F32),
        ),
        in_specs=[pl.BlockSpec((tile, bot), lambda i: (i, 0)), pl.BlockSpec((bot, cols), lambda i: (0, 0))],
        out_specs=(
            pl.BlockSpec((tile, cols), lambda i: (i, 0)),
            pl.BlockSpec((tile, bot), lambda i: (jnp.minimum(i, 1), 0)),
            pl.BlockSpec((tile, bot), lambda i: (jnp.maximum(i - 2, 0), 0)),
            pl.BlockSpec((tile, 1), lambda i: (i, 0)),
        ),
        compiler_params=params(),
        cost_estimate=pl.CostEstimate(flops=5 * 10**9, bytes_accessed=10**7, transcendentals=0),
    )(student, pnb)


def second_kernel(d_ref, got_ref, kern_ref, esum_ref, msg_ref):
    mass = unfold(jnp.sum(got_ref[...], axis=0))
    _, mass = row_mass(kern_ref[...], mass)
    half = esum_ref.shape[0] // 2
    own, other = to_row(esum_ref[:half]), to_row(esum_ref[half:])
    first = d_ref[0] == 0
    mass = to_row(mass)
    n = msg_ref.shape[0] // 2
    for k, row in enumerate((jnp.where(first, own, other), jnp.where(first, other, own))):
        part = jnp.concatenate([mass, row], axis=1)
        msg_ref[k * n : (k + 1) * n] = jnp.broadcast_to(part[None], (n,) + part.shape)


def third_kernel(d_ref, got_ref, kern_ref, pnb_ref, esum_ref, last_ref, mine_ref, yours_ref):
    teach = kern_ref.shape[0]
    got = jnp.sum(got_ref[...], axis=0)
    esum_ref[...] = to_col(got[:, teach:])
    kern = kern_ref[...]
    scale, mass = row_mass(kern, to_col(got[:, :teach]))
    last = (kern * scale).astype(BF16)
    last_ref[...] = last
    sums = dot(last, pnb_ref[...], ((1,), (1,)))
    sums = jnp.concatenate([sums, jnp.broadcast_to(mass, (teach, 128))], axis=1)
    half = teach // 2
    first = d_ref[0] == 0
    mine_ref[...] = jnp.where(first, sums[:half], sums[half:])
    yours_ref[...] = jnp.where(first, sums[half:], sums[:half])


def message_kernel(sums_ref, b0_ref, b1_ref, out_ref):
    n = out_ref.shape[0]
    rows, bot = sums_ref.shape
    sums = sums_ref[...].astype(F32).reshape(n, rows // n, bot)
    both = b0_ref[...] + b1_ref[...]
    mass = both[:, bot:]
    high = mass.astype(BF16).astype(F32)
    tail = jnp.concatenate([high, mass - high], axis=1)
    teach = both.shape[0]
    both = both[:, :bot].reshape(n, teach // n, bot)
    out_ref[...] = jnp.concatenate([sums, both, tail.reshape(n, teach // n, bot)], axis=1).astype(BF16)


def bottleneck_kernel(factor, p_ref, got_ref, zn_ref, view_ref, scale_ref, out_ref):
    sr = view_ref.shape[0] // out_ref.shape[0]
    mine = pl.ds(pl.multiple_of(p_ref[0] * sr, sr), sr)
    tr = zn_ref.shape[0] - sr
    per = sr // (tr // 2)
    out = jnp.sum(got_ref[...].astype(F32), axis=0)
    tail = out[sr + tr :]
    image = factor / (tail[:, :1] + tail[:, 128:129])
    sums = out[sr : sr + tr] * image
    bot = got_ref.shape[2]
    zn, zinv = zn_ref[:sr, :bot], zn_ref[:sr, bot : bot + 1]
    znb = zn.astype(BF16).astype(F32)
    view = view_ref[mine].astype(jnp.int32)
    which = lax.broadcasted_iota(jnp.int32, (sr, 1), 0)
    dzn = scale_ref[mine] * out[:sr]
    own = []
    for t in range(tr):
        base = (t // 2) * per
        pick = (which >= base) & (which < base + per) & (view != t % 2)
        dzn = dzn - jnp.where(pick, sums[t : t + 1], 0.0)
        own.append(jnp.sum(jnp.where(pick, znb, 0.0), axis=0, keepdims=True) * image[t : t + 1])
    dz = zinv * (dzn - zn * jnp.sum(zn * dzn, axis=1, keepdims=True))
    both = jnp.concatenate([dz] + own, axis=0)
    out_ref[...] = jnp.broadcast_to(both[None], out_ref.shape).astype(BF16)


def hidden_kernel(f0_ref, f1_ref, w1_ref, h0_ref, h1_ref, s0_ref, s1_ref):
    for f, h, s in ((f0_ref, h0_ref, s0_ref), (f1_ref, h1_ref, s1_ref)):
        act = dot(f[...], w1_ref[...], ((1,), (0,))).T
        phi = 0.5 * (1.0 + lax.erf(act * 0.7071067811865476))
        h[...] = (act * phi).astype(BF16)
        s[...] = phi + act * jnp.exp(-0.5 * act * act) * 0.3989422804014327


def slopes_kernel(d_ref, p_ref, f_ref, own_ref, other_ref, slope_ref, w2_ref, w1_ref):
    hs = own_ref.shape[2]
    deep = f_ref.shape[1] // 2
    first = d_ref[0] == 0
    own, other = own_ref[...], other_ref[...]
    low = jnp.where(first, own, other)
    high = jnp.where(first, other, own)
    a, b = (jnp.concatenate([x[0], x[1]], axis=1) for x in (low[:, :deep], high[:, :deep]))
    act = dot(f_ref[:, :deep], a, ((1,), (0,))) + dot(f_ref[:, deep:], b, ((1,), (0,)))
    phi = 0.5 * (1.0 + lax.erf(act * 0.7071067811865476))
    slope_ref[...] = phi + act * jnp.exp(-0.5 * act * act) * 0.3989422804014327
    groups, width = w1_ref.shape[0], w1_ref.shape[1]
    blocks = deep // width
    for k in range(groups):
        chip = p_ref[0] ^ (k * NEAR)
        at = pl.multiple_of(lax.rem(chip, blocks) * width, width)
        mine = (chip // blocks) == d_ref[0]
        rows = jnp.where(mine, own_ref[:, pl.ds(at, width)], other_ref[:, pl.ds(at, width)])
        w1_ref[k] = jnp.concatenate([rows[0], rows[1]], axis=1)
    half = hs // 2
    for k in range(2):
        for part, x in ((0, low), (1, high)):
            tail = jnp.concatenate([x[k, deep : deep + half], x[k, deep + half :]], axis=1)
            w2_ref[k * hs + part * half : k * hs + (part + 1) * half] = tail


def slopes_of(d, p, features, own, other, width, groups):
    n, tall, hs = own.shape
    rows = features.shape[0]
    whole = lambda k, d, p: (0, 0)
    return pl.pallas_call(
        slopes_kernel,
        name="slopes_kernel",
        grid_spec=pltpu.PrefetchScalarGridSpec(
            num_scalar_prefetch=2,
            grid=(n // 2,),
            in_specs=[
                pl.BlockSpec(features.shape, whole),
                pl.BlockSpec((2, tall, hs), lambda k, d, p: (k, 0, 0)),
                pl.BlockSpec((2, tall, hs), lambda k, d, p: (k, 0, 0)),
            ],
            out_specs=(
                pl.BlockSpec((rows, 2 * hs), lambda k, d, p: (0, k)),
                pl.BlockSpec((2 * hs, 2 * hs), lambda k, d, p: (k, 0)),
                pl.BlockSpec((groups, width, 2 * hs), lambda k, d, p: (0, 0, k)),
            ),
        ),
        out_shape=(shape((rows, n * hs), F32), shape((n * hs, 2 * hs), BF16), shape((groups, width, n * hs), BF16)),
        compiler_params=params(),
        cost_estimate=pl.CostEstimate(flops=4 * 10**9, bytes_accessed=3 * 10**7, transcendentals=0),
    )(d.reshape(1), p.reshape(1), features, own, other)


def fetch(pairs, sems):
    copies = [pltpu.make_async_copy(x, y, sems.at[k]) for k, (x, y) in enumerate(pairs)]
    for copy in copies:
        copy.start()
    return copies


def put_back(got, place):
    n, _, bot = got.shape
    rows = place.shape[1]
    _, along = grids((rows, rows))
    back = jnp.where(to_col(place).astype(jnp.int32) == along, 1.0, 0.0).astype(BF16)
    dz = got.astype(F32)[:, : rows // n].reshape(rows, bot).astype(BF16)
    return dot(back, dz, ((1,), (0,))).astype(BF16)


def features_kernel(step, *refs):
    ins, held, sems = refs[:5], refs[-6:-1], refs[-1]
    dz_ref, own_ref, *far_refs = refs[5:-6]
    got, place, slope, w2, w1 = held
    groups, width = w1.shape[:2]
    pieces = [pl.ds(k, step) for k in range(0, slope.shape[1], step)]
    small = fetch([(ins[k], held[k]) for k in (0, 1, 4)], sems.at[pl.ds(0, 3)])
    large = []
    for k, piece in enumerate(pieces):
        pairs = [(ins[2].at[:, piece], slope.at[:, piece]), (ins[3].at[piece], w2.at[piece])]
        large.append(fetch(pairs, sems.at[pl.ds(3 + 2 * k, 2)]))
    for copy in small:
        copy.wait()
    dz = put_back(got[...], place[...])
    dz_ref[...] = dz
    total = None
    for piece, copies in zip(pieces, large):
        for copy in copies:
            copy.wait()
        dhid = (dot(dz, w2[piece], ((1,), (1,))) * slope[:, piece]).astype(BF16)
        part = dot(w1[:, :, piece].reshape(groups * width, step), dhid, ((1,), (1,)))
        total = part if total is None else total + part
    own_ref[...] = total[:width]
    for k, far_ref in enumerate(far_refs, 1):
        far_ref[...] = total[k * width : (k + 1) * width].astype(BF16)


def feature_grads(got, place, slope, w2, w1):
    args = (got, place, slope, w2, w1)
    rows, hidden = slope.shape
    bot, step = got.shape[2], 256
    groups, width = w1.shape[:2]
    outs = (shape((rows, bot), BF16), shape((width, rows), F32)) + (shape((width, rows), BF16),) * (groups - 1)
    return pl.pallas_call(
        functools.partial(features_kernel, step),
        name="features_kernel",
        grid=(1,),
        out_shape=outs,
        in_specs=[pl.BlockSpec(memory_space=pl.ANY)] * len(args),
        out_specs=tuple(block(x.shape) for x in outs),
        scratch_shapes=[pltpu.VMEM(x.shape, x.dtype) for x in args]
        + [pltpu.SemaphoreType.DMA((3 + 2 * (hidden // step),))],
        compiler_params=params(),
    )(*args)


def last_kernel(tile, d_ref, *refs):
    ins, (gp_hbm, g1_hbm, g2_hbm) = refs[:16], refs[16:19]
    held, (gp, g1, g2, sems, tile_sems, out_sems) = refs[19:35], refs[35:]
    dz0, got0, got1, place1, protos, down, dother, lown, lother, f0, f1, h0, h1, s0, s1, w2 = held
    cols = protos.shape[1] // 2
    steps = cols // tile
    rows = dz0.shape[0]
    n, slot, bot = got0.shape
    early = fetch([(ins[k], held[k]) for k in range(4)], sems)
    tiles = []
    for k in range(2 * steps):
        own = k < steps
        here = pl.multiple_of((d_ref[0] if own else 1 - d_ref[0]) * cols + (k % steps) * tile, tile)
        there = pl.ds((k % steps) * tile, tile)
        a, b = (5, 7) if own else (6, 8)
        pairs = [
            (ins[4].at[:, pl.ds(here, tile)], protos.at[:, pl.ds(here, tile)]),
            (ins[a].at[:, there], held[a].at[:, there]),
            (ins[b].at[:, there], held[b].at[:, there]),
        ]
        tiles.append((here, there, a, b, fetch(pairs, tile_sems.at[k])))
    late = fetch([(ins[k], held[k]) for k in range(9, 16)], sems.at[pl.ds(4, 7)])
    for copy in early:
        copy.wait()
    first = d_ref[0] == 0
    right0 = got0[...].astype(F32)[:, rows // n :].reshape(-1, bot)
    right1 = got1[...].astype(F32)[:, rows // n :].reshape(-1, bot)
    right = jnp.concatenate([jnp.where(first, right0, right1), jnp.where(first, right1, right0)], axis=0)
    right = right.T.astype(BF16)
    dz1 = put_back(got1[...], place1[...])
    outs = []
    for k, (here, there, a, b, copies) in enumerate(tiles):
        for copy in copies:
            copy.wait()
        mat = protos[:, pl.ds(here, tile)].astype(F32)
        inv = lax.rsqrt(jnp.sum(mat * mat, axis=0, keepdims=True) + 1e-06)
        pn = mat * inv
        dpn = held[a][:, there].astype(F32) - dot(right, held[b][:, there], ((1,), (0,)))
        gp[:, pl.ds(here, tile)] = inv * (dpn - pn * jnp.sum(pn * dpn, axis=0, keepdims=True))
        out = pltpu.make_async_copy(gp.at[:, pl.ds(here, tile)], gp_hbm.at[:, pl.ds(here, tile)], out_sems.at[k])
        out.start()
        outs.append(out)
    for copy in late:
        copy.wait()
    sums1, sums2 = [], []
    for f, dz, h, sl in ((f0, dz0[...], h0, s0), (f1, dz1, h1, s1)):
        sums2.append(dot(h[...], dz, ((1,), (0,))))
        dhid = (dot(w2[...], dz, ((1,), (1,))) * sl[...]).astype(BF16)
        sums1.append(dot(dhid, f[...], ((1,), (0,))))
    g1[...] = (sums1[0] + sums1[1]).T
    g2[...] = sums2[0] + sums2[1]
    for k, (x, y) in enumerate(((g1, g1_hbm), (g2, g2_hbm))):
        out = pltpu.make_async_copy(x, y, out_sems.at[2 * steps + k])
        out.start()
        outs.append(out)
    for out in outs:
        out.wait()


def last_grads(d, head_w1, *args):
    tile = 512
    protos, head_w2 = args[4], args[15]
    tiles = protos.shape[1] // tile
    outs = (shape(protos.shape, F32), shape(head_w1.shape, F32), shape(head_w2.shape, F32))
    anywhere = pl.BlockSpec(memory_space=pl.ANY)
    return pl.pallas_call(
        functools.partial(last_kernel, tile),
        name="last_kernel",
        out_shape=outs,
        in_specs=[pl.BlockSpec(memory_space=pltpu.SMEM)] + [anywhere] * len(args),
        out_specs=(anywhere,) * 3,
        scratch_shapes=[pltpu.VMEM(x.shape, x.dtype) for x in args + outs]
        + [
            pltpu.SemaphoreType.DMA((11,)),
            pltpu.SemaphoreType.DMA((tiles, 3)),
            pltpu.SemaphoreType.DMA((tiles + 2,)),
        ],
        compiler_params=params(),
    )(d.reshape(1), *args)


def tied(*values):
    return lax.optimization_barrier(values)


def paired_body(
    features,
    teacher_features,
    crop_image,
    crop_view,
    head_w1,
    head_w2,
    protos,
    teacher_w1,
    teacher_w2,
    teacher_protos,
):
    nd, n = lax.axis_size("dp"), lax.axis_size("proto")
    d, p = lax.axis_index("dp"), lax.axis_index("proto")
    rows, teach = features.shape[0], teacher_features.shape[0]
    sr, tr = rows // n, teach // n
    wide, hs = head_w1.shape
    bot = head_w2.shape[1]
    everyone = nd * n
    factor = 10.0 / (9 * teach * nd)

    feat_other = swap(features, "dp", 1)
    heads = (features, head_w1, head_w2, teacher_features, teacher_w1, teacher_w2)
    parts, place, view, weights = pl.pallas_call(
        head_kernel,
        grid=(1,),
        out_shape=(
            shape((n, sr + tr, bot), BF16),
            shape((1, rows), F32),
            shape((rows, 1), F32),
            shape((wide // 2 + hs, hs), BF16),
        ),
        in_specs=[pl.BlockSpec(memory_space=pltpu.SMEM)]
        + [pl.BlockSpec(memory_space=pl.ANY)] * 6
        + [block((rows,))] * 2,
        out_specs=(block((n, sr + tr, bot)), block((1, rows)), block((rows, 1)), block((wide // 2 + hs, hs))),
        scratch_shapes=[pltpu.VMEM(x.shape, x.dtype) for x in heads] + [pltpu.SemaphoreType.DMA((6,))],
        compiler_params=params(62),
        name="head_kernel",
    )(d.reshape(1), *heads, crop_image, crop_view)
    weights = [weights] + [swap(weights, "proto", k) for k in range(1, NEAR)]
    parts_got = lax.all_to_all(parts, "proto", 0, 0)
    protos_late, tprotos_late, _ = tied(protos, teacher_protos, parts)
    cols = protos.shape[1] // nd
    pnb = unit_cols(lax.dynamic_slice_in_dim(protos_late, d * cols, cols, 1))[0].astype(BF16)
    tpnb = unit_cols(lax.dynamic_slice_in_dim(tprotos_late, d * cols, cols, 1))[0].astype(BF16)
    parts_got, pnb, tpnb = tied(parts_got, pnb, tpnb)

    got, zn = call(
        rows_kernel,
        (shape((n, sr + tr, bot), BF16), shape((sr + tr, bot + 128), F32)),
        [],
        parts_got,
        mib=40,
    )
    sent = got
    got = lax.all_to_all(got, "proto", 0, 0)
    w1_late, feat_late, feat_other_late, weights, _ = tied(head_w1, features, feat_other, weights, sent)
    h0, h1, s0, s1 = call(
        hidden_kernel,
        (shape((hs, rows), BF16),) * 2 + (shape((hs, rows), F32),) * 2,
        [],
        feat_late, feat_other_late, w1_late,
        us=4,
    )
    weights = jnp.stack(weights)
    got, h0, h1, s0, s1, weights = tied(got, h0, h1, s0, s1, weights)
    weights_other = swap(weights, "dp", 1)
    got_other = swap(got, "dp", 1)
    kern, msg, student = call(
        kern_kernel,
        (shape((nd * teach, cols), F32), shape((everyone, nd * teach // 128, 128), F32), shape((nd * rows, bot), BF16)),
        [d],
        got, got_other, tpnb,
        us=3,
    )
    msg_got = lax.all_to_all(msg, ALL, 0, 0)
    student, _ = tied(student, msg)
    exb, sums, sums_other, esum = student_sums(student, pnb)
    msg = call(
        second_kernel,
        shape((everyone, 1, nd * teach + rows), F32),
        [d],
        msg_got, kern, esum,
        mib=56,
    )
    msg_got = lax.all_to_all(msg, ALL, 0, 0)
    sums, sums_other, _ = tied(sums, sums_other, msg)
    sums_other = swap(sums_other, "dp", 1)
    sums = (sums + sums_other).astype(BF16)
    msg_got, sums = tied(msg_got, sums)
    esum, last, mine, yours = call(
        third_kernel,
        (
            shape((rows, 1), F32),
            shape((nd * teach, cols), BF16),
            shape((teach, bot + 128), F32),
            shape((teach, bot + 128), F32),
        ),
        [d],
        msg_got, kern, pnb,
        us=2,
    )
    yours = swap(yours, "dp", 1)
    msg = call(message_kernel, shape((n, sr + 2 * tr, bot), BF16), [], sums, mine, yours)
    msg_got = lax.all_to_all(msg, "proto", 0, 0)

    esum, view_late, last, weights, place, _ = tied(esum, view, last, weights, place, msg)
    place_other = swap(place, "dp", 1)
    crop_scale = jnp.where(view_late == 2, 2.0, 1.0) * factor / esum
    scale_other = swap(crop_scale, "dp", 1)
    left = (student.astype(F32) * jnp.concatenate([crop_scale, scale_other], axis=0)).astype(BF16)
    dpn = dot(left, exb, ((0,), (0,))).astype(BF16)
    msg_got, dpn = tied(msg_got, dpn)
    dpn_other, last_other = swap(dpn, "dp", 1), swap(last, "dp", 1)
    dz = call(
        functools.partial(bottleneck_kernel, factor),
        shape((n, sr + tr, bot), BF16),
        [p],
        msg_got, zn, view_late, crop_scale,
    )
    got = lax.all_to_all(dz, "proto", 0, 0)
    weights, feat_late, _ = tied(weights, features, dz)
    slopes = slopes_of(d, p, feat_late, weights, weights_other, wide // n, n // NEAR)
    got, slopes = tied(got, slopes)

    got_other = swap(got, "dp", 1)
    dz, grad_features, *far = feature_grads(got, place, *slopes)
    far = [swap(x, "proto", k * NEAR) for k, x in enumerate(far, 1)]
    grad_protos, grad_w1, grad_w2 = last_grads(
        d, head_w1, dz, got, got_other, place_other, protos, dpn, dpn_other, last, last_other,
        features, feat_other, h0, h1, s0, s1, head_w2,
    )
    grad_protos, *far = tied(grad_protos, *far)
    grad_features = (grad_features + sum(x.astype(F32) for x in far)).astype(BF16).T
    return (grad_features, grad_w1, grad_w2, grad_protos)


def body(features, teacher_features, *rest):
    n = lax.axis_size("proto")
    slot = (features.shape[0] // n, teacher_features.shape[0] // n)
    paired = lax.axis_size("dp") == 2 and n == 4 * NEAR and slot[0] % 8 == 0 and slot[1] % 8 == 0
    paired = paired and features.shape[0] % teacher_features.shape[0] == 0
    return (paired_body if paired else general_body)(features, teacher_features, *rest)


def solution(mesh):
    in_specs = (
        P("dp", None),
        P("dp", None),
        P("dp"),
        P("dp"),
        P(None, "proto"),
        P("proto", None),
        P(None, "proto"),
        P(None, "proto"),
        P("proto", None),
        P(None, "proto"),
    )
    out_specs = (P("dp", "proto"), P(None, "proto"), P("proto", None), P(None, "proto"))
    return jax.shard_map(body, mesh=mesh, in_specs=in_specs, out_specs=out_specs, check_vma=False)
```

```python
import functools

import jax
import jax.numpy as jnp
from jax import lax
from jax.experimental import pallas as pl
from jax.experimental.pallas import tpu as pltpu
from jax.sharding import PartitionSpec as P

ITERS = 3
ALL = ("dp", "proto")
NEAR = 4
F32 = jnp.float32
BF16 = jnp.bfloat16


def gelu_parts(act):
    phi = 0.5 * (1.0 + lax.erf(act * 0.7071067811865476))
    slope = phi + act * jnp.exp(-0.5 * act * act) * 0.3989422804014327
    return (act * phi).astype(BF16), slope


def dot(a, b, dims):
    return lax.dot_general(a, b, (dims, ((), ())), preferred_element_type=F32)


def swap(value, axis, step):
    count = lax.axis_size(axis)
    return lax.ppermute(value, axis, [(i, i ^ step) for i in range(count)])


def over_dp(value):
    return [value] + [swap(value, "dp", s) for s in range(1, lax.axis_size("dp"))]


def tree_sum(parts):
    while len(parts) > 1:
        parts = [parts[i] + parts[i + 1] for i in range(0, len(parts), 2)]
    return parts[0]


def send_all(value, axes):
    count = lax.axis_size(axes)
    return lax.all_to_all(jnp.broadcast_to(value[None], (count,) + value.shape), axes, 0, 0)


def unit_cols(mat):
    matf = mat.astype(F32)
    inv = lax.rsqrt(jnp.sum(matf * matf, axis=0, keepdims=True) + 1e-06)
    return matf * inv, inv


def general_body(
    features,
    teacher_features,
    crop_image,
    crop_view,
    head_w1,
    head_w2,
    protos,
    teacher_w1,
    teacher_w2,
    teacher_protos,
):
    nd, n = lax.axis_size("dp"), lax.axis_size("proto")
    d, p = lax.axis_index("dp"), lax.axis_index("proto")
    rows, img = features.shape[0], teacher_features.shape[0] // 2
    per = rows // img
    sr, tr = rows // n, 2 * img // n
    bot = head_w2.shape[1]
    factor = 10.0 / (18 * img * nd)
    absolute = d ^ jnp.arange(nd)

    im = crop_image - d * img
    at = jnp.arange(rows, dtype=jnp.int32)
    rank = jnp.sum((im[:, None] == im[None, :]) & (at[None, :] < at[:, None]), axis=1)
    place = im * per + rank
    hit = at[:, None] == place[None, :]
    order = hit.astype(BF16)
    view = jnp.sum(jnp.where(hit, crop_view[None, :], 0), axis=1)
    views = jnp.stack(over_dp(view))[absolute]

    w1_block = lax.all_to_all(head_w1, "proto", split_axis=0, concat_axis=1, tiled=True)
    feats = over_dp(features)
    act = jnp.dot(features, head_w1, preferred_element_type=F32)
    hidden, slope = gelu_parts(act)
    zpart = jnp.dot(hidden, head_w2, preferred_element_type=F32).astype(BF16)
    zpart = jnp.dot(order, zpart, preferred_element_type=F32).astype(BF16)
    tact = jnp.dot(teacher_features, teacher_w1, preferred_element_type=F32)
    thidden, _ = gelu_parts(tact)
    tpart = jnp.dot(thidden, teacher_w2, preferred_element_type=F32).astype(BF16)
    parts = jnp.concatenate([zpart.reshape(n, sr, bot), tpart.reshape(n, tr, bot)], axis=1)
    parts = lax.all_to_all(parts, "proto", 0, 0)
    early = jnp.concatenate(
        [(slope - 0.5).astype(BF16)] + [head_w2[:, i : i + head_w1.shape[1]] for i in range(0, bot, head_w1.shape[1])],
        axis=0,
    )
    early = lax.all_gather(early, "proto")
    zrow = jnp.sum(parts.astype(F32), axis=0)
    zinv = lax.rsqrt(jnp.sum(zrow * zrow, axis=1, keepdims=True) + 1e-06)
    zn = zrow * zinv
    znb = send_all(zn.astype(BF16), "proto")
    znb = jnp.stack(over_dp(znb))[absolute]
    student = znb[:, :, :sr].reshape(nd * rows, bot)
    teacher = znb[:, :, sr:].reshape(nd * 2 * img, bot)

    cols = protos.shape[1] // nd
    pn, pinv = unit_cols(lax.dynamic_slice_in_dim(protos, d * cols, cols, 1))
    pnb = pn.astype(BF16)
    tpnb = unit_cols(lax.dynamic_slice_in_dim(teacher_protos, d * cols, cols, 1))[0].astype(BF16)

    kern = jnp.exp(jnp.dot(teacher, tpnb, preferred_element_type=F32) / 0.07)
    ex = jnp.exp(jnp.dot(student, pnb, preferred_element_type=F32) / 0.1)
    esum = jnp.sum(ex, axis=1)
    exb = ex.astype(BF16)
    sums = dot(exb, pnb, ((1,), (1,)))
    colscale = 1.0 / jnp.sum(kern, axis=0)
    for step in range(ITERS - 1):
        mass = jnp.sum(send_all(jnp.sum(kern * colscale[None, :], axis=1), ALL), axis=0)
        colscale = 1.0 / jnp.sum(kern / mass[:, None], axis=0)
    last = kern * colscale[None, :]
    lastb = last.astype(BF16)
    tsums = dot(lastb, pnb, ((1,), (1,)))
    tot = jnp.sum(send_all(jnp.concatenate([esum, jnp.sum(last, axis=1)]), ALL), axis=0)
    esum, mass = tot[: nd * rows], tot[nd * rows :]

    out = jnp.concatenate([sums.reshape(nd, n, sr, bot), tsums.reshape(nd, n, tr, bot)], axis=2)
    out = out[absolute]
    out = tree_sum([out[0]] + [swap(out[s], "dp", s) for s in range(1, nd)])
    out = jnp.sum(lax.all_to_all(out, "proto", 0, 0), axis=0)
    crop_scale = jnp.where(views == 2, 2.0, 1.0).reshape(-1) / esum * factor
    image_scale = factor / mass
    mine = (d * n + p)
    my_view = lax.dynamic_slice_in_dim(views.reshape(-1), mine * sr, sr)
    my_scale = lax.dynamic_slice_in_dim(crop_scale, mine * sr, sr)
    my_image = lax.dynamic_slice_in_dim(image_scale, mine * tr, tr)
    slot = jnp.arange(tr)
    pick = (slot[None, :] // 2 == jnp.arange(sr)[:, None] // per) & (slot[None, :] % 2 != my_view[:, None])
    target = jnp.sum(jnp.where(pick, my_image[None, :], 0.0)[:, :, None] * out[None, sr:], axis=1)
    dzn = my_scale[:, None] * out[:sr] - target
    zs, zi = zn[:sr], zinv[:sr]
    dz = (zi * (dzn - zs * jnp.sum(zs * dzn, axis=1, keepdims=True))).astype(BF16)
    dz = send_all(dz, "proto").reshape(rows, bot)
    dz = dot(order, dz, ((0,), (0,))).astype(BF16)
    dzs = over_dp(dz)

    tslot = jnp.arange(2 * img)
    picks = (tslot[None, None, :] // 2 == at[None, :, None] // per) & (tslot[None, None, :] % 2 != views[:, :, None])
    own = lax.dot_general(
        picks.astype(BF16), student.reshape(nd, rows, bot), (((1,), (1,)), ((0,), (0,))), preferred_element_type=F32
    ).reshape(nd * 2 * img, bot)
    left = (student.astype(F32) * crop_scale[:, None]).astype(BF16)
    right = (own * image_scale[:, None]).astype(BF16)
    dpn = dot(left, exb, ((0,), (0,))) - dot(right, lastb, ((0,), (0,)))
    gp = pinv * (dpn - pn * jnp.sum(pn * dpn, axis=0, keepdims=True))
    gps = over_dp(gp)
    grad_protos = jnp.zeros(protos.shape, F32)
    for s in range(nd):
        grad_protos = lax.dynamic_update_slice_in_dim(grad_protos, gps[s], (d ^ s) * cols, 1)

    w1_parts, w2_parts = [], []
    for s in range(nd):
        if s:
            hid, slp = gelu_parts(jnp.dot(feats[s], head_w1, preferred_element_type=F32))
        else:
            hid, slp = hidden, slope
        w2_parts.append(dot(hid, dzs[s], ((0,), (0,))))
        dhid = (dot(dzs[s], head_w2, ((1,), (1,))) * slp).astype(BF16)
        w1_parts.append(dot(feats[s], dhid, ((0,), (0,))))
    grad_w1, grad_w2 = tree_sum(w1_parts), tree_sum(w2_parts)
    slopes = 0.5 + early[:, :rows].astype(F32).transpose(1, 0, 2).reshape(rows, -1)
    w2_all = early[:, rows:].reshape(n, -1, head_w1.shape[1], head_w1.shape[1]).transpose(1, 3, 0, 2)
    w2_all = w2_all.reshape(bot, -1)
    dhid = (jnp.dot(dz, w2_all, preferred_element_type=F32) * slopes).astype(BF16)
    grad_features = dot(dhid, w1_block, ((1,), (1,))).astype(BF16)
    return (grad_features, grad_w1, grad_w2, grad_protos)


def params(mib=50):
    return pltpu.CompilerParams(vmem_limit_bytes=mib * 1024 * 1024)


def shape(dims, dtype):
    return jax.ShapeDtypeStruct(dims, dtype)


def kernel_name(kernel):
    return getattr(kernel, "func", kernel).__name__


def block(dims):
    return pl.BlockSpec(dims, lambda i: (0,) * len(dims))


def call(kernel, outs, scalars, *args, us=1, mib=50):
    smem = [jnp.asarray(s, jnp.int32).reshape(1) for s in scalars]
    return pl.pallas_call(
        kernel,
        grid=(1,),
        out_shape=outs,
        in_specs=[pl.BlockSpec(memory_space=pltpu.SMEM)] * len(smem) + [block(x.shape) for x in args],
        out_specs=jax.tree.map(lambda x: block(x.shape), outs),
        compiler_params=params(mib),
        name=kernel_name(kernel),
        cost_estimate=pl.CostEstimate(flops=us * 10**9, bytes_accessed=us * 10**6, transcendentals=0),
    )(*smem, *args)


def grids(dims):
    return lax.broadcasted_iota(jnp.int32, dims, 0), lax.broadcasted_iota(jnp.int32, dims, 1)


def to_row(col):
    down, along = grids((col.shape[0], col.shape[0]))
    return jnp.sum(jnp.where(down == along, col, jnp.zeros_like(col)), axis=0, keepdims=True)


def to_col(row):
    down, along = grids((row.shape[1], row.shape[1]))
    return jnp.sum(jnp.where(down == along, row, jnp.zeros_like(row)), axis=1, keepdims=True)


def head_kernel(d_ref, *refs):
    sources, im_ref, view_ref = refs[:6], refs[6], refs[7]
    parts_ref, place_ref, vs_ref, pack_ref = refs[8:12]
    held, sems = refs[12:18], refs[18]
    copies = [pltpu.make_async_copy(a, b, sems.at[k]) for k, (a, b) in enumerate(zip(sources, held))]
    for copy in copies:
        copy.start()
    f_ref, w1_ref, w2_ref, tf_ref, tw1_ref, tw2_ref = held
    rows, teach = f_ref.shape[0], tf_ref.shape[0]
    n = parts_ref.shape[0]
    img = teach // 2
    per = rows // img
    im = (im_ref[...].reshape(1, rows) - d_ref[0] * img).astype(F32)
    down, along = grids((rows, rows))
    imc = to_col(im)
    same = im == imc
    after = jnp.where(same & (down < along), 1.0, 0.0)
    row = im * per + jnp.sum(after, axis=0, keepdims=True)
    place_ref[...] = row
    hit = row.astype(jnp.int32) == down
    vs_ref[...] = jnp.sum(jnp.where(hit, view_ref[...].reshape(1, rows).astype(F32), 0.0), axis=1, keepdims=True)
    order = jnp.where(hit, 1.0, 0.0).astype(BF16)

    for copy in copies:
        copy.wait()

    deep, hs = w1_ref.shape[0] // 2, w1_ref.shape[1]
    half = hs // 2
    pack_ref[:deep] = w1_ref[pl.ds(pl.multiple_of(d_ref[0] * deep, deep), deep)]
    w2_half = w2_ref[pl.ds(pl.multiple_of(d_ref[0] * half, half), half)]
    pack_ref[deep : deep + half] = w2_half[:, :hs]
    pack_ref[deep + half :] = w2_half[:, hs:]

    def part(x, first, second):
        act = dot(x[...], first[...], ((1,), (0,)))
        hidden = (act * 0.5 * (1.0 + lax.erf(act * 0.7071067811865476))).astype(BF16)
        return dot(hidden, second[...], ((1,), (0,)))

    z = part(f_ref, w1_ref, w2_ref).astype(BF16)
    z = dot(order, z, ((1,), (0,))).reshape(n, rows // n, -1)
    t = part(tf_ref, tw1_ref, tw2_ref).reshape(n, teach // n, -1)
    parts_ref[...] = jnp.concatenate([z, t], axis=1).astype(BF16)


def rows_kernel(parts_ref, out_ref, zn_ref):
    z = jnp.sum(parts_ref[...].astype(F32), axis=0)
    inv = lax.rsqrt(jnp.sum(z * z, axis=1, keepdims=True) + 1e-06)
    zn = z * inv
    zn_ref[...] = jnp.concatenate([zn, jnp.broadcast_to(inv, (zn.shape[0], 128))], axis=1)
    out_ref[...] = jnp.broadcast_to(zn[None], out_ref.shape).astype(BF16)


def row_mass(kern, mass):
    if mass is None:
        scale = 1.0 / jnp.sum(kern, axis=0, keepdims=True)
    else:
        scale = 1.0 / jnp.sum(kern * (1.0 / mass), axis=0, keepdims=True)
    return scale, jnp.sum(kern * scale, axis=1, keepdims=True)


def fold(col):
    row = to_row(col)
    return jnp.concatenate([row[:, k : k + 128] for k in range(0, row.shape[1], 128)], axis=0)


def unfold(block):
    return to_col(jnp.concatenate([block[k : k + 1] for k in range(block.shape[0])], axis=1))


def kern_kernel(d_ref, got_ref, other_ref, tpnb_ref, kern_ref, msg_ref, student_ref):
    n, slot, bot = got_ref.shape
    rows = student_ref.shape[0] // 2
    sr = rows // n
    own, other = got_ref[...].astype(F32), other_ref[...].astype(F32)
    student_ref[:rows] = own[:, :sr].reshape(rows, bot).astype(BF16)
    student_ref[rows:] = other[:, :sr].reshape(rows, bot).astype(BF16)
    own, other = own[:, sr:].reshape(-1, bot), other[:, sr:].reshape(-1, bot)
    first = d_ref[0] == 0
    teacher = jnp.concatenate([jnp.where(first, own, other), jnp.where(first, other, own)], axis=0).astype(BF16)
    kern = jnp.exp(dot(teacher, tpnb_ref[...], ((1,), (0,))) * (1.0 / 0.07))
    kern_ref[...] = kern
    _, mass = row_mass(kern, None)
    msg_ref[...] = jnp.broadcast_to(fold(mass)[None], msg_ref.shape)


def student_kernel(z_ref, pnb_ref, exb_ref, own_ref, other_ref, esum_ref):
    step = pl.program_id(0)
    ex = jnp.exp(dot(z_ref[...], pnb_ref[...], ((1,), (0,))) * 10.0)
    esum_ref[...] = jnp.sum(ex, axis=1, keepdims=True)
    exb = ex.astype(BF16)
    exb_ref[...] = exb
    sums = dot(exb, pnb_ref[...], ((1,), (1,)))

    @pl.when(step < pl.num_programs(0) // 2)
    def _():
        own_ref[...] = sums

    @pl.when(step >= pl.num_programs(0) // 2)
    def _():
        other_ref[...] = sums


def student_sums(student, pnb):
    total, bot = student.shape
    cols = pnb.shape[1]
    tile = total // 4
    return pl.pallas_call(
        student_kernel,
        name="student_kernel",
        grid=(4,),
        out_shape=(
            shape((total, cols), BF16),
            shape((total // 2, bot), F32),
            shape((total // 2, bot), F32),
            shape((total, 1), F32),
        ),
        in_specs=[pl.BlockSpec((tile, bot), lambda i: (i, 0)), pl.BlockSpec((bot, cols), lambda i: (0, 0))],
        out_specs=(
            pl.BlockSpec((tile, cols), lambda i: (i, 0)),
            pl.BlockSpec((tile, bot), lambda i: (jnp.minimum(i, 1), 0)),
            pl.BlockSpec((tile, bot), lambda i: (jnp.maximum(i - 2, 0), 0)),
            pl.BlockSpec((tile, 1), lambda i: (i, 0)),
        ),
        compiler_params=params(),
        cost_estimate=pl.CostEstimate(flops=5 * 10**9, bytes_accessed=10**7, transcendentals=0),
    )(student, pnb)


def second_kernel(d_ref, got_ref, kern_ref, esum_ref, msg_ref):
    mass = unfold(jnp.sum(got_ref[...], axis=0))
    _, mass = row_mass(kern_ref[...], mass)
    half = esum_ref.shape[0] // 2
    own, other = to_row(esum_ref[:half]), to_row(esum_ref[half:])
    first = d_ref[0] == 0
    mass = to_row(mass)
    n = msg_ref.shape[0] // 2
    for k, row in enumerate((jnp.where(first, own, other), jnp.where(first, other, own))):
        part = jnp.concatenate([mass, row], axis=1)
        msg_ref[k * n : (k + 1) * n] = jnp.broadcast_to(part[None], (n,) + part.shape)


def third_kernel(d_ref, got_ref, kern_ref, pnb_ref, esum_ref, last_ref, mine_ref, yours_ref):
    teach = kern_ref.shape[0]
    got = jnp.sum(got_ref[...], axis=0)
    esum_ref[...] = to_col(got[:, teach:])
    kern = kern_ref[...]
    scale, mass = row_mass(kern, to_col(got[:, :teach]))
    last = (kern * scale).astype(BF16)
    last_ref[...] = last
    sums = dot(last, pnb_ref[...], ((1,), (1,)))
    sums = jnp.concatenate([sums, jnp.broadcast_to(mass, (teach, 128))], axis=1)
    half = teach // 2
    first = d_ref[0] == 0
    mine_ref[...] = jnp.where(first, sums[:half], sums[half:])
    yours_ref[...] = jnp.where(first, sums[half:], sums[:half])


def message_kernel(sums_ref, b0_ref, b1_ref, out_ref):
    n = out_ref.shape[0]
    rows, bot = sums_ref.shape
    sums = sums_ref[...].astype(F32).reshape(n, rows // n, bot)
    both = b0_ref[...] + b1_ref[...]
    mass = both[:, bot:]
    high = mass.astype(BF16).astype(F32)
    tail = jnp.concatenate([high, mass - high], axis=1)
    teach = both.shape[0]
    both = both[:, :bot].reshape(n, teach // n, bot)
    out_ref[...] = jnp.concatenate([sums, both, tail.reshape(n, teach // n, bot)], axis=1).astype(BF16)


def bottleneck_kernel(factor, p_ref, got_ref, zn_ref, view_ref, scale_ref, out_ref):
    sr = view_ref.shape[0] // out_ref.shape[0]
    mine = pl.ds(pl.multiple_of(p_ref[0] * sr, sr), sr)
    tr = zn_ref.shape[0] - sr
    per = sr // (tr // 2)
    out = jnp.sum(got_ref[...].astype(F32), axis=0)
    tail = out[sr + tr :]
    image = factor / (tail[:, :1] + tail[:, 128:129])
    sums = out[sr : sr + tr] * image
    bot = got_ref.shape[2]
    zn, zinv = zn_ref[:sr, :bot], zn_ref[:sr, bot : bot + 1]
    znb = zn.astype(BF16).astype(F32)
    view = view_ref[mine].astype(jnp.int32)
    which = lax.broadcasted_iota(jnp.int32, (sr, 1), 0)
    dzn = scale_ref[mine] * out[:sr]
    own = []
    for t in range(tr):
        base = (t // 2) * per
        pick = (which >= base) & (which < base + per) & (view != t % 2)
        dzn = dzn - jnp.where(pick, sums[t : t + 1], 0.0)
        own.append(jnp.sum(jnp.where(pick, znb, 0.0), axis=0, keepdims=True) * image[t : t + 1])
    dz = zinv * (dzn - zn * jnp.sum(zn * dzn, axis=1, keepdims=True))
    both = jnp.concatenate([dz] + own, axis=0)
    out_ref[...] = jnp.broadcast_to(both[None], out_ref.shape).astype(BF16)


def hidden_kernel(f0_ref, f1_ref, w1_ref, h0_ref, h1_ref, s0_ref, s1_ref):
    for f, h, s in ((f0_ref, h0_ref, s0_ref), (f1_ref, h1_ref, s1_ref)):
        act = dot(f[...], w1_ref[...], ((1,), (0,))).T
        phi = 0.5 * (1.0 + lax.erf(act * 0.7071067811865476))
        h[...] = (act * phi).astype(BF16)
        s[...] = phi + act * jnp.exp(-0.5 * act * act) * 0.3989422804014327


def slopes_kernel(d_ref, p_ref, f_ref, own_ref, other_ref, slope_ref, w2_ref, w1_ref):
    hs = own_ref.shape[2]
    deep = f_ref.shape[1] // 2
    first = d_ref[0] == 0
    own, other = own_ref[...], other_ref[...]
    low = jnp.where(first, own, other)
    high = jnp.where(first, other, own)
    a, b = (jnp.concatenate([x[0], x[1]], axis=1) for x in (low[:, :deep], high[:, :deep]))
    act = dot(f_ref[:, :deep], a, ((1,), (0,))) + dot(f_ref[:, deep:], b, ((1,), (0,)))
    phi = 0.5 * (1.0 + lax.erf(act * 0.7071067811865476))
    slope_ref[...] = phi + act * jnp.exp(-0.5 * act * act) * 0.3989422804014327
    groups, width = w1_ref.shape[0], w1_ref.shape[1]
    blocks = deep // width
    for k in range(groups):
        chip = p_ref[0] ^ (k * NEAR)
        at = pl.multiple_of(lax.rem(chip, blocks) * width, width)
        mine = (chip // blocks) == d_ref[0]
        rows = jnp.where(mine, own_ref[:, pl.ds(at, width)], other_ref[:, pl.ds(at, width)])
        w1_ref[k] = jnp.concatenate([rows[0], rows[1]], axis=1)
    half = hs // 2
    for k in range(2):
        for part, x in ((0, low), (1, high)):
            tail = jnp.concatenate([x[k, deep : deep + half], x[k, deep + half :]], axis=1)
            w2_ref[k * hs + part * half : k * hs + (part + 1) * half] = tail


def slopes_of(d, p, features, own, other, width, groups):
    n, tall, hs = own.shape
    rows = features.shape[0]
    whole = lambda k, d, p: (0, 0)
    return pl.pallas_call(
        slopes_kernel,
        name="slopes_kernel",
        grid_spec=pltpu.PrefetchScalarGridSpec(
            num_scalar_prefetch=2,
            grid=(n // 2,),
            in_specs=[
                pl.BlockSpec(features.shape, whole),
                pl.BlockSpec((2, tall, hs), lambda k, d, p: (k, 0, 0)),
                pl.BlockSpec((2, tall, hs), lambda k, d, p: (k, 0, 0)),
            ],
            out_specs=(
                pl.BlockSpec((rows, 2 * hs), lambda k, d, p: (0, k)),
                pl.BlockSpec((2 * hs, 2 * hs), lambda k, d, p: (k, 0)),
                pl.BlockSpec((groups, width, 2 * hs), lambda k, d, p: (0, 0, k)),
            ),
        ),
        out_shape=(shape((rows, n * hs), F32), shape((n * hs, 2 * hs), BF16), shape((groups, width, n * hs), BF16)),
        compiler_params=params(),
        cost_estimate=pl.CostEstimate(flops=4 * 10**9, bytes_accessed=3 * 10**7, transcendentals=0),
    )(d.reshape(1), p.reshape(1), features, own, other)


def fetch(pairs, sems):
    copies = [pltpu.make_async_copy(x, y, sems.at[k]) for k, (x, y) in enumerate(pairs)]
    for copy in copies:
        copy.start()
    return copies


def put_back(got, place):
    n, _, bot = got.shape
    rows = place.shape[1]
    _, along = grids((rows, rows))
    back = jnp.where(to_col(place).astype(jnp.int32) == along, 1.0, 0.0).astype(BF16)
    dz = got.astype(F32)[:, : rows // n].reshape(rows, bot).astype(BF16)
    return dot(back, dz, ((1,), (0,))).astype(BF16)


def features_kernel(step, *refs):
    ins, held, sems = refs[:5], refs[-6:-1], refs[-1]
    dz_ref, own_ref, *far_refs = refs[5:-6]
    got, place, slope, w2, w1 = held
    groups, width = w1.shape[:2]
    pieces = [pl.ds(k, step) for k in range(0, slope.shape[1], step)]
    small = fetch([(ins[k], held[k]) for k in (0, 1, 4)], sems.at[pl.ds(0, 3)])
    large = []
    for k, piece in enumerate(pieces):
        pairs = [(ins[2].at[:, piece], slope.at[:, piece]), (ins[3].at[piece], w2.at[piece])]
        large.append(fetch(pairs, sems.at[pl.ds(3 + 2 * k, 2)]))
    for copy in small:
        copy.wait()
    dz = put_back(got[...], place[...])
    dz_ref[...] = dz
    total = None
    for piece, copies in zip(pieces, large):
        for copy in copies:
            copy.wait()
        dhid = (dot(dz, w2[piece], ((1,), (1,))) * slope[:, piece]).astype(BF16)
        part = dot(w1[:, :, piece].reshape(groups * width, step), dhid, ((1,), (1,)))
        total = part if total is None else total + part
    own_ref[...] = total[:width]
    for k, far_ref in enumerate(far_refs, 1):
        far_ref[...] = total[k * width : (k + 1) * width].astype(BF16)


def feature_grads(got, place, slope, w2, w1):
    args = (got, place, slope, w2, w1)
    rows, hidden = slope.shape
    bot, step = got.shape[2], 256
    groups, width = w1.shape[:2]
    outs = (shape((rows, bot), BF16), shape((width, rows), F32)) + (shape((width, rows), BF16),) * (groups - 1)
    return pl.pallas_call(
        functools.partial(features_kernel, step),
        name="features_kernel",
        grid=(1,),
        out_shape=outs,
        in_specs=[pl.BlockSpec(memory_space=pl.ANY)] * len(args),
        out_specs=tuple(block(x.shape) for x in outs),
        scratch_shapes=[pltpu.VMEM(x.shape, x.dtype) for x in args]
        + [pltpu.SemaphoreType.DMA((3 + 2 * (hidden // step),))],
        compiler_params=params(),
    )(*args)


def last_kernel(tile, d_ref, *refs):
    ins, (gp_hbm, g1_hbm, g2_hbm) = refs[:16], refs[16:19]
    held, (gp, g1, g2, sems, tile_sems, out_sems) = refs[19:35], refs[35:]
    dz0, got0, got1, place1, protos, down, dother, lown, lother, f0, f1, h0, h1, s0, s1, w2 = held
    cols = protos.shape[1] // 2
    steps = cols // tile
    rows = dz0.shape[0]
    n, slot, bot = got0.shape
    early = fetch([(ins[k], held[k]) for k in range(4)], sems)
    tiles = []
    for k in range(2 * steps):
        own = k < steps
        here = pl.multiple_of((d_ref[0] if own else 1 - d_ref[0]) * cols + (k % steps) * tile, tile)
        there = pl.ds((k % steps) * tile, tile)
        a, b = (5, 7) if own else (6, 8)
        pairs = [
            (ins[4].at[:, pl.ds(here, tile)], protos.at[:, pl.ds(here, tile)]),
            (ins[a].at[:, there], held[a].at[:, there]),
            (ins[b].at[:, there], held[b].at[:, there]),
        ]
        tiles.append((here, there, a, b, fetch(pairs, tile_sems.at[k])))
    late = fetch([(ins[k], held[k]) for k in range(9, 16)], sems.at[pl.ds(4, 7)])
    for copy in early:
        copy.wait()
    first = d_ref[0] == 0
    right0 = got0[...].astype(F32)[:, rows // n :].reshape(-1, bot)
    right1 = got1[...].astype(F32)[:, rows // n :].reshape(-1, bot)
    right = jnp.concatenate([jnp.where(first, right0, right1), jnp.where(first, right1, right0)], axis=0)
    right = right.T.astype(BF16)
    dz1 = put_back(got1[...], place1[...])
    outs = []
    for k, (here, there, a, b, copies) in enumerate(tiles):
        for copy in copies:
            copy.wait()
        mat = protos[:, pl.ds(here, tile)].astype(F32)
        inv = lax.rsqrt(jnp.sum(mat * mat, axis=0, keepdims=True) + 1e-06)
        pn = mat * inv
        dpn = held[a][:, there].astype(F32) - dot(right, held[b][:, there], ((1,), (0,)))
        gp[:, pl.ds(here, tile)] = inv * (dpn - pn * jnp.sum(pn * dpn, axis=0, keepdims=True))
        out = pltpu.make_async_copy(gp.at[:, pl.ds(here, tile)], gp_hbm.at[:, pl.ds(here, tile)], out_sems.at[k])
        out.start()
        outs.append(out)
    for copy in late:
        copy.wait()
    sums1, sums2 = [], []
    for f, dz, h, sl in ((f0, dz0[...], h0, s0), (f1, dz1, h1, s1)):
        sums2.append(dot(h[...], dz, ((1,), (0,))))
        dhid = (dot(w2[...], dz, ((1,), (1,))) * sl[...]).astype(BF16)
        sums1.append(dot(dhid, f[...], ((1,), (0,))))
    g1[...] = (sums1[0] + sums1[1]).T
    g2[...] = sums2[0] + sums2[1]
    for k, (x, y) in enumerate(((g1, g1_hbm), (g2, g2_hbm))):
        out = pltpu.make_async_copy(x, y, out_sems.at[2 * steps + k])
        out.start()
        outs.append(out)
    for out in outs:
        out.wait()


def last_grads(d, head_w1, *args):
    tile = 512
    protos, head_w2 = args[4], args[15]
    tiles = protos.shape[1] // tile
    outs = (shape(protos.shape, F32), shape(head_w1.shape, F32), shape(head_w2.shape, F32))
    anywhere = pl.BlockSpec(memory_space=pl.ANY)
    return pl.pallas_call(
        functools.partial(last_kernel, tile),
        name="last_kernel",
        out_shape=outs,
        in_specs=[pl.BlockSpec(memory_space=pltpu.SMEM)] + [anywhere] * len(args),
        out_specs=(anywhere,) * 3,
        scratch_shapes=[pltpu.VMEM(x.shape, x.dtype) for x in args + outs]
        + [
            pltpu.SemaphoreType.DMA((11,)),
            pltpu.SemaphoreType.DMA((tiles, 3)),
            pltpu.SemaphoreType.DMA((tiles + 2,)),
        ],
        compiler_params=params(),
    )(d.reshape(1), *args)


def tied(*values):
    return lax.optimization_barrier(values)


def paired_body(
    features,
    teacher_features,
    crop_image,
    crop_view,
    head_w1,
    head_w2,
    protos,
    teacher_w1,
    teacher_w2,
    teacher_protos,
):
    nd, n = lax.axis_size("dp"), lax.axis_size("proto")
    d, p = lax.axis_index("dp"), lax.axis_index("proto")
    rows, teach = features.shape[0], teacher_features.shape[0]
    sr, tr = rows // n, teach // n
    wide, hs = head_w1.shape
    bot = head_w2.shape[1]
    everyone = nd * n
    factor = 10.0 / (9 * teach * nd)

    feat_other = swap(features, "dp", 1)
    heads = (features, head_w1, head_w2, teacher_features, teacher_w1, teacher_w2)
    parts, place, view, weights = pl.pallas_call(
        head_kernel,
        grid=(1,),
        out_shape=(
            shape((n, sr + tr, bot), BF16),
            shape((1, rows), F32),
            shape((rows, 1), F32),
            shape((wide // 2 + hs, hs), BF16),
        ),
        in_specs=[pl.BlockSpec(memory_space=pltpu.SMEM)]
        + [pl.BlockSpec(memory_space=pl.ANY)] * 6
        + [block((rows,))] * 2,
        out_specs=(block((n, sr + tr, bot)), block((1, rows)), block((rows, 1)), block((wide // 2 + hs, hs))),
        scratch_shapes=[pltpu.VMEM(x.shape, x.dtype) for x in heads] + [pltpu.SemaphoreType.DMA((6,))],
        compiler_params=params(62),
        name="head_kernel",
    )(d.reshape(1), *heads, crop_image, crop_view)
    parts_got = lax.all_to_all(parts, "proto", 0, 0)
    protos_late, tprotos_late, _ = tied(protos, teacher_protos, parts)
    cols = protos.shape[1] // nd
    pnb = unit_cols(lax.dynamic_slice_in_dim(protos_late, d * cols, cols, 1))[0].astype(BF16)
    tpnb = unit_cols(lax.dynamic_slice_in_dim(tprotos_late, d * cols, cols, 1))[0].astype(BF16)
    parts_got, pnb, tpnb = tied(parts_got, pnb, tpnb)

    got, zn = call(
        rows_kernel,
        (shape((n, sr + tr, bot), BF16), shape((sr + tr, bot + 128), F32)),
        [],
        parts_got,
        mib=40,
    )
    sent = got
    got = lax.all_to_all(got, "proto", 0, 0)
    w1_late, feat_late, feat_other_late, _ = tied(head_w1, features, feat_other, sent)
    h0, h1, s0, s1 = call(
        hidden_kernel,
        (shape((hs, rows), BF16),) * 2 + (shape((hs, rows), F32),) * 2,
        [],
        feat_late, feat_other_late, w1_late,
        us=4,
    )
    got, h0, h1, s0, s1 = tied(got, h0, h1, s0, s1)
    got_other = swap(got, "dp", 1)
    kern, msg, student = call(
        kern_kernel,
        (shape((nd * teach, cols), F32), shape((everyone, nd * teach // 128, 128), F32), shape((nd * rows, bot), BF16)),
        [d],
        got, got_other, tpnb,
        us=3,
    )
    msg_got = lax.all_to_all(msg, ALL, 0, 0)
    student, weights, _ = tied(student, weights, msg)
    weights = [weights] + [swap(weights, "proto", k) for k in range(1, NEAR)]
    exb, sums, sums_other, esum = student_sums(student, pnb)
    msg = call(
        second_kernel,
        shape((everyone, 1, nd * teach + rows), F32),
        [d],
        msg_got, kern, esum,
        mib=56,
    )
    msg_got = lax.all_to_all(msg, ALL, 0, 0)
    sums, sums_other, *weights, _ = tied(sums, sums_other, *weights, msg)
    weights = jnp.stack(weights)
    sums_other = swap(sums_other, "dp", 1)
    sums = (sums + sums_other).astype(BF16)
    msg_got, sums, weights = tied(msg_got, sums, weights)
    weights_other = swap(weights, "dp", 1)
    esum, last, mine, yours = call(
        third_kernel,
        (
            shape((rows, 1), F32),
            shape((nd * teach, cols), BF16),
            shape((teach, bot + 128), F32),
            shape((teach, bot + 128), F32),
        ),
        [d],
        msg_got, kern, pnb,
        us=2,
    )
    yours = swap(yours, "dp", 1)
    msg = call(message_kernel, shape((n, sr + 2 * tr, bot), BF16), [], sums, mine, yours)
    msg_got = lax.all_to_all(msg, "proto", 0, 0)

    esum, view_late, last, weights, place, _ = tied(esum, view, last, weights, place, msg)
    place_other = swap(place, "dp", 1)
    crop_scale = jnp.where(view_late == 2, 2.0, 1.0) * factor / esum
    scale_other = swap(crop_scale, "dp", 1)
    left = (student.astype(F32) * jnp.concatenate([crop_scale, scale_other], axis=0)).astype(BF16)
    dpn = dot(left, exb, ((0,), (0,))).astype(BF16)
    msg_got, dpn = tied(msg_got, dpn)
    dpn_other, last_other = swap(dpn, "dp", 1), swap(last, "dp", 1)
    dz = call(
        functools.partial(bottleneck_kernel, factor),
        shape((n, sr + tr, bot), BF16),
        [p],
        msg_got, zn, view_late, crop_scale,
    )
    got = lax.all_to_all(dz, "proto", 0, 0)
    weights, feat_late, _ = tied(weights, features, dz)
    slopes = slopes_of(d, p, feat_late, weights, weights_other, wide // n, n // NEAR)
    got, slopes = tied(got, slopes)

    got_other = swap(got, "dp", 1)
    dz, grad_features, *far = feature_grads(got, place, *slopes)
    far = [swap(x, "proto", k * NEAR) for k, x in enumerate(far, 1)]
    grad_protos, grad_w1, grad_w2 = last_grads(
        d, head_w1, dz, got, got_other, place_other, protos, dpn, dpn_other, last, last_other,
        features, feat_other, h0, h1, s0, s1, head_w2,
    )
    grad_protos, *far = tied(grad_protos, *far)
    grad_features = (grad_features + sum(x.astype(F32) for x in far)).astype(BF16).T
    return (grad_features, grad_w1, grad_w2, grad_protos)


def body(features, teacher_features, *rest):
    n = lax.axis_size("proto")
    slot = (features.shape[0] // n, teacher_features.shape[0] // n)
    paired = lax.axis_size("dp") == 2 and n == 4 * NEAR and slot[0] % 8 == 0 and slot[1] % 8 == 0
    paired = paired and features.shape[0] % teacher_features.shape[0] == 0
    return (paired_body if paired else general_body)(features, teacher_features, *rest)


def solution(mesh):
    in_specs = (
        P("dp", None),
        P("dp", None),
        P("dp"),
        P("dp"),
        P(None, "proto"),
        P("proto", None),
        P(None, "proto"),
        P(None, "proto"),
        P("proto", None),
        P(None, "proto"),
    )
    out_specs = (P("dp", "proto"), P(None, "proto"), P("proto", None), P(None, "proto"))
    return jax.shard_map(body, mesh=mesh, in_specs=in_specs, out_specs=out_specs, check_vma=False)
```

```python
import functools

import jax
import jax.numpy as jnp
from jax import lax
from jax.experimental import pallas as pl
from jax.experimental.pallas import tpu as pltpu
from jax.sharding import PartitionSpec as P

ITERS = 3
ALL = ("dp", "proto")
NEAR = 4
F32 = jnp.float32
BF16 = jnp.bfloat16


def gelu_parts(act):
    phi = 0.5 * (1.0 + lax.erf(act * 0.7071067811865476))
    slope = phi + act * jnp.exp(-0.5 * act * act) * 0.3989422804014327
    return (act * phi).astype(BF16), slope


def dot(a, b, dims):
    return lax.dot_general(a, b, (dims, ((), ())), preferred_element_type=F32)


def swap(value, axis, step):
    count = lax.axis_size(axis)
    return lax.ppermute(value, axis, [(i, i ^ step) for i in range(count)])


def over_dp(value):
    return [value] + [swap(value, "dp", s) for s in range(1, lax.axis_size("dp"))]


def tree_sum(parts):
    while len(parts) > 1:
        parts = [parts[i] + parts[i + 1] for i in range(0, len(parts), 2)]
    return parts[0]


def send_all(value, axes):
    count = lax.axis_size(axes)
    return lax.all_to_all(jnp.broadcast_to(value[None], (count,) + value.shape), axes, 0, 0)


def unit_cols(mat):
    matf = mat.astype(F32)
    inv = lax.rsqrt(jnp.sum(matf * matf, axis=0, keepdims=True) + 1e-06)
    return matf * inv, inv


def general_body(
    features,
    teacher_features,
    crop_image,
    crop_view,
    head_w1,
    head_w2,
    protos,
    teacher_w1,
    teacher_w2,
    teacher_protos,
):
    nd, n = lax.axis_size("dp"), lax.axis_size("proto")
    d, p = lax.axis_index("dp"), lax.axis_index("proto")
    rows, img = features.shape[0], teacher_features.shape[0] // 2
    per = rows // img
    sr, tr = rows // n, 2 * img // n
    bot = head_w2.shape[1]
    factor = 10.0 / (18 * img * nd)
    absolute = d ^ jnp.arange(nd)

    im = crop_image - d * img
    at = jnp.arange(rows, dtype=jnp.int32)
    rank = jnp.sum((im[:, None] == im[None, :]) & (at[None, :] < at[:, None]), axis=1)
    place = im * per + rank
    hit = at[:, None] == place[None, :]
    order = hit.astype(BF16)
    view = jnp.sum(jnp.where(hit, crop_view[None, :], 0), axis=1)
    views = jnp.stack(over_dp(view))[absolute]

    w1_block = lax.all_to_all(head_w1, "proto", split_axis=0, concat_axis=1, tiled=True)
    feats = over_dp(features)
    act = jnp.dot(features, head_w1, preferred_element_type=F32)
    hidden, slope = gelu_parts(act)
    zpart = jnp.dot(hidden, head_w2, preferred_element_type=F32).astype(BF16)
    zpart = jnp.dot(order, zpart, preferred_element_type=F32).astype(BF16)
    tact = jnp.dot(teacher_features, teacher_w1, preferred_element_type=F32)
    thidden, _ = gelu_parts(tact)
    tpart = jnp.dot(thidden, teacher_w2, preferred_element_type=F32).astype(BF16)
    parts = jnp.concatenate([zpart.reshape(n, sr, bot), tpart.reshape(n, tr, bot)], axis=1)
    parts = lax.all_to_all(parts, "proto", 0, 0)
    early = jnp.concatenate(
        [(slope - 0.5).astype(BF16)] + [head_w2[:, i : i + head_w1.shape[1]] for i in range(0, bot, head_w1.shape[1])],
        axis=0,
    )
    early = lax.all_gather(early, "proto")
    zrow = jnp.sum(parts.astype(F32), axis=0)
    zinv = lax.rsqrt(jnp.sum(zrow * zrow, axis=1, keepdims=True) + 1e-06)
    zn = zrow * zinv
    znb = send_all(zn.astype(BF16), "proto")
    znb = jnp.stack(over_dp(znb))[absolute]
    student = znb[:, :, :sr].reshape(nd * rows, bot)
    teacher = znb[:, :, sr:].reshape(nd * 2 * img, bot)

    cols = protos.shape[1] // nd
    pn, pinv = unit_cols(lax.dynamic_slice_in_dim(protos, d * cols, cols, 1))
    pnb = pn.astype(BF16)
    tpnb = unit_cols(lax.dynamic_slice_in_dim(teacher_protos, d * cols, cols, 1))[0].astype(BF16)

    kern = jnp.exp(jnp.dot(teacher, tpnb, preferred_element_type=F32) / 0.07)
    ex = jnp.exp(jnp.dot(student, pnb, preferred_element_type=F32) / 0.1)
    esum = jnp.sum(ex, axis=1)
    exb = ex.astype(BF16)
    sums = dot(exb, pnb, ((1,), (1,)))
    colscale = 1.0 / jnp.sum(kern, axis=0)
    for step in range(ITERS - 1):
        mass = jnp.sum(send_all(jnp.sum(kern * colscale[None, :], axis=1), ALL), axis=0)
        colscale = 1.0 / jnp.sum(kern / mass[:, None], axis=0)
    last = kern * colscale[None, :]
    lastb = last.astype(BF16)
    tsums = dot(lastb, pnb, ((1,), (1,)))
    tot = jnp.sum(send_all(jnp.concatenate([esum, jnp.sum(last, axis=1)]), ALL), axis=0)
    esum, mass = tot[: nd * rows], tot[nd * rows :]

    out = jnp.concatenate([sums.reshape(nd, n, sr, bot), tsums.reshape(nd, n, tr, bot)], axis=2)
    out = out[absolute]
    out = tree_sum([out[0]] + [swap(out[s], "dp", s) for s in range(1, nd)])
    out = jnp.sum(lax.all_to_all(out, "proto", 0, 0), axis=0)
    crop_scale = jnp.where(views == 2, 2.0, 1.0).reshape(-1) / esum * factor
    image_scale = factor / mass
    mine = (d * n + p)
    my_view = lax.dynamic_slice_in_dim(views.reshape(-1), mine * sr, sr)
    my_scale = lax.dynamic_slice_in_dim(crop_scale, mine * sr, sr)
    my_image = lax.dynamic_slice_in_dim(image_scale, mine * tr, tr)
    slot = jnp.arange(tr)
    pick = (slot[None, :] // 2 == jnp.arange(sr)[:, None] // per) & (slot[None, :] % 2 != my_view[:, None])
    target = jnp.sum(jnp.where(pick, my_image[None, :], 0.0)[:, :, None] * out[None, sr:], axis=1)
    dzn = my_scale[:, None] * out[:sr] - target
    zs, zi = zn[:sr], zinv[:sr]
    dz = (zi * (dzn - zs * jnp.sum(zs * dzn, axis=1, keepdims=True))).astype(BF16)
    dz = send_all(dz, "proto").reshape(rows, bot)
    dz = dot(order, dz, ((0,), (0,))).astype(BF16)
    dzs = over_dp(dz)

    tslot = jnp.arange(2 * img)
    picks = (tslot[None, None, :] // 2 == at[None, :, None] // per) & (tslot[None, None, :] % 2 != views[:, :, None])
    own = lax.dot_general(
        picks.astype(BF16), student.reshape(nd, rows, bot), (((1,), (1,)), ((0,), (0,))), preferred_element_type=F32
    ).reshape(nd * 2 * img, bot)
    left = (student.astype(F32) * crop_scale[:, None]).astype(BF16)
    right = (own * image_scale[:, None]).astype(BF16)
    dpn = dot(left, exb, ((0,), (0,))) - dot(right, lastb, ((0,), (0,)))
    gp = pinv * (dpn - pn * jnp.sum(pn * dpn, axis=0, keepdims=True))
    gps = over_dp(gp)
    grad_protos = jnp.zeros(protos.shape, F32)
    for s in range(nd):
        grad_protos = lax.dynamic_update_slice_in_dim(grad_protos, gps[s], (d ^ s) * cols, 1)

    w1_parts, w2_parts = [], []
    for s in range(nd):
        if s:
            hid, slp = gelu_parts(jnp.dot(feats[s], head_w1, preferred_element_type=F32))
        else:
            hid, slp = hidden, slope
        w2_parts.append(dot(hid, dzs[s], ((0,), (0,))))
        dhid = (dot(dzs[s], head_w2, ((1,), (1,))) * slp).astype(BF16)
        w1_parts.append(dot(feats[s], dhid, ((0,), (0,))))
    grad_w1, grad_w2 = tree_sum(w1_parts), tree_sum(w2_parts)
    slopes = 0.5 + early[:, :rows].astype(F32).transpose(1, 0, 2).reshape(rows, -1)
    w2_all = early[:, rows:].reshape(n, -1, head_w1.shape[1], head_w1.shape[1]).transpose(1, 3, 0, 2)
    w2_all = w2_all.reshape(bot, -1)
    dhid = (jnp.dot(dz, w2_all, preferred_element_type=F32) * slopes).astype(BF16)
    grad_features = dot(dhid, w1_block, ((1,), (1,))).astype(BF16)
    return (grad_features, grad_w1, grad_w2, grad_protos)


def params(mib=51):
    return pltpu.CompilerParams(vmem_limit_bytes=mib * 1024 * 1024)


def shape(dims, dtype):
    return jax.ShapeDtypeStruct(dims, dtype)


def kernel_name(kernel):
    return getattr(kernel, "func", kernel).__name__


def block(dims):
    return pl.BlockSpec(dims, lambda i: (0,) * len(dims))


def call(kernel, outs, scalars, *args, us=1, mib=51):
    smem = [jnp.asarray(s, jnp.int32).reshape(1) for s in scalars]
    return pl.pallas_call(
        kernel,
        grid=(1,),
        out_shape=outs,
        in_specs=[pl.BlockSpec(memory_space=pltpu.SMEM)] * len(smem) + [block(x.shape) for x in args],
        out_specs=jax.tree.map(lambda x: block(x.shape), outs),
        compiler_params=params(mib),
        name=kernel_name(kernel),
        cost_estimate=pl.CostEstimate(flops=us * 10**9, bytes_accessed=us * 10**6, transcendentals=0),
    )(*smem, *args)


def grids(dims):
    return lax.broadcasted_iota(jnp.int32, dims, 0), lax.broadcasted_iota(jnp.int32, dims, 1)


def to_row(col):
    down, along = grids((col.shape[0], col.shape[0]))
    return jnp.sum(jnp.where(down == along, col, jnp.zeros_like(col)), axis=0, keepdims=True)


def to_col(row):
    down, along = grids((row.shape[1], row.shape[1]))
    return jnp.sum(jnp.where(down == along, row, jnp.zeros_like(row)), axis=1, keepdims=True)


def head_kernel(d_ref, *refs):
    sources, im_ref, view_ref = refs[:6], refs[6], refs[7]
    parts_ref, place_ref, vs_ref, pack_ref = refs[8:12]
    held, sems = refs[12:18], refs[18]
    copies = [pltpu.make_async_copy(a, b, sems.at[k]) for k, (a, b) in enumerate(zip(sources, held))]
    for copy in copies:
        copy.start()
    f_ref, w1_ref, w2_ref, tf_ref, tw1_ref, tw2_ref = held
    rows, teach = f_ref.shape[0], tf_ref.shape[0]
    n = parts_ref.shape[0]
    img = teach // 2
    per = rows // img
    im = (im_ref[...].reshape(1, rows) - d_ref[0] * img).astype(F32)
    down, along = grids((rows, rows))
    imc = to_col(im)
    same = im == imc
    after = jnp.where(same & (down < along), 1.0, 0.0)
    row = im * per + jnp.sum(after, axis=0, keepdims=True)
    place_ref[...] = row
    hit = row.astype(jnp.int32) == down
    vs_ref[...] = jnp.sum(jnp.where(hit, view_ref[...].reshape(1, rows).astype(F32), 0.0), axis=1, keepdims=True)
    order = jnp.where(hit, 1.0, 0.0).astype(BF16)

    for copy in copies:
        copy.wait()

    deep, hs = w1_ref.shape[0] // 2, w1_ref.shape[1]
    half = hs // 2
    pack_ref[:deep] = w1_ref[pl.ds(pl.multiple_of(d_ref[0] * deep, deep), deep)]
    w2_half = w2_ref[pl.ds(pl.multiple_of(d_ref[0] * half, half), half)]
    pack_ref[deep : deep + half] = w2_half[:, :hs]
    pack_ref[deep + half :] = w2_half[:, hs:]

    def part(x, first, second):
        act = dot(x[...], first[...], ((1,), (0,)))
        hidden = (act * 0.5 * (1.0 + lax.erf(act * 0.7071067811865476))).astype(BF16)
        return dot(hidden, second[...], ((1,), (0,)))

    z = part(f_ref, w1_ref, w2_ref).astype(BF16)
    z = dot(order, z, ((1,), (0,))).reshape(n, rows // n, -1)
    t = part(tf_ref, tw1_ref, tw2_ref).reshape(n, teach // n, -1)
    parts_ref[...] = jnp.concatenate([z, t], axis=1).astype(BF16)


def rows_kernel(parts_ref, out_ref, zn_ref):
    z = jnp.sum(parts_ref[...].astype(F32), axis=0)
    inv = lax.rsqrt(jnp.sum(z * z, axis=1, keepdims=True) + 1e-06)
    zn = z * inv
    zn_ref[...] = jnp.concatenate([zn, jnp.broadcast_to(inv, (zn.shape[0], 128))], axis=1)
    out_ref[...] = jnp.broadcast_to(zn[None], out_ref.shape).astype(BF16)


def row_mass(kern, mass):
    if mass is None:
        scale = 1.0 / jnp.sum(kern, axis=0, keepdims=True)
    else:
        scale = 1.0 / jnp.sum(kern * (1.0 / mass), axis=0, keepdims=True)
    return scale, jnp.sum(kern * scale, axis=1, keepdims=True)


def fold(col):
    row = to_row(col)
    return jnp.concatenate([row[:, k : k + 128] for k in range(0, row.shape[1], 128)], axis=0)


def unfold(block):
    return to_col(jnp.concatenate([block[k : k + 1] for k in range(block.shape[0])], axis=1))


def kern_kernel(d_ref, got_ref, other_ref, tpnb_ref, kern_ref, msg_ref, student_ref):
    n, slot, bot = got_ref.shape
    rows = student_ref.shape[0] // 2
    sr = rows // n
    own, other = got_ref[...].astype(F32), other_ref[...].astype(F32)
    student_ref[:rows] = own[:, :sr].reshape(rows, bot).astype(BF16)
    student_ref[rows:] = other[:, :sr].reshape(rows, bot).astype(BF16)
    own, other = own[:, sr:].reshape(-1, bot), other[:, sr:].reshape(-1, bot)
    first = d_ref[0] == 0
    teacher = jnp.concatenate([jnp.where(first, own, other), jnp.where(first, other, own)], axis=0).astype(BF16)
    kern = jnp.exp(dot(teacher, tpnb_ref[...], ((1,), (0,))) * (1.0 / 0.07))
    kern_ref[...] = kern
    _, mass = row_mass(kern, None)
    msg_ref[...] = jnp.broadcast_to(fold(mass)[None], msg_ref.shape)


def student_kernel(z_ref, pnb_ref, exb_ref, own_ref, other_ref, esum_ref):
    step = pl.program_id(0)
    ex = jnp.exp(dot(z_ref[...], pnb_ref[...], ((1,), (0,))) * 10.0)
    esum_ref[...] = jnp.sum(ex, axis=1, keepdims=True)
    exb = ex.astype(BF16)
    exb_ref[...] = exb
    sums = dot(exb, pnb_ref[...], ((1,), (1,)))

    @pl.when(step < pl.num_programs(0) // 2)
    def _():
        own_ref[...] = sums

    @pl.when(step >= pl.num_programs(0) // 2)
    def _():
        other_ref[...] = sums


def student_sums(student, pnb):
    total, bot = student.shape
    cols = pnb.shape[1]
    tile = total // 4
    return pl.pallas_call(
        student_kernel,
        name="student_kernel",
        grid=(4,),
        out_shape=(
            shape((total, cols), BF16),
            shape((total // 2, bot), F32),
            shape((total // 2, bot), F32),
            shape((total, 1), F32),
        ),
        in_specs=[pl.BlockSpec((tile, bot), lambda i: (i, 0)), pl.BlockSpec((bot, cols), lambda i: (0, 0))],
        out_specs=(
            pl.BlockSpec((tile, cols), lambda i: (i, 0)),
            pl.BlockSpec((tile, bot), lambda i: (jnp.minimum(i, 1), 0)),
            pl.BlockSpec((tile, bot), lambda i: (jnp.maximum(i - 2, 0), 0)),
            pl.BlockSpec((tile, 1), lambda i: (i, 0)),
        ),
        compiler_params=params(),
        cost_estimate=pl.CostEstimate(flops=5 * 10**9, bytes_accessed=10**7, transcendentals=0),
    )(student, pnb)


def second_kernel(d_ref, got_ref, kern_ref, esum_ref, msg_ref):
    mass = unfold(jnp.sum(got_ref[...], axis=0))
    _, mass = row_mass(kern_ref[...], mass)
    half = esum_ref.shape[0] // 2
    own, other = to_row(esum_ref[:half]), to_row(esum_ref[half:])
    first = d_ref[0] == 0
    mass = to_row(mass)
    n = msg_ref.shape[0] // 2
    for k, row in enumerate((jnp.where(first, own, other), jnp.where(first, other, own))):
        part = jnp.concatenate([mass, row], axis=1)
        msg_ref[k * n : (k + 1) * n] = jnp.broadcast_to(part[None], (n,) + part.shape)


def third_kernel(d_ref, got_ref, kern_ref, pnb_ref, esum_ref, last_ref, mine_ref, yours_ref):
    teach = kern_ref.shape[0]
    got = jnp.sum(got_ref[...], axis=0)
    esum_ref[...] = to_col(got[:, teach:])
    kern = kern_ref[...]
    scale, mass = row_mass(kern, to_col(got[:, :teach]))
    last = (kern * scale).astype(BF16)
    last_ref[...] = last
    sums = dot(last, pnb_ref[...], ((1,), (1,)))
    sums = jnp.concatenate([sums, jnp.broadcast_to(mass, (teach, 128))], axis=1)
    half = teach // 2
    first = d_ref[0] == 0
    mine_ref[...] = jnp.where(first, sums[:half], sums[half:])
    yours_ref[...] = jnp.where(first, sums[half:], sums[:half])


def message_kernel(sums_ref, b0_ref, b1_ref, out_ref):
    n = out_ref.shape[0]
    rows, bot = sums_ref.shape
    sums = sums_ref[...].astype(F32).reshape(n, rows // n, bot)
    both = b0_ref[...] + b1_ref[...]
    mass = both[:, bot:]
    high = mass.astype(BF16).astype(F32)
    tail = jnp.concatenate([high, mass - high], axis=1)
    teach = both.shape[0]
    both = both[:, :bot].reshape(n, teach // n, bot)
    out_ref[...] = jnp.concatenate([sums, both, tail.reshape(n, teach // n, bot)], axis=1).astype(BF16)


def bottleneck_kernel(factor, p_ref, got_ref, zn_ref, view_ref, scale_ref, out_ref):
    sr = view_ref.shape[0] // out_ref.shape[0]
    mine = pl.ds(pl.multiple_of(p_ref[0] * sr, sr), sr)
    tr = zn_ref.shape[0] - sr
    per = sr // (tr // 2)
    out = jnp.sum(got_ref[...].astype(F32), axis=0)
    tail = out[sr + tr :]
    image = factor / (tail[:, :1] + tail[:, 128:129])
    sums = out[sr : sr + tr] * image
    bot = got_ref.shape[2]
    zn, zinv = zn_ref[:sr, :bot], zn_ref[:sr, bot : bot + 1]
    znb = zn.astype(BF16).astype(F32)
    view = view_ref[mine].astype(jnp.int32)
    which = lax.broadcasted_iota(jnp.int32, (sr, 1), 0)
    dzn = scale_ref[mine] * out[:sr]
    own = []
    for t in range(tr):
        base = (t // 2) * per
        pick = (which >= base) & (which < base + per) & (view != t % 2)
        dzn = dzn - jnp.where(pick, sums[t : t + 1], 0.0)
        own.append(jnp.sum(jnp.where(pick, znb, 0.0), axis=0, keepdims=True) * image[t : t + 1])
    dz = zinv * (dzn - zn * jnp.sum(zn * dzn, axis=1, keepdims=True))
    both = jnp.concatenate([dz] + own, axis=0)
    out_ref[...] = jnp.broadcast_to(both[None], out_ref.shape).astype(BF16)


def hidden_kernel(f0_ref, f1_ref, w1_ref, h0_ref, h1_ref, s0_ref, s1_ref):
    for f, h, s in ((f0_ref, h0_ref, s0_ref), (f1_ref, h1_ref, s1_ref)):
        act = dot(f[...], w1_ref[...], ((1,), (0,))).T
        phi = 0.5 * (1.0 + lax.erf(act * 0.7071067811865476))
        h[...] = (act * phi).astype(BF16)
        s[...] = phi + act * jnp.exp(-0.5 * act * act) * 0.3989422804014327


def slopes_kernel(d_ref, p_ref, f_ref, own_ref, other_ref, slope_ref, w2_ref, w1_ref):
    hs = own_ref.shape[2]
    deep = f_ref.shape[1] // 2
    first = d_ref[0] == 0
    own, other = own_ref[...], other_ref[...]
    low = jnp.where(first, own, other)
    high = jnp.where(first, other, own)
    a, b = (jnp.concatenate([x[0], x[1]], axis=1) for x in (low[:, :deep], high[:, :deep]))
    act = dot(f_ref[:, :deep], a, ((1,), (0,))) + dot(f_ref[:, deep:], b, ((1,), (0,)))
    phi = 0.5 * (1.0 + lax.erf(act * 0.7071067811865476))
    slope_ref[...] = phi + act * jnp.exp(-0.5 * act * act) * 0.3989422804014327
    groups, width = w1_ref.shape[0], w1_ref.shape[1]
    blocks = deep // width
    for k in range(groups):
        chip = p_ref[0] ^ (k * NEAR)
        at = pl.multiple_of(lax.rem(chip, blocks) * width, width)
        mine = (chip // blocks) == d_ref[0]
        rows = jnp.where(mine, own_ref[:, pl.ds(at, width)], other_ref[:, pl.ds(at, width)])
        w1_ref[k] = jnp.concatenate([rows[0], rows[1]], axis=1)
    half = hs // 2
    for k in range(2):
        for part, x in ((0, low), (1, high)):
            tail = jnp.concatenate([x[k, deep : deep + half], x[k, deep + half :]], axis=1)
            w2_ref[k * hs + part * half : k * hs + (part + 1) * half] = tail


def slopes_of(d, p, features, own, other, width, groups):
    n, tall, hs = own.shape
    rows = features.shape[0]
    whole = lambda k, d, p: (0, 0)
    return pl.pallas_call(
        slopes_kernel,
        name="slopes_kernel",
        grid_spec=pltpu.PrefetchScalarGridSpec(
            num_scalar_prefetch=2,
            grid=(n // 2,),
            in_specs=[
                pl.BlockSpec(features.shape, whole),
                pl.BlockSpec((2, tall, hs), lambda k, d, p: (k, 0, 0)),
                pl.BlockSpec((2, tall, hs), lambda k, d, p: (k, 0, 0)),
            ],
            out_specs=(
                pl.BlockSpec((rows, 2 * hs), lambda k, d, p: (0, k)),
                pl.BlockSpec((2 * hs, 2 * hs), lambda k, d, p: (k, 0)),
                pl.BlockSpec((groups, width, 2 * hs), lambda k, d, p: (0, 0, k)),
            ),
        ),
        out_shape=(shape((rows, n * hs), F32), shape((n * hs, 2 * hs), BF16), shape((groups, width, n * hs), BF16)),
        compiler_params=params(),
        cost_estimate=pl.CostEstimate(flops=4 * 10**9, bytes_accessed=3 * 10**7, transcendentals=0),
    )(d.reshape(1), p.reshape(1), features, own, other)


def fetch(pairs, sems):
    copies = [pltpu.make_async_copy(x, y, sems.at[k]) for k, (x, y) in enumerate(pairs)]
    for copy in copies:
        copy.start()
    return copies


def put_back(got, place):
    n, _, bot = got.shape
    rows = place.shape[1]
    _, along = grids((rows, rows))
    back = jnp.where(to_col(place).astype(jnp.int32) == along, 1.0, 0.0).astype(BF16)
    dz = got.astype(F32)[:, : rows // n].reshape(rows, bot).astype(BF16)
    return dot(back, dz, ((1,), (0,))).astype(BF16)


def features_kernel(step, *refs):
    ins, held, sems = refs[:5], refs[-6:-1], refs[-1]
    dz_ref, own_ref, *far_refs = refs[5:-6]
    got, place, slope, w2, w1 = held
    groups, width = w1.shape[:2]
    pieces = [pl.ds(k, step) for k in range(0, slope.shape[1], step)]
    small = fetch([(ins[k], held[k]) for k in (0, 1, 4)], sems.at[pl.ds(0, 3)])
    large = []
    for k, piece in enumerate(pieces):
        pairs = [(ins[2].at[:, piece], slope.at[:, piece]), (ins[3].at[piece], w2.at[piece])]
        large.append(fetch(pairs, sems.at[pl.ds(3 + 2 * k, 2)]))
    for copy in small:
        copy.wait()
    dz = put_back(got[...], place[...])
    dz_ref[...] = dz
    total = None
    for piece, copies in zip(pieces, large):
        for copy in copies:
            copy.wait()
        dhid = (dot(dz, w2[piece], ((1,), (1,))) * slope[:, piece]).astype(BF16)
        part = dot(w1[:, :, piece].reshape(groups * width, step), dhid, ((1,), (1,)))
        total = part if total is None else total + part
    own_ref[...] = total[:width]
    for k, far_ref in enumerate(far_refs, 1):
        far_ref[...] = total[k * width : (k + 1) * width].astype(BF16)


def feature_grads(got, place, slope, w2, w1):
    args = (got, place, slope, w2, w1)
    rows, hidden = slope.shape
    bot, step = got.shape[2], 256
    groups, width = w1.shape[:2]
    outs = (shape((rows, bot), BF16), shape((width, rows), F32)) + (shape((width, rows), BF16),) * (groups - 1)
    return pl.pallas_call(
        functools.partial(features_kernel, step),
        name="features_kernel",
        grid=(1,),
        out_shape=outs,
        in_specs=[pl.BlockSpec(memory_space=pl.ANY)] * len(args),
        out_specs=tuple(block(x.shape) for x in outs),
        scratch_shapes=[pltpu.VMEM(x.shape, x.dtype) for x in args]
        + [pltpu.SemaphoreType.DMA((3 + 2 * (hidden // step),))],
        compiler_params=params(),
    )(*args)


def last_kernel(tile, d_ref, *refs):
    ins, (gp_hbm, g1_hbm, g2_hbm) = refs[:16], refs[16:19]
    held, (gp, g1, g2, sems, tile_sems, out_sems) = refs[19:35], refs[35:]
    dz0, got0, got1, place1, protos, down, dother, lown, lother, f0, f1, h0, h1, s0, s1, w2 = held
    cols = protos.shape[1] // 2
    steps = cols // tile
    rows = dz0.shape[0]
    n, slot, bot = got0.shape
    early = fetch([(ins[k], held[k]) for k in range(4)], sems)
    tiles = []
    for k in range(2 * steps):
        own = k < steps
        here = pl.multiple_of((d_ref[0] if own else 1 - d_ref[0]) * cols + (k % steps) * tile, tile)
        there = pl.ds((k % steps) * tile, tile)
        a, b = (5, 7) if own else (6, 8)
        pairs = [
            (ins[4].at[:, pl.ds(here, tile)], protos.at[:, pl.ds(here, tile)]),
            (ins[a].at[:, there], held[a].at[:, there]),
            (ins[b].at[:, there], held[b].at[:, there]),
        ]
        tiles.append((here, there, a, b, fetch(pairs, tile_sems.at[k])))
    late = fetch([(ins[k], held[k]) for k in range(9, 16)], sems.at[pl.ds(4, 7)])
    for copy in early:
        copy.wait()
    first = d_ref[0] == 0
    right0 = got0[...].astype(F32)[:, rows // n :].reshape(-1, bot)
    right1 = got1[...].astype(F32)[:, rows // n :].reshape(-1, bot)
    right = jnp.concatenate([jnp.where(first, right0, right1), jnp.where(first, right1, right0)], axis=0)
    right = right.T.astype(BF16)
    dz1 = put_back(got1[...], place1[...])
    outs = []
    for k, (here, there, a, b, copies) in enumerate(tiles):
        for copy in copies:
            copy.wait()
        mat = protos[:, pl.ds(here, tile)].astype(F32)
        inv = lax.rsqrt(jnp.sum(mat * mat, axis=0, keepdims=True) + 1e-06)
        pn = mat * inv
        dpn = held[a][:, there].astype(F32) - dot(right, held[b][:, there], ((1,), (0,)))
        gp[:, pl.ds(here, tile)] = inv * (dpn - pn * jnp.sum(pn * dpn, axis=0, keepdims=True))
        out = pltpu.make_async_copy(gp.at[:, pl.ds(here, tile)], gp_hbm.at[:, pl.ds(here, tile)], out_sems.at[k])
        out.start()
        outs.append(out)
    for copy in late:
        copy.wait()
    sums1, sums2 = [], []
    for f, dz, h, sl in ((f0, dz0[...], h0, s0), (f1, dz1, h1, s1)):
        sums2.append(dot(h[...], dz, ((1,), (0,))))
        dhid = (dot(w2[...], dz, ((1,), (1,))) * sl[...]).astype(BF16)
        sums1.append(dot(dhid, f[...], ((1,), (0,))))
    g1[...] = (sums1[0] + sums1[1]).T
    g2[...] = sums2[0] + sums2[1]
    for k, (x, y) in enumerate(((g1, g1_hbm), (g2, g2_hbm))):
        out = pltpu.make_async_copy(x, y, out_sems.at[2 * steps + k])
        out.start()
        outs.append(out)
    for out in outs:
        out.wait()


def last_grads(d, head_w1, *args):
    tile = 512
    protos, head_w2 = args[4], args[15]
    tiles = protos.shape[1] // tile
    outs = (shape(protos.shape, F32), shape(head_w1.shape, F32), shape(head_w2.shape, F32))
    anywhere = pl.BlockSpec(memory_space=pl.ANY)
    return pl.pallas_call(
        functools.partial(last_kernel, tile),
        name="last_kernel",
        out_shape=outs,
        in_specs=[pl.BlockSpec(memory_space=pltpu.SMEM)] + [anywhere] * len(args),
        out_specs=(anywhere,) * 3,
        scratch_shapes=[pltpu.VMEM(x.shape, x.dtype) for x in args + outs]
        + [
            pltpu.SemaphoreType.DMA((11,)),
            pltpu.SemaphoreType.DMA((tiles, 3)),
            pltpu.SemaphoreType.DMA((tiles + 2,)),
        ],
        compiler_params=params(),
    )(d.reshape(1), *args)


def tied(*values):
    return lax.optimization_barrier(values)


def paired_body(
    features,
    teacher_features,
    crop_image,
    crop_view,
    head_w1,
    head_w2,
    protos,
    teacher_w1,
    teacher_w2,
    teacher_protos,
):
    nd, n = lax.axis_size("dp"), lax.axis_size("proto")
    d, p = lax.axis_index("dp"), lax.axis_index("proto")
    rows, teach = features.shape[0], teacher_features.shape[0]
    sr, tr = rows // n, teach // n
    wide, hs = head_w1.shape
    bot = head_w2.shape[1]
    everyone = nd * n
    factor = 10.0 / (9 * teach * nd)

    heads = (features, head_w1, head_w2, teacher_features, teacher_w1, teacher_w2)
    parts, place, view, weights = pl.pallas_call(
        head_kernel,
        grid=(1,),
        out_shape=(
            shape((n, sr + tr, bot), BF16),
            shape((1, rows), F32),
            shape((rows, 1), F32),
            shape((wide // 2 + hs, hs), BF16),
        ),
        in_specs=[pl.BlockSpec(memory_space=pltpu.SMEM)]
        + [pl.BlockSpec(memory_space=pl.ANY)] * 6
        + [block((rows,))] * 2,
        out_specs=(block((n, sr + tr, bot)), block((1, rows)), block((rows, 1)), block((wide // 2 + hs, hs))),
        scratch_shapes=[pltpu.VMEM(x.shape, x.dtype) for x in heads] + [pltpu.SemaphoreType.DMA((6,))],
        compiler_params=params(62),
        name="head_kernel",
    )(d.reshape(1), *heads, crop_image, crop_view)
    parts_got = lax.all_to_all(parts, "proto", 0, 0)
    protos_late, tprotos_late, feat_late, _ = tied(protos, teacher_protos, features, parts)
    feat_other = swap(feat_late, "dp", 1)
    cols = protos.shape[1] // nd
    pnb = unit_cols(lax.dynamic_slice_in_dim(protos_late, d * cols, cols, 1))[0].astype(BF16)
    tpnb = unit_cols(lax.dynamic_slice_in_dim(tprotos_late, d * cols, cols, 1))[0].astype(BF16)
    parts_got, pnb, tpnb = tied(parts_got, pnb, tpnb)

    got, zn = call(
        rows_kernel,
        (shape((n, sr + tr, bot), BF16), shape((sr + tr, bot + 128), F32)),
        [],
        parts_got,
        mib=40,
    )
    sent = got
    got = lax.all_to_all(got, "proto", 0, 0)
    w1_late, feat_late, feat_other_late, _ = tied(head_w1, features, feat_other, sent)
    h0, h1, s0, s1 = call(
        hidden_kernel,
        (shape((hs, rows), BF16),) * 2 + (shape((hs, rows), F32),) * 2,
        [],
        feat_late, feat_other_late, w1_late,
        us=4,
    )
    got, h0, h1, s0, s1 = tied(got, h0, h1, s0, s1)
    got_other = swap(got, "dp", 1)
    kern, msg, student = call(
        kern_kernel,
        (shape((nd * teach, cols), F32), shape((everyone, nd * teach // 128, 128), F32), shape((nd * rows, bot), BF16)),
        [d],
        got, got_other, tpnb,
        us=3,
    )
    msg_got = lax.all_to_all(msg, ALL, 0, 0)
    student, weights, _ = tied(student, weights, msg)
    weights = [weights] + [swap(weights, "proto", k) for k in range(1, NEAR)]
    exb, sums, sums_other, esum = student_sums(student, pnb)
    msg = call(
        second_kernel,
        shape((everyone, 1, nd * teach + rows), F32),
        [d],
        msg_got, kern, esum,
        mib=56,
    )
    msg_got = lax.all_to_all(msg, ALL, 0, 0)
    sums, sums_other, *weights, _ = tied(sums, sums_other, *weights, msg)
    weights = jnp.stack(weights)
    sums_other = swap(sums_other, "dp", 1)
    sums = (sums + sums_other).astype(BF16)
    msg_got, sums, weights = tied(msg_got, sums, weights)
    weights_other = swap(weights, "dp", 1)
    esum, last, mine, yours = call(
        third_kernel,
        (
            shape((rows, 1), F32),
            shape((nd * teach, cols), BF16),
            shape((teach, bot + 128), F32),
            shape((teach, bot + 128), F32),
        ),
        [d],
        msg_got, kern, pnb,
        us=2,
    )
    yours = swap(yours, "dp", 1)
    msg = call(message_kernel, shape((n, sr + 2 * tr, bot), BF16), [], sums, mine, yours)
    msg_got = lax.all_to_all(msg, "proto", 0, 0)

    esum, view_late, last, weights, place, _ = tied(esum, view, last, weights, place, msg)
    place_other = swap(place, "dp", 1)
    crop_scale = jnp.where(view_late == 2, 2.0, 1.0) * factor / esum
    scale_other = swap(crop_scale, "dp", 1)
    left = (student.astype(F32) * jnp.concatenate([crop_scale, scale_other], axis=0)).astype(BF16)
    dpn = dot(left, exb, ((0,), (0,))).astype(BF16)
    msg_got, dpn = tied(msg_got, dpn)
    dpn_other, last_other = swap(dpn, "dp", 1), swap(last, "dp", 1)
    dz = call(
        functools.partial(bottleneck_kernel, factor),
        shape((n, sr + tr, bot), BF16),
        [p],
        msg_got, zn, view_late, crop_scale,
    )
    got = lax.all_to_all(dz, "proto", 0, 0)
    weights, feat_late, _ = tied(weights, features, dz)
    slopes = slopes_of(d, p, feat_late, weights, weights_other, wide // n, n // NEAR)
    got, slopes = tied(got, slopes)

    got_other = swap(got, "dp", 1)
    dz, grad_features, *far = feature_grads(got, place, *slopes)
    far = [swap(x, "proto", k * NEAR) for k, x in enumerate(far, 1)]
    grad_protos, grad_w1, grad_w2 = last_grads(
        d, head_w1, dz, got, got_other, place_other, protos, dpn, dpn_other, last, last_other,
        features, feat_other, h0, h1, s0, s1, head_w2,
    )
    grad_protos, *far = tied(grad_protos, *far)
    grad_features = (grad_features + sum(x.astype(F32) for x in far)).astype(BF16).T
    return (grad_features, grad_w1, grad_w2, grad_protos)


def body(features, teacher_features, *rest):
    n = lax.axis_size("proto")
    slot = (features.shape[0] // n, teacher_features.shape[0] // n)
    paired = lax.axis_size("dp") == 2 and n == 4 * NEAR and slot[0] % 8 == 0 and slot[1] % 8 == 0
    paired = paired and features.shape[0] % teacher_features.shape[0] == 0
    return (paired_body if paired else general_body)(features, teacher_features, *rest)


def solution(mesh):
    in_specs = (
        P("dp", None),
        P("dp", None),
        P("dp"),
        P("dp"),
        P(None, "proto"),
        P("proto", None),
        P(None, "proto"),
        P(None, "proto"),
        P("proto", None),
        P(None, "proto"),
    )
    out_specs = (P("dp", "proto"), P(None, "proto"), P("proto", None), P(None, "proto"))
    return jax.shard_map(body, mesh=mesh, in_specs=in_specs, out_specs=out_specs, check_vma=False)
```
